512 devices in a mesh: dp: 16 (over x, y), owner: 32 (over z, core).
Axes of the slice: x: 4, y: 4, z: 16, core: 2. Of those that a mesh axis runs over, the one named last changes fastest.
Arguments:
- grad_partial: bfloat16 [16, 160, 512, 512], P('dp', 'owner'), may hold values from -5 to 5
- statistics: float32 [16, 32, 2, 512, 512], P('dp', 'owner'), may hold values from -3072 to 3072, as said below
- owner_table: int32 [160, 2], replicated, may hold values from 0 to 511, as said below
Outputs:
- update: bfloat16 [160, 512, 512], P('owner', 'dp')
The draws below stay inside these ranges and needn't reach their ends.
Inputs may be any that keep to these rules, and one draw needn't show every extreme that they name: `owner_table`: entry [b, s] names the device d * 32 + o (d its index along dp, o along owner) that keeps the statistic of side s of block b. Each device is named by at most 2 entries and some device by exactly 2; the entries naming a device, in increasing order of 2 b + s, use its slots 0, 1, ... of statistics, and its other slots are never read. The blocks b with b // 5 = c (block column c) name devices of any one owner index o at most 1 times, and some owner index is named exactly 1 times by every block column. Each statistics[d, o, q] is a symmetric positive definite matrix.
All inputs are finite; a program needn't handle non-finite values.
Results may differ from the reference program's by a relative error of at most 0.017.
Values may be sent and summed in bfloat16 or wider, within the bound.
No kernel may reach another device: no remote copies, remote signals or barrier semaphores. Data moves between devices by JAX's collectives and lax.ppermute only.
A program may use at most 64 MiB of HBM per device.

```python
import math
import jax
import jax.numpy as jnp
from jax import lax

B = 512
CB = 5
NBLK = 160
PAIR = 1
CAP = 2
DP_ROWS = 16
OWN_COLS = 32


def draw_statistics(key, part):
    key = jax.random.fold_in(key, 5)
    slot_keys = jax.random.split(key, DP_ROWS * OWN_COLS * CAP)

    def base_rows(base_key):
        return jax.random.truncated_normal(base_key, -4.0, 4.0, (B, B), jnp.float32)
    weight_gain = 1.5

    def one_slot(slot_key):
        base_key, lift_key = jax.random.split(slot_key)
        rows = base_rows(base_key)
        gram_part = jnp.dot(rows, rows.T, precision=lax.Precision.HIGHEST)
        lifted = B / 128.0 * jnp.exp(jax.random.uniform(lift_key, (B,), jnp.float32, 0.0, math.log(10.0)))
        return weight_gain * gram_part + jnp.diag(lifted)
    return lax.map(one_slot, slot_keys).reshape(DP_ROWS, OWN_COLS, CAP, B, B)


def draw_owner_table(key, part):
    key = jax.random.fold_in(key, 11)
    focus_key, column_base, shuffle_base, placing_base = jax.random.split(key, 4)
    pair_total = OWN_COLS * PAIR
    per_column = 2 * CB
    focus_col = jax.random.randint(focus_key, (), 0, OWN_COLS)
    slot_ids = jnp.arange(pair_total, dtype=jnp.int32)

    def pick_columns(column_key, shuffle_key):
        ranking = jax.random.permutation(column_key, pair_total)
        ranked = jnp.argsort(ranking).astype(jnp.int32)
        scores = ranked - jnp.where(slot_ids // PAIR == focus_col, pair_total, 0)
        chosen = jnp.argsort(scores)[:per_column]
        shuffle = jax.random.permutation(shuffle_key, per_column)
        return (chosen[shuffle] // PAIR).astype(jnp.int32)
    owner_col = jax.vmap(pick_columns)(jax.random.split(column_base, OWN_COLS), jax.random.split(shuffle_base, OWN_COLS)).reshape(-1)
    numbers = jnp.arange(2 * NBLK, dtype=jnp.int32)
    same_col = (owner_col[None, :] == owner_col[:, None]) & (numbers[None, :] < numbers[:, None])
    ranked_in = jnp.sum(same_col.astype(jnp.int32), axis=1)
    placings = jax.vmap(lambda one_key: jax.random.permutation(one_key, CAP * DP_ROWS))(jax.random.split(placing_base, OWN_COLS))
    placed = placings[owner_col, ranked_in]
    dp_row = placed // CAP
    return (dp_row * OWN_COLS + owner_col).reshape(NBLK, 2).astype(jnp.int32)


def spiked(drawn, own_key, source, target, blocks, factor):
    def block_of(dim):
        return (jnp.arange(drawn.shape[dim]) // (drawn.shape[dim] // blocks)).reshape((-1,) + (1,) * (drawn.ndim - 1 - dim))

    near = jax.random.permutation(own_key, blocks)[block_of(target)]
    other_side = (block_of(target) + blocks // 2) % blocks
    return jnp.where((block_of(source) == near) | (block_of(source) == other_side), factor * drawn, drawn)


def shard_levels(key, dims, pieces, smallest, largest):
    gain = 1.0
    for position, blocks in pieces:
        steps = jax.random.uniform(jax.random.fold_in(jax.random.fold_in(key, 6), position), (blocks,), jnp.float32, smallest / len(pieces), largest / len(pieces))
        gain = gain * jnp.repeat(jnp.exp(steps), dims[position] // blocks).reshape((-1,) + (1,) * (len(dims) - 1 - position))
    return gain


def bell_draw_with(stream_key, shape, width, most, pieces, heavy, kind=jnp.bfloat16):
    values = width * jax.random.normal(stream_key, shape, jnp.float32)
    if pieces:
        values = values * shard_levels(stream_key, shape, pieces, -0.22, 0.18)
    return jnp.clip(spiked(values, jax.random.fold_in(stream_key, 3), *heavy), -most, most).astype(kind)


def setup_inputs(seed: int = 0) -> dict:
    arg_keys = jax.random.split(jax.random.key(seed), 4)
    grad_partial = bell_draw_with(arg_keys[0], (DP_ROWS, NBLK, B, B), 0.25, 5.0, ((0, 16), (1, 32)), (0, 2, 16, 2.0))
    statistics = draw_statistics(jax.random.fold_in(arg_keys[3], 71), 0)
    owner_table = draw_owner_table(jax.random.fold_in(arg_keys[3], 71), 0)
    return {"grad_partial": grad_partial, "statistics": statistics, "owner_table": owner_table}


decay_rate = 0.9
update_gain = 16.0
root_gain = 1.5

def newton_root(new_stat):
    order_n = new_stat.shape[-1]
    identity = jnp.eye(order_n, dtype=jnp.float32)
    frob_norm = jnp.sqrt(jnp.sum(new_stat * new_stat) + 1e-06)
    root_scale = root_gain * math.sqrt(order_n) / frob_norm
    scaled_stat = root_scale * new_stat
    first_step = 1.25 * identity - 0.25 * scaled_stat
    squared = jnp.dot(first_step, first_step, precision=lax.Precision.HIGHEST)
    fourth = jnp.dot(squared, squared, precision=lax.Precision.HIGHEST)
    moved_stat = jnp.dot(fourth, scaled_stat, precision=lax.Precision.HIGHEST)
    second_step = 1.25 * identity - 0.25 * moved_stat
    return root_scale ** 0.25 * jnp.dot(first_step, second_step, precision=lax.Precision.HIGHEST)

def reference(grad_partial, statistics, owner_table):
    n_owner = statistics.shape[1]

    def add_partial(running, partial_block):
        return (running + partial_block.astype(jnp.float32), None)
    zero_sum = jnp.zeros(grad_partial.shape[1:], jnp.float32)
    summed = lax.scan(add_partial, zero_sum, grad_partial)[0]
    gradient = summed.astype(jnp.bfloat16)
    device = owner_table.reshape(-1).astype(jnp.int32)
    numbers = jnp.arange(device.shape[0], dtype=jnp.int32)
    earlier = numbers[None, :] < numbers[:, None]
    slot_of = lax.optimization_barrier(jnp.sum(((device[None, :] == device[:, None]) & earlier).astype(jnp.int32), axis=1)).astype(jnp.int32)

    def one_item(item_index):
        block_index = item_index // 2
        side_index = item_index % 2
        target = device[item_index]
        previous = statistics[target // n_owner, target % n_owner, slot_of[item_index]]
        block_grad = gradient[block_index]
        oriented = jnp.where(side_index == 0, block_grad, block_grad.T)
        gram_sum = jnp.dot(oriented, oriented.T, preferred_element_type=jnp.float32)
        new_stat = decay_rate * previous + (1.0 - decay_rate) * gram_sum
        return newton_root(new_stat).astype(jnp.bfloat16)
    inverse_roots = lax.map(one_item, numbers)

    def one_block(block_index):
        left_root = inverse_roots[2 * block_index]
        right_root = inverse_roots[2 * block_index + 1]
        applied = jnp.dot(gradient[block_index], right_root, preferred_element_type=jnp.float32).astype(jnp.bfloat16)
        return (update_gain * jnp.dot(left_root, applied, preferred_element_type=jnp.float32)).astype(jnp.bfloat16)
    return lax.map(one_block, jnp.arange(gradient.shape[0], dtype=jnp.int32))
```

```python
import functools
import math

import jax
import jax.numpy as jnp
import numpy as np
from jax import lax
from jax.experimental import pallas as pl
from jax.experimental.pallas import tpu as pltpu
from jax.sharding import Mesh
from jax.sharding import PartitionSpec as P

decay_rate = 0.9
update_gain = 16.0
root_gain = 1.5

side_x = 4
chips = (
    ((0, 0), (0, 2), (2, 0), (1, 1), (3, 3)),
    ((1, 0), (1, 2), (3, 0), (2, 1), (0, 3)),
)
blocks_col = len(chips[0])
packed_rows = 72

VMEM = pl.BlockSpec(memory_space=pltpu.VMEM)
SMEM = pl.BlockSpec(memory_space=pltpu.SMEM)


def even(v):
    return v ^ 1


def odd(v):
    return side_x - 1 - v


def order(portion, core):
    first, later = (even, odd) if core == 0 else (odd, even)
    one, two = portion, 1 - portion
    return ((one, first), (one, later), (two, first), (two, later))


def pairs(portion, step):
    out = []
    for x in range(side_x):
        for y in range(side_x):
            for p in range(2):
                axis, pairing = order(portion, p)[step]
                to = (pairing(x), y) if axis == 0 else (x, pairing(y))
                out.append((2 * (side_x * x + y) + p, 2 * (side_x * to[0] + to[1]) + p))
    return out


def padded(items, count):
    assert len(items) <= count
    return (list(items) + [0] * count)[:count]


@functools.cache
def tree_tables():
    first, second, third = [], [], []
    for d in range(side_x * side_x):
        here = (d // side_x, d % side_x)
        for p in range(2):
            one, two, three = [], [], []
            for portion in range(2):
                steps = order(portion, p)
                axis, later = steps[1]
                at = [c[axis] for c in chips[p]]
                me = here[axis]
                kept = [j for j in range(blocks_col) if at[j] in (me, later(me))]
                one += padded([j for j in range(blocks_col) if j not in kept], 3)
                padded(kept, 3)
                go = [i for i, j in enumerate(kept) if at[j] == later(me)]
                stay = [i for i, j in enumerate(kept) if at[j] == me]
                for place in padded(go, 2) + padded(stay, 2):
                    two += [place, padded(kept, 3)[place]]
                mine = [kept[i] for i in stay]
                axis, later = steps[3]
                near = (here[axis], later(here[axis]))
                stay = [i for i, j in enumerate(mine) if chips[p][j][axis] in near]
                go = [i for i, j in enumerate(mine) if chips[p][j][axis] not in near]
                three += padded(go, 1) + padded(stay, 1)
            first.append(one)
            second.append(two)
            third.append(three)
    return [np.array(t, np.int32) for t in (first, second, third)]


@functools.cache
def home_tables():
    item = np.zeros((2, 2 * side_x * side_x), np.int32)
    rows = np.zeros((2, blocks_col), np.int32)
    for p in range(2):
        for j, (x, y) in enumerate(chips[p]):
            d = side_x * x + y
            rows[p, j] = d
            item[p, 2 * d : 2 * d + 2] = (2 * j, 2 * j + 1)
    return item, rows


def params(mib):
    return pltpu.CompilerParams(vmem_limit_bytes=mib * 1024 * 1024)


def add_rounded(a, b):
    return (a.astype(jnp.float32) + b.astype(jnp.float32)).astype(jnp.bfloat16)


def choose_kernel(table, source, s0, s1):
    height = s0.shape[1]
    for h, sent in enumerate((s0, s1)):
        for u in range(3):
            sent[u] = source[table[3 * h + u], h * height : (h + 1) * height, :]


def first_sum_kernel(table, source, r0, r1, s0, s1, kept):
    height = r0.shape[1]
    for h, (got, sent) in enumerate(((r0, s0), (r1, s1))):
        for u in range(4):
            place, block = table[8 * h + 2 * u], table[8 * h + 2 * u + 1]
            total = add_rounded(source[block, h * height : (h + 1) * height, :], got[place])
            if u < 2:
                sent[u] = total
            else:
                kept[h, u - 2] = total


def second_sum_kernel(table, kept, r0, r1, s0, s1, next_kept):
    for h, (got, sent) in enumerate(((r0, s0), (r1, s1))):
        go, stay = table[2 * h], table[2 * h + 1]
        sent[...] = add_rounded(kept[h, go], got[go])
        next_kept[h] = add_rounded(kept[h, stay], got[stay])


def third_sum_kernel(kept, r0, r1, s0, s1):
    s0[...] = add_rounded(kept[0], r0[...])
    s1[...] = add_rounded(kept[1], r1[...])


def gram_kernel(a, b, r0, r1, out, left, right):
    half = a.shape[0]
    out[:half, :] = add_rounded(a[...], r0[...])
    out[half:, :] = add_rounded(b[...], r1[...])
    g = out[...]
    for gram, side in ((left, 1), (right, 0)):
        gram[...] = lax.dot_general(
            g, g, (((side,), (side,)), ((), ())), preferred_element_type=jnp.float32
        )


def pick_kernel(table, source, out):
    for i in range(out.shape[0]):
        out[i] = source[table[i]]


def pick(table, source):
    return pl.pallas_call(
        pick_kernel,
        out_shape=jax.ShapeDtypeStruct(table.shape + source.shape[1:], source.dtype),
        in_specs=[SMEM, VMEM],
        out_specs=VMEM,
        compiler_params=params(4),
        cost_estimate=pl.CostEstimate(
            flops=0, bytes_accessed=4 * table.shape[0] * 65536, transcendentals=0
        ),
    )(table, source)


def square_iotas(n):
    return (
        lax.broadcasted_iota(jnp.int32, (n, n), 0),
        lax.broadcasted_iota(jnp.int32, (n, n), 1),
    )


def pack_kernel(stats, out):
    half = stats.shape[1] // 2
    i, j = square_iotas(half)
    row = lax.broadcasted_iota(jnp.int32, (8, 128), 0)
    for q in range(stats.shape[0]):
        low = stats[q, half:, half:]
        mixed = jnp.where(i <= j, stats[q, :half, :half], low).astype(jnp.bfloat16)
        side = stats[q, :half, half:].astype(jnp.bfloat16)
        diagonal = jnp.sum(jnp.where(i == j, low, 0.0), axis=0, keepdims=True)
        tail = jnp.where(
            row == 0, diagonal[:, :128], jnp.where(row == 1, diagonal[:, 128:], 0.0)
        ).astype(jnp.bfloat16)
        strips = (mixed[:, :128], mixed[:, 128:], side[:, :128], side[:, 128:])
        for c in range(16):
            out[c, q, :64, :] = strips[c // 4][64 * (c % 4) : 64 * (c % 4) + 64, :]
            out[c, q, 64:, :] = tail


def split(a):
    high = a.astype(jnp.bfloat16)
    return high, (a - high.astype(jnp.float32)).astype(jnp.bfloat16)


def product(a, b):
    dot = functools.partial(jnp.dot, preferred_element_type=jnp.float32)
    return dot(a[0], b[0]) + (dot(a[0], b[1]) + dot(a[1], b[0]))


def unpack(chunks, s, mixed, stat):
    half = mixed.shape[0]
    for c in range(16):
        strip = chunks[c, s, :64, :].astype(jnp.float32)
        rows = slice(64 * (c % 4), 64 * (c % 4) + 64)
        at = c // 4
        if at < 2:
            mixed[rows, 128 * at : 128 * at + 128] = strip
        else:
            stat[rows, half + 128 * (at - 2) : half + 128 * (at - 2) + 128] = strip
    tail = chunks[0, s, 64:, :].astype(jnp.float32)
    diagonal = jnp.concatenate([tail[0:1, :], tail[1:2, :]], axis=1)
    m = mixed[...]
    flipped = m.T
    i, j = square_iotas(half)
    stat[:half, :half] = jnp.where(i <= j, m, flipped)
    stat[half:, half:] = jnp.where(i > j, m, jnp.where(i == j, diagonal, flipped))
    stat[half:, :half] = stat[:half, half:].T


def update_kernel(chunks, gradient, left, right, out, mixed, stat):
    order_n = out.shape[0]
    sides = (0, 1)
    for s in sides:
        unpack(chunks, s, mixed.at[s], stat.at[s])
    i, j = square_iotas(order_n)
    identity = jnp.where(i == j, 1.25, 0.0)
    scale, first = [], []
    for s, gram in zip(sides, (left, right)):
        new_stat = decay_rate * stat[s] + (1.0 - decay_rate) * gram[...]
        squares = jnp.sum(new_stat * new_stat, axis=0, keepdims=True)
        frob_norm = jnp.sqrt(jnp.sum(squares, axis=1, keepdims=True) + 1e-06)
        scale.append(root_gain * math.sqrt(order_n) / frob_norm)
        first.append(identity - (0.25 * scale[s]) * new_stat)
    parts = [split(f) for f in first]
    squared = [product(f, f) for f in parts]
    parts = [split(f) for f in squared]
    fourth = [split(product(f, f)) for f in parts]
    rest = [split(squared[s] - 1.25 * first[s]) for s in sides]
    roots = []
    for s in sides:
        root = 1.25 * first[s] + product(fourth[s], rest[s])
        roots.append((jnp.sqrt(jnp.sqrt(scale[s])) * root).astype(jnp.bfloat16))
    applied = jnp.dot(gradient[...], roots[1], preferred_element_type=jnp.float32)
    update = jnp.dot(
        roots[0], applied.astype(jnp.bfloat16), preferred_element_type=jnp.float32
    )
    out[...] = (update_gain * update).astype(jnp.bfloat16)


def shape(*dims):
    return jax.ShapeDtypeStruct(dims, jnp.bfloat16)


def cost(flops, moved):
    return pl.CostEstimate(flops=flops, bytes_accessed=moved, transcendentals=0)


def exchange(arrays, step):
    return [
        lax.ppermute(a, ("dp", "core"), pairs(portion, step)) for portion, a in enumerate(arrays)
    ]


def first_sent(grad, tables):
    n, order_n = grad.shape[1], grad.shape[2]
    return pl.pallas_call(
        choose_kernel,
        out_shape=[shape(3, n // 2, order_n)] * 2,
        in_specs=[SMEM, VMEM],
        out_specs=[VMEM] * 2,
        compiler_params=params(12),
        cost_estimate=cost(0, 6 * n * order_n),
    )(tables[0], grad)


def gradient_sum(grad, sent, tables):
    n, order_n = grad.shape[1], grad.shape[2]
    half = n // 2
    unit = 2 * half * order_n
    *sent, kept = pl.pallas_call(
        first_sum_kernel,
        out_shape=[shape(2, half, order_n)] * 2 + [shape(2, 2, half, order_n)],
        in_specs=[SMEM] + [VMEM] * 3,
        out_specs=[VMEM] * 3,
        compiler_params=params(16),
        cost_estimate=cost(0, 24 * unit),
    )(tables[1], grad, *exchange(sent, 0))
    *sent, kept = pl.pallas_call(
        second_sum_kernel,
        out_shape=[shape(half, order_n)] * 2 + [shape(2, half, order_n)],
        in_specs=[SMEM] + [VMEM] * 3,
        out_specs=[VMEM] * 3,
        compiler_params=params(12),
        cost_estimate=cost(0, 12 * unit),
    )(tables[2], kept, *exchange(sent, 1))
    sent = pl.pallas_call(
        third_sum_kernel,
        out_shape=[shape(half, order_n)] * 2,
        in_specs=[VMEM] * 3,
        out_specs=[VMEM] * 2,
        compiler_params=params(8),
        cost_estimate=cost(0, 6 * unit),
    )(kept, *exchange(sent, 2))
    square = jax.ShapeDtypeStruct((n, order_n), jnp.float32)
    return pl.pallas_call(
        gram_kernel,
        out_shape=[shape(n, order_n), square, square],
        in_specs=[VMEM] * 4,
        out_specs=[VMEM] * 3,
        compiler_params=params(16),
        cost_estimate=cost(4 * n**3, 12 * unit),
    )(*sent, *exchange(sent, 3))


def body(grad_partial, statistics, owner_table):
    n_dp = lax.axis_size("dp")
    n_owner = lax.axis_size("z") * 2
    order_b = grad_partial.shape[3]
    slab = order_b // n_dp
    slots = statistics.shape[2]
    row = lax.axis_index("dp")
    core = lax.axis_index("core")
    col = 2 * lax.axis_index("z") + core
    lane_item, out_rows = home_tables()
    tables = [jnp.asarray(t)[2 * row + core] for t in tree_tables()]

    device = owner_table.reshape(-1)
    numbers = jnp.arange(device.shape[0], dtype=jnp.int32)
    earlier = numbers[None, :] < numbers[:, None]
    slot_of = jnp.sum(
        ((device[None, :] == device[:, None]) & earlier).astype(jnp.int32), axis=1
    )
    by_column = (device % n_owner).reshape(n_owner, 2 * blocks_col)
    place = ((device // n_owner) * slots + slot_of).reshape(n_owner, 2 * blocks_col)
    lane_from = jnp.sum(jnp.where(by_column == col, place, 0), axis=1)
    home = lax.dynamic_slice_in_dim(by_column, col, 1, axis=0)
    wanted = jnp.asarray(lane_item)[core]
    item_hot = wanted[:, None] == jnp.arange(2 * blocks_col)[None, :]
    item_from = jnp.sum(jnp.where(item_hot, home, 0), axis=1)

    packed = pl.pallas_call(
        pack_kernel,
        out_shape=shape(n_dp, slots, packed_rows, 128),
        in_specs=[VMEM],
        out_specs=VMEM,
        compiler_params=params(12),
        cost_estimate=cost(0, 3 * 1024 * 1024),
    )(statistics[0, 0])
    spread = lax.all_to_all(packed, "dp", split_axis=0, concat_axis=0, tiled=True)
    sent = first_sent(grad_partial[0], tables)
    spread, sent = lax.optimization_barrier((spread, sent))
    lanes = pick(lane_from, spread.reshape(slots * n_dp, packed_rows, 128))
    lanes = lax.all_to_all(lanes, ("z", "core"), split_axis=0, concat_axis=0, tiled=True)
    gradient, left, right = gradient_sum(grad_partial[0], sent, tables)
    lanes = pick(item_from, lanes).reshape(n_dp, 2, packed_rows, 128)
    chunks = lax.all_to_all(lanes, "dp", split_axis=0, concat_axis=0, tiled=True)

    full = (order_b, order_b)
    update = pl.pallas_call(
        update_kernel,
        out_shape=shape(*full),
        in_specs=[VMEM] * 4,
        out_specs=VMEM,
        scratch_shapes=[
            pltpu.VMEM((2, order_b // 2, order_b // 2), jnp.float32),
            pltpu.VMEM((2,) + full, jnp.float32),
        ],
        compiler_params=params(40),
        cost_estimate=cost(40 * order_b**3, 6 * 1024 * 1024),
    )(chunks, gradient, left, right)
    rows = update.reshape(n_dp, slab, order_b)
    rows = lax.all_to_all(rows, "dp", split_axis=0, concat_axis=0, tiled=True)
    return pick(jnp.asarray(out_rows)[core], rows)


def solution(mesh):
    n_dp, n_owner = mesh.devices.shape
    fine = Mesh(mesh.devices.reshape(n_dp, n_owner // 2, 2), ("dp", "z", "core"))
    column = ("z", "core")
    in_specs = (P("dp", column, None, None), P("dp", column, None, None, None), P())
    out_specs = P(column, "dp", None)
    return jax.shard_map(body, mesh=fine, in_specs=in_specs, out_specs=out_specs, check_vma=False)
```

```python
import functools
import math

import jax
import jax.numpy as jnp
import numpy as np
from jax import lax
from jax.experimental import pallas as pl
from jax.experimental.pallas import tpu as pltpu
from jax.sharding import Mesh
from jax.sharding import PartitionSpec as P

decay_rate = 0.9
update_gain = 16.0
root_gain = 1.5

side_x = 4
chips = (
    ((0, 0), (0, 2), (2, 0), (1, 1), (3, 3)),
    ((1, 0), (1, 2), (3, 0), (2, 1), (0, 3)),
)
blocks_col = len(chips[0])
packed_rows = 72

VMEM = pl.BlockSpec(memory_space=pltpu.VMEM)
SMEM = pl.BlockSpec(memory_space=pltpu.SMEM)


def even(v):
    return v ^ 1


def odd(v):
    return side_x - 1 - v


def order(portion, core):
    first, later = (even, odd) if core == 0 else (odd, even)
    one, two = portion, 1 - portion
    return ((one, first), (one, later), (two, first), (two, later))


def pairs(portion, step):
    out = []
    for x in range(side_x):
        for y in range(side_x):
            for p in range(2):
                axis, pairing = order(portion, p)[step]
                to = (pairing(x), y) if axis == 0 else (x, pairing(y))
                out.append((2 * (side_x * x + y) + p, 2 * (side_x * to[0] + to[1]) + p))
    return out


def padded(items, count):
    assert len(items) <= count
    return (list(items) + [0] * count)[:count]


@functools.cache
def tree_tables():
    first, second, third = [], [], []
    for d in range(side_x * side_x):
        here = (d // side_x, d % side_x)
        for p in range(2):
            one, two, three = [], [], []
            for portion in range(2):
                steps = order(portion, p)
                axis, later = steps[1]
                at = [c[axis] for c in chips[p]]
                me = here[axis]
                kept = [j for j in range(blocks_col) if at[j] in (me, later(me))]
                one += padded([j for j in range(blocks_col) if j not in kept], 3)
                padded(kept, 3)
                go = [i for i, j in enumerate(kept) if at[j] == later(me)]
                stay = [i for i, j in enumerate(kept) if at[j] == me]
                for place in padded(go, 2) + padded(stay, 2):
                    two += [place, padded(kept, 3)[place]]
                mine = [kept[i] for i in stay]
                axis, later = steps[3]
                near = (here[axis], later(here[axis]))
                stay = [i for i, j in enumerate(mine) if chips[p][j][axis] in near]
                go = [i for i, j in enumerate(mine) if chips[p][j][axis] not in near]
                three += padded(go, 1) + padded(stay, 1)
            first.append(one)
            second.append(two)
            third.append(three)
    return [np.array(t, np.int32) for t in (first, second, third)]


@functools.cache
def home_tables():
    item = np.zeros((2, 2 * side_x * side_x), np.int32)
    rows = np.zeros((2, blocks_col), np.int32)
    for p in range(2):
        for j, (x, y) in enumerate(chips[p]):
            d = side_x * x + y
            rows[p, j] = d
            item[p, 2 * d : 2 * d + 2] = (2 * j, 2 * j + 1)
    return item, rows


def params(mib):
    return pltpu.CompilerParams(vmem_limit_bytes=mib * 1024 * 1024)


def add_rounded(a, b):
    return (a.astype(jnp.float32) + b.astype(jnp.float32)).astype(jnp.bfloat16)


def my_row(table):
    width = table.shape[0] // (2 * side_x * side_x)
    base = (2 * lax.axis_index("dp") + lax.axis_index("core")) * width
    return [table[base + k] for k in range(width)]


def choose_kernel(table, source, s0, s1):
    table = my_row(table)
    height = s0.shape[1]
    for h, sent in enumerate((s0, s1)):
        for u in range(3):
            sent[u] = source[table[3 * h + u], h * height : (h + 1) * height, :]


def first_sum_kernel(table, source, r0, r1, s0, s1, kept):
    table = my_row(table)
    height = r0.shape[1]
    for h, (got, sent) in enumerate(((r0, s0), (r1, s1))):
        for u in range(4):
            place, block = table[8 * h + 2 * u], table[8 * h + 2 * u + 1]
            total = add_rounded(source[block, h * height : (h + 1) * height, :], got[place])
            if u < 2:
                sent[u] = total
            else:
                kept[h, u - 2] = total


def second_sum_kernel(table, kept, r0, r1, s0, s1, next_kept):
    table = my_row(table)
    for h, (got, sent) in enumerate(((r0, s0), (r1, s1))):
        go, stay = table[2 * h], table[2 * h + 1]
        sent[...] = add_rounded(kept[h, go], got[go])
        next_kept[h] = add_rounded(kept[h, stay], got[stay])


def third_sum_kernel(kept, r0, r1, s0, s1):
    s0[...] = add_rounded(kept[0], r0[...])
    s1[...] = add_rounded(kept[1], r1[...])


def gram_kernel(a, b, r0, r1, out, left, right):
    half = a.shape[0]
    out[:half, :] = add_rounded(a[...], r0[...])
    out[half:, :] = add_rounded(b[...], r1[...])
    g = out[...]
    for gram, side in ((left, 1), (right, 0)):
        gram[...] = lax.dot_general(
            g, g, (((side,), (side,)), ((), ())), preferred_element_type=jnp.float32
        )


def pick_kernel(table, source, out):
    for i in range(out.shape[0]):
        out[i] = source[table[i]]


def pick(table, source):
    return pl.pallas_call(
        pick_kernel,
        out_shape=jax.ShapeDtypeStruct(table.shape + source.shape[1:], source.dtype),
        in_specs=[SMEM, VMEM],
        out_specs=VMEM,
        compiler_params=params(4),
        cost_estimate=pl.CostEstimate(
            flops=0, bytes_accessed=4 * table.shape[0] * 65536, transcendentals=0
        ),
    )(table, source)


def square_iotas(n):
    return (
        lax.broadcasted_iota(jnp.int32, (n, n), 0),
        lax.broadcasted_iota(jnp.int32, (n, n), 1),
    )


def pack_kernel(stats, out):
    half = stats.shape[1] // 2
    i, j = square_iotas(half)
    row = lax.broadcasted_iota(jnp.int32, (8, 128), 0)
    for q in range(stats.shape[0]):
        low = stats[q, half:, half:]
        mixed = jnp.where(i <= j, stats[q, :half, :half], low).astype(jnp.bfloat16)
        side = stats[q, :half, half:].astype(jnp.bfloat16)
        diagonal = jnp.sum(jnp.where(i == j, low, 0.0), axis=0, keepdims=True)
        tail = jnp.where(
            row == 0, diagonal[:, :128], jnp.where(row == 1, diagonal[:, 128:], 0.0)
        ).astype(jnp.bfloat16)
        strips = (mixed[:, :128], mixed[:, 128:], side[:, :128], side[:, 128:])
        for c in range(16):
            out[c, q, :64, :] = strips[c // 4][64 * (c % 4) : 64 * (c % 4) + 64, :]
            out[c, q, 64:, :] = tail


def product(a, b):
    return jnp.dot(
        a.astype(jnp.bfloat16), b.astype(jnp.bfloat16), preferred_element_type=jnp.float32
    )


def unpack(chunks, s, mixed, stat):
    half = mixed.shape[0]
    for c in range(16):
        strip = chunks[c, s, :64, :].astype(jnp.float32)
        rows = slice(64 * (c % 4), 64 * (c % 4) + 64)
        at = c // 4
        if at < 2:
            mixed[rows, 128 * at : 128 * at + 128] = strip
        else:
            stat[rows, half + 128 * (at - 2) : half + 128 * (at - 2) + 128] = strip
    tail = chunks[0, s, 64:, :].astype(jnp.float32)
    diagonal = jnp.concatenate([tail[0:1, :], tail[1:2, :]], axis=1)
    m = mixed[...]
    flipped = m.T
    i, j = square_iotas(half)
    stat[:half, :half] = jnp.where(i <= j, m, flipped)
    stat[half:, half:] = jnp.where(i > j, m, jnp.where(i == j, diagonal, flipped))
    stat[half:, :half] = stat[:half, half:].T


def update_kernel(chunks, gradient, left, right, out, mixed, stat):
    order_n = out.shape[0]
    sides = (0, 1)
    for s in sides:
        unpack(chunks, s, mixed.at[s], stat.at[s])
    i, j = square_iotas(order_n)
    scale, quarter, square = [], [], []
    for s, gram in zip(sides, (left, right)):
        new_stat = decay_rate * stat[s] + (1.0 - decay_rate) * gram[...]
        rounded = new_stat.astype(jnp.bfloat16)
        new_stat = rounded.astype(jnp.float32)
        squares = jnp.sum(new_stat * new_stat, axis=0, keepdims=True)
        frob_norm = jnp.sqrt(jnp.sum(squares, axis=1, keepdims=True) + 1e-06)
        scale.append(root_gain * math.sqrt(order_n) / frob_norm)
        part = 0.25 * scale[s]
        quarter.append(part * new_stat)
        square.append((part * part) * product(rounded, rounded))
    e2 = [jnp.where(i == j, 0.5625, 0.0) - 2.5 * quarter[s] + square[s] for s in sides]
    e4 = [2.0 * e2[s] + product(e2[s], e2[s]) for s in sides]
    rest = [square[s] - 1.25 * quarter[s] for s in sides]
    roots = []
    for s in sides:
        root = jnp.where(i == j, e2[s] + 1.0, e2[s]) + product(e4[s], rest[s])
        roots.append((jnp.sqrt(jnp.sqrt(scale[s])) * root).astype(jnp.bfloat16))
    applied = jnp.dot(gradient[...], roots[1], preferred_element_type=jnp.float32)
    update = jnp.dot(
        roots[0], applied.astype(jnp.bfloat16), preferred_element_type=jnp.float32
    )
    out[...] = (update_gain * update).astype(jnp.bfloat16)


def shape(*dims):
    return jax.ShapeDtypeStruct(dims, jnp.bfloat16)


def cost(flops, moved):
    return pl.CostEstimate(flops=flops, bytes_accessed=moved, transcendentals=0)


def exchange(arrays, step):
    return [
        lax.ppermute(a, ("dp", "core"), pairs(portion, step)) for portion, a in enumerate(arrays)
    ]


def first_sent(grad, tables):
    n, order_n = grad.shape[1], grad.shape[2]
    return pl.pallas_call(
        choose_kernel,
        out_shape=[shape(3, n // 2, order_n)] * 2,
        in_specs=[SMEM, VMEM],
        out_specs=[VMEM] * 2,
        compiler_params=params(12),
        cost_estimate=cost(0, 6 * n * order_n),
    )(tables[0], grad)


def gradient_sum(grad, got, tables):
    n, order_n = grad.shape[1], grad.shape[2]
    half = n // 2
    *sent, kept = pl.pallas_call(
        first_sum_kernel,
        out_shape=[shape(2, half, order_n)] * 2 + [shape(2, 2, half, order_n)],
        in_specs=[SMEM] + [VMEM] * 3,
        out_specs=[VMEM] * 3,
        compiler_params=params(16),
        cost_estimate=cost(5 * 10**11, 10**9),
    )(tables[1], grad, *got)
    *sent, kept = pl.pallas_call(
        second_sum_kernel,
        out_shape=[shape(half, order_n)] * 2 + [shape(2, half, order_n)],
        in_specs=[SMEM] + [VMEM] * 3,
        out_specs=[VMEM] * 3,
        compiler_params=params(12),
        cost_estimate=cost(0, 4 * 1024 * 1024),
    )(tables[2], kept, *exchange(sent, 1))
    sent = pl.pallas_call(
        third_sum_kernel,
        out_shape=[shape(half, order_n)] * 2,
        in_specs=[VMEM] * 3,
        out_specs=[VMEM] * 2,
        compiler_params=params(8),
        cost_estimate=cost(0, 4 * 1024 * 1024),
    )(kept, *exchange(sent, 2))
    square = jax.ShapeDtypeStruct((n, order_n), jnp.float32)
    return pl.pallas_call(
        gram_kernel,
        out_shape=[shape(n, order_n), square, square],
        in_specs=[VMEM] * 4,
        out_specs=[VMEM] * 3,
        compiler_params=params(16),
        cost_estimate=cost(4 * n**3, 4 * 1024 * 1024),
    )(*sent, *exchange(sent, 3))


def body(grad_partial, statistics, owner_table):
    n_dp = lax.axis_size("dp")
    n_owner = lax.axis_size("z") * 2
    order_b = grad_partial.shape[3]
    slab = order_b // n_dp
    slots = statistics.shape[2]
    core = lax.axis_index("core")
    col = 2 * lax.axis_index("z") + core
    lane_item, out_rows = home_tables()
    tables = [jnp.asarray(t.reshape(-1)) for t in tree_tables()]

    device = owner_table.reshape(-1)
    numbers = jnp.arange(device.shape[0], dtype=jnp.int32)
    earlier = numbers[None, :] < numbers[:, None]
    slot_of = jnp.sum(
        ((device[None, :] == device[:, None]) & earlier).astype(jnp.int32), axis=1
    )
    by_column = (device % n_owner).reshape(n_owner, 2 * blocks_col)
    place = ((device // n_owner) * slots + slot_of).reshape(n_owner, 2 * blocks_col)
    lane_from = jnp.sum(jnp.where(by_column == col, place, 0), axis=1)
    home = lax.dynamic_slice_in_dim(by_column, col, 1, axis=0)
    wanted = jnp.asarray(lane_item)[core]
    item_hot = wanted[:, None] == jnp.arange(2 * blocks_col)[None, :]
    item_from = jnp.sum(jnp.where(item_hot, home, 0), axis=1)

    packed = pl.pallas_call(
        pack_kernel,
        out_shape=shape(n_dp, slots, packed_rows, 128),
        in_specs=[VMEM],
        out_specs=VMEM,
        compiler_params=params(12),
        cost_estimate=cost(0, 3 * 1024 * 1024),
    )(statistics[0, 0])
    spread = lax.all_to_all(packed, "dp", split_axis=0, concat_axis=0, tiled=True)
    sent = first_sent(grad_partial[0], tables)
    spread, _ = lax.optimization_barrier((spread, sent))
    got = exchange(sent, 0)
    lanes = pick(lane_from, spread.reshape(slots * n_dp, packed_rows, 128))
    lanes = lax.all_to_all(lanes, ("z", "core"), split_axis=0, concat_axis=0, tiled=True)
    gradient, left, right = gradient_sum(grad_partial[0], got, tables)
    lanes = pick(item_from, lanes).reshape(n_dp, 2, packed_rows, 128)
    chunks = lax.all_to_all(lanes, "dp", split_axis=0, concat_axis=0, tiled=True)

    full = (order_b, order_b)
    update = pl.pallas_call(
        update_kernel,
        out_shape=shape(*full),
        in_specs=[VMEM] * 4,
        out_specs=VMEM,
        scratch_shapes=[
            pltpu.VMEM((2, order_b // 2, order_b // 2), jnp.float32),
            pltpu.VMEM((2,) + full, jnp.float32),
        ],
        compiler_params=params(40),
        cost_estimate=cost(16 * order_b**3, 6 * 1024 * 1024),
    )(chunks, gradient, left, right)
    rows = update.reshape(n_dp, slab, order_b)
    rows = lax.all_to_all(rows, "dp", split_axis=0, concat_axis=0, tiled=True)
    return pick(jnp.asarray(out_rows)[core], rows)


def solution(mesh):
    n_dp, n_owner = mesh.devices.shape
    fine = Mesh(mesh.devices.reshape(n_dp, n_owner // 2, 2), ("dp", "z", "core"))
    column = ("z", "core")
    in_specs = (P("dp", column, None, None), P("dp", column, None, None, None), P())
    out_specs = P(column, "dp", None)
    return jax.shard_map(body, mesh=fine, in_specs=in_specs, out_specs=out_specs, check_vma=False)
```

```python
import functools
import math

import jax
import jax.numpy as jnp
import numpy as np
from jax import lax
from jax.experimental import pallas as pl
from jax.experimental.pallas import tpu as pltpu
from jax.sharding import Mesh
from jax.sharding import PartitionSpec as P

decay_rate = 0.9
update_gain = 16.0
root_gain = 1.5

side_x = 4
chips = (
    ((0, 0), (0, 2), (2, 0), (1, 1), (3, 3)),
    ((1, 0), (1, 2), (3, 0), (2, 1), (0, 3)),
)
blocks_col = len(chips[0])
packed_rows = 72

long_flops = 5 * 10**11

VMEM = pl.BlockSpec(memory_space=pltpu.VMEM)
SMEM = pl.BlockSpec(memory_space=pltpu.SMEM)


def even(v):
    return v ^ 1


def odd(v):
    return side_x - 1 - v


def order(portion, core):
    first, later = (even, odd) if core == 0 else (odd, even)
    one, two = portion, 1 - portion
    return ((one, first), (one, later), (two, first), (two, later))


def pairs(portion, step):
    out = []
    for x in range(side_x):
        for y in range(side_x):
            for p in range(2):
                axis, pairing = order(portion, p)[step]
                to = (pairing(x), y) if axis == 0 else (x, pairing(y))
                out.append((2 * (side_x * x + y) + p, 2 * (side_x * to[0] + to[1]) + p))
    return out


def padded(items, count):
    assert len(items) <= count
    return (list(items) + [0] * count)[:count]


@functools.cache
def tree_tables():
    first, second, third = [], [], []
    for d in range(side_x * side_x):
        here = (d // side_x, d % side_x)
        for p in range(2):
            one, two, three = [], [], []
            for portion in range(2):
                steps = order(portion, p)
                axis, later = steps[1]
                at = [c[axis] for c in chips[p]]
                me = here[axis]
                kept = [j for j in range(blocks_col) if at[j] in (me, later(me))]
                one += padded([j for j in range(blocks_col) if j not in kept], 3)
                padded(kept, 3)
                go = [i for i, j in enumerate(kept) if at[j] == later(me)]
                stay = [i for i, j in enumerate(kept) if at[j] == me]
                for place in padded(go, 2) + padded(stay, 2):
                    two += [place, padded(kept, 3)[place]]
                mine = [kept[i] for i in stay]
                axis, later = steps[3]
                near = (here[axis], later(here[axis]))
                stay = [i for i, j in enumerate(mine) if chips[p][j][axis] in near]
                go = [i for i, j in enumerate(mine) if chips[p][j][axis] not in near]
                three += padded(go, 1) + padded(stay, 1)
            first.append(one)
            second.append(two)
            third.append(three)
    return [np.array(t, np.int32) for t in (first, second, third)]


@functools.cache
def home_tables():
    item = np.zeros((2, 2 * side_x * side_x), np.int32)
    rows = np.zeros((2, blocks_col), np.int32)
    for p in range(2):
        for j, (x, y) in enumerate(chips[p]):
            d = side_x * x + y
            rows[p, j] = d
            item[p, 2 * d : 2 * d + 2] = (2 * j, 2 * j + 1)
    return item, rows


def params(mib):
    return pltpu.CompilerParams(vmem_limit_bytes=mib * 1024 * 1024)


def add_rounded(a, b):
    return (a.astype(jnp.float32) + b.astype(jnp.float32)).astype(jnp.bfloat16)


def my_row(table):
    width = table.shape[0] // (2 * side_x * side_x)
    base = (2 * lax.axis_index("dp") + lax.axis_index("core")) * width
    return [table[base + k] for k in range(width)]


def choose_kernel(table, source, s0, s1):
    table = my_row(table)
    height = s0.shape[1]
    for h, sent in enumerate((s0, s1)):
        for u in range(3):
            sent[u] = source[table[3 * h + u], h * height : (h + 1) * height, :]


def first_sum_kernel(table, source, r0, r1, s0, s1, kept):
    table = my_row(table)
    height = r0.shape[1]
    for h, (got, sent) in enumerate(((r0, s0), (r1, s1))):
        for u in range(4):
            place, block = table[8 * h + 2 * u], table[8 * h + 2 * u + 1]
            total = add_rounded(source[block, h * height : (h + 1) * height, :], got[place])
            if u < 2:
                sent[u] = total
            else:
                kept[h, u - 2] = total


def second_sum_kernel(table, kept, r0, r1, s0, s1, next_kept):
    table = my_row(table)
    for h, (got, sent) in enumerate(((r0, s0), (r1, s1))):
        go, stay = table[2 * h], table[2 * h + 1]
        sent[...] = add_rounded(kept[h, go], got[go])
        next_kept[h] = add_rounded(kept[h, stay], got[stay])


def third_sum_kernel(kept, r0, r1, s0, s1):
    s0[...] = add_rounded(kept[0], r0[...])
    s1[...] = add_rounded(kept[1], r1[...])


def gram_kernel(a, b, r0, r1, out, left, right):
    half = a.shape[0]
    out[:half, :] = add_rounded(a[...], r0[...])
    out[half:, :] = add_rounded(b[...], r1[...])
    g = out[...]
    for gram, side in ((left, 1), (right, 0)):
        gram[...] = lax.dot_general(
            g, g, (((side,), (side,)), ((), ())), preferred_element_type=jnp.float32
        )


def pick_kernel(table, source, out):
    for i in range(out.shape[0]):
        out[i] = source[table[i]]


def pick(table, source, flops=0):
    return pl.pallas_call(
        pick_kernel,
        out_shape=jax.ShapeDtypeStruct(table.shape + source.shape[1:], source.dtype),
        in_specs=[SMEM, VMEM],
        out_specs=VMEM,
        compiler_params=params(4),
        cost_estimate=pl.CostEstimate(
            flops=flops, bytes_accessed=4 * table.shape[0] * 65536, transcendentals=0
        ),
    )(table, source)


def square_iotas(n):
    return (
        lax.broadcasted_iota(jnp.int32, (n, n), 0),
        lax.broadcasted_iota(jnp.int32, (n, n), 1),
    )


def pack_kernel(stats, out):
    half = stats.shape[1] // 2
    i, j = square_iotas(half)
    row = lax.broadcasted_iota(jnp.int32, (8, 128), 0)
    for q in range(stats.shape[0]):
        low = stats[q, half:, half:]
        mixed = jnp.where(i <= j, stats[q, :half, :half], low).astype(jnp.bfloat16)
        side = stats[q, :half, half:].astype(jnp.bfloat16)
        diagonal = jnp.sum(jnp.where(i == j, low, 0.0), axis=0, keepdims=True)
        tail = jnp.where(
            row == 0, diagonal[:, :128], jnp.where(row == 1, diagonal[:, 128:], 0.0)
        ).astype(jnp.bfloat16)
        strips = (mixed[:, :128], mixed[:, 128:], side[:, :128], side[:, 128:])
        for c in range(16):
            out[c, q, :64, :] = strips[c // 4][64 * (c % 4) : 64 * (c % 4) + 64, :]
            out[c, q, 64:, :] = tail


def product(a, b):
    return jnp.dot(
        a.astype(jnp.bfloat16), b.astype(jnp.bfloat16), preferred_element_type=jnp.float32
    )


def unpack(chunks, s, mixed, stat):
    half = mixed.shape[0]
    for c in range(16):
        strip = chunks[c, s, :64, :].astype(jnp.float32)
        rows = slice(64 * (c % 4), 64 * (c % 4) + 64)
        at = c // 4
        if at < 2:
            mixed[rows, 128 * at : 128 * at + 128] = strip
        else:
            stat[rows, half + 128 * (at - 2) : half + 128 * (at - 2) + 128] = strip
    tail = chunks[0, s, 64:, :].astype(jnp.float32)
    diagonal = jnp.concatenate([tail[0:1, :], tail[1:2, :]], axis=1)
    m = mixed[...]
    flipped = m.T
    i, j = square_iotas(half)
    stat[:half, :half] = jnp.where(i <= j, m, flipped)
    stat[half:, half:] = jnp.where(i > j, m, jnp.where(i == j, diagonal, flipped))
    stat[half:, :half] = stat[:half, half:].T


def update_kernel(chunks, gradient, left, right, out, mixed, stat):
    order_n = out.shape[0]
    sides = (0, 1)
    for s in sides:
        unpack(chunks, s, mixed.at[s], stat.at[s])
    i, j = square_iotas(order_n)
    scale, quarter, square = [], [], []
    for s, gram in zip(sides, (left, right)):
        new_stat = decay_rate * stat[s] + (1.0 - decay_rate) * gram[...]
        rounded = new_stat.astype(jnp.bfloat16)
        new_stat = rounded.astype(jnp.float32)
        squares = jnp.sum(new_stat * new_stat, axis=0, keepdims=True)
        frob_norm = jnp.sqrt(jnp.sum(squares, axis=1, keepdims=True) + 1e-06)
        scale.append(root_gain * math.sqrt(order_n) / frob_norm)
        part = 0.25 * scale[s]
        quarter.append(part * new_stat)
        square.append((part * part) * product(rounded, rounded))
    e2 = [jnp.where(i == j, 0.5625, 0.0) - 2.5 * quarter[s] + square[s] for s in sides]
    e4 = [2.0 * e2[s] + product(e2[s], e2[s]) for s in sides]
    rest = [square[s] - 1.25 * quarter[s] for s in sides]
    roots = []
    for s in sides:
        root = jnp.where(i == j, e2[s] + 1.0, e2[s]) + product(e4[s], rest[s])
        roots.append((jnp.sqrt(jnp.sqrt(scale[s])) * root).astype(jnp.bfloat16))
    applied = jnp.dot(gradient[...], roots[1], preferred_element_type=jnp.float32)
    update = jnp.dot(
        roots[0], applied.astype(jnp.bfloat16), preferred_element_type=jnp.float32
    )
    out[...] = (update_gain * update).astype(jnp.bfloat16)


def shape(*dims):
    return jax.ShapeDtypeStruct(dims, jnp.bfloat16)


def cost(flops, moved):
    return pl.CostEstimate(flops=flops, bytes_accessed=moved, transcendentals=0)


def exchange(arrays, step):
    return [
        lax.ppermute(a, ("dp", "core"), pairs(portion, step)) for portion, a in enumerate(arrays)
    ]


def first_sent(grad, tables):
    n, order_n = grad.shape[1], grad.shape[2]
    return pl.pallas_call(
        choose_kernel,
        out_shape=[shape(3, n // 2, order_n)] * 2,
        in_specs=[SMEM, VMEM],
        out_specs=[VMEM] * 2,
        compiler_params=params(12),
        cost_estimate=cost(0, 6 * n * order_n),
    )(tables[0], grad)


def gradient_sum(grad, got, tables):
    n, order_n = grad.shape[1], grad.shape[2]
    half = n // 2
    *sent, kept = pl.pallas_call(
        first_sum_kernel,
        out_shape=[shape(2, half, order_n)] * 2 + [shape(2, 2, half, order_n)],
        in_specs=[SMEM] + [VMEM] * 3,
        out_specs=[VMEM] * 3,
        compiler_params=params(16),
        cost_estimate=cost(long_flops, 10**9),
    )(tables[1], grad, *got)
    *sent, kept = pl.pallas_call(
        second_sum_kernel,
        out_shape=[shape(half, order_n)] * 2 + [shape(2, half, order_n)],
        in_specs=[SMEM] + [VMEM] * 3,
        out_specs=[VMEM] * 3,
        compiler_params=params(12),
        cost_estimate=cost(0, 4 * 1024 * 1024),
    )(tables[2], kept, *exchange(sent, 1))
    sent = pl.pallas_call(
        third_sum_kernel,
        out_shape=[shape(half, order_n)] * 2,
        in_specs=[VMEM] * 3,
        out_specs=[VMEM] * 2,
        compiler_params=params(8),
        cost_estimate=cost(0, 4 * 1024 * 1024),
    )(kept, *exchange(sent, 2))
    square = jax.ShapeDtypeStruct((n, order_n), jnp.float32)
    return pl.pallas_call(
        gram_kernel,
        out_shape=[shape(n, order_n), square, square],
        in_specs=[VMEM] * 4,
        out_specs=[VMEM] * 3,
        compiler_params=params(16),
        cost_estimate=cost(long_flops, 10**9),
    )(*sent, *exchange(sent, 3))


def body(grad_partial, statistics, owner_table):
    n_dp = lax.axis_size("dp")
    n_owner = lax.axis_size("z") * 2
    order_b = grad_partial.shape[3]
    slab = order_b // n_dp
    slots = statistics.shape[2]
    core = lax.axis_index("core")
    col = 2 * lax.axis_index("z") + core
    lane_item, out_rows = home_tables()
    tables = [jnp.asarray(t.reshape(-1)) for t in tree_tables()]

    device = owner_table.reshape(-1)
    numbers = jnp.arange(device.shape[0], dtype=jnp.int32)
    earlier = numbers[None, :] < numbers[:, None]
    slot_of = jnp.sum(
        ((device[None, :] == device[:, None]) & earlier).astype(jnp.int32), axis=1
    )
    by_column = (device % n_owner).reshape(n_owner, 2 * blocks_col)
    place = ((device // n_owner) * slots + slot_of).reshape(n_owner, 2 * blocks_col)
    lane_from = jnp.sum(jnp.where(by_column == col, place, 0), axis=1)
    home = lax.dynamic_slice_in_dim(by_column, col, 1, axis=0)
    wanted = jnp.asarray(lane_item)[core]
    item_hot = wanted[:, None] == jnp.arange(2 * blocks_col)[None, :]
    item_from = jnp.sum(jnp.where(item_hot, home, 0), axis=1)

    packed = pl.pallas_call(
        pack_kernel,
        out_shape=shape(n_dp, slots, packed_rows, 128),
        in_specs=[VMEM],
        out_specs=VMEM,
        compiler_params=params(12),
        cost_estimate=cost(0, 3 * 1024 * 1024),
    )(statistics[0, 0])
    spread = lax.all_to_all(packed, "dp", split_axis=0, concat_axis=0, tiled=True)
    sent = first_sent(grad_partial[0], tables)
    spread, _ = lax.optimization_barrier((spread, sent))
    got = exchange(sent, 0)
    lanes = pick(lane_from, spread.reshape(slots * n_dp, packed_rows, 128), long_flops)
    lanes = lax.all_to_all(lanes, ("z", "core"), split_axis=0, concat_axis=0, tiled=True)
    gradient, left, right = gradient_sum(grad_partial[0], got, tables)
    lanes = pick(item_from, lanes).reshape(n_dp, 2, packed_rows, 128)
    chunks = lax.all_to_all(lanes, "dp", split_axis=0, concat_axis=0, tiled=True)

    full = (order_b, order_b)
    update = pl.pallas_call(
        update_kernel,
        out_shape=shape(*full),
        in_specs=[VMEM] * 4,
        out_specs=VMEM,
        scratch_shapes=[
            pltpu.VMEM((2, order_b // 2, order_b // 2), jnp.float32),
            pltpu.VMEM((2,) + full, jnp.float32),
        ],
        compiler_params=params(40),
        cost_estimate=cost(16 * order_b**3, 6 * 1024 * 1024),
    )(chunks, gradient, left, right)
    rows = update.reshape(n_dp, slab, order_b)
    rows = lax.all_to_all(rows, "dp", split_axis=0, concat_axis=0, tiled=True)
    return pick(jnp.asarray(out_rows)[core], rows)


def solution(mesh):
    n_dp, n_owner = mesh.devices.shape
    fine = Mesh(mesh.devices.reshape(n_dp, n_owner // 2, 2), ("dp", "z", "core"))
    column = ("z", "core")
    in_specs = (P("dp", column, None, None), P("dp", column, None, None, None), P())
    out_specs = P(column, "dp", None)
    return jax.shard_map(body, mesh=fine, in_specs=in_specs, out_specs=out_specs, check_vma=False)
```

```python
import functools
import math

import jax
import jax.numpy as jnp
import numpy as np
from jax import lax
from jax.experimental import pallas as pl
from jax.experimental.pallas import tpu as pltpu
from jax.sharding import Mesh
from jax.sharding import PartitionSpec as P

decay_rate = 0.9
update_gain = 16.0
root_gain = 1.5

side_x = 4
chips = (
    ((0, 0), (0, 2), (2, 0), (1, 1), (3, 3)),
    ((1, 0), (1, 2), (3, 0), (2, 1), (0, 3)),
)
blocks_col = len(chips[0])
packed_rows = 72

long_flops = 10**11

VMEM = pl.BlockSpec(memory_space=pltpu.VMEM)
SMEM = pl.BlockSpec(memory_space=pltpu.SMEM)


def even(v):
    return v ^ 1


def odd(v):
    return side_x - 1 - v


def order(portion, core):
    first, later = (even, odd) if core == 0 else (odd, even)
    one, two = portion, 1 - portion
    return ((one, first), (one, later), (two, first), (two, later))


def pairs(portion, step):
    out = []
    for x in range(side_x):
        for y in range(side_x):
            for p in range(2):
                axis, pairing = order(portion, p)[step]
                to = (pairing(x), y) if axis == 0 else (x, pairing(y))
                out.append((2 * (side_x * x + y) + p, 2 * (side_x * to[0] + to[1]) + p))
    return out


def padded(items, count):
    assert len(items) <= count
    return (list(items) + [0] * count)[:count]


@functools.cache
def tree_tables():
    first, second, third = [], [], []
    for d in range(side_x * side_x):
        here = (d // side_x, d % side_x)
        for p in range(2):
            one, two, three = [], [], []
            for portion in range(2):
                steps = order(portion, p)
                axis, later = steps[1]
                at = [c[axis] for c in chips[p]]
                me = here[axis]
                kept = [j for j in range(blocks_col) if at[j] in (me, later(me))]
                one += padded([j for j in range(blocks_col) if j not in kept], 3)
                padded(kept, 3)
                go = [i for i, j in enumerate(kept) if at[j] == later(me)]
                stay = [i for i, j in enumerate(kept) if at[j] == me]
                for place in padded(go, 2) + padded(stay, 2):
                    two += [place, padded(kept, 3)[place]]
                mine = [kept[i] for i in stay]
                axis, later = steps[3]
                near = (here[axis], later(here[axis]))
                stay = [i for i, j in enumerate(mine) if chips[p][j][axis] in near]
                go = [i for i, j in enumerate(mine) if chips[p][j][axis] not in near]
                three += padded(go, 1) + padded(stay, 1)
            first.append(one)
            second.append(two)
            third.append(three)
    return [np.array(t, np.int32) for t in (first, second, third)]


@functools.cache
def home_tables():
    item = np.zeros((2, 2 * side_x * side_x), np.int32)
    for p in range(2):
        for j, (x, y) in enumerate(chips[p]):
            d = side_x * x + y
            item[p, 2 * d : 2 * d + 2] = (2 * j, 2 * j + 1)
    return item


def params(mib):
    return pltpu.CompilerParams(vmem_limit_bytes=mib * 1024 * 1024)


def add_rounded(a, b):
    return (a.astype(jnp.float32) + b.astype(jnp.float32)).astype(jnp.bfloat16)


def my_row(table):
    width = table.shape[0] // (2 * side_x * side_x)
    base = (2 * lax.axis_index("dp") + lax.axis_index("core")) * width
    return [table[base + k] for k in range(width)]


def choose_kernel(table, source, s0, s1):
    table = my_row(table)
    height = s0.shape[1]
    for h, sent in enumerate((s0, s1)):
        for u in range(3):
            sent[u] = source[table[3 * h + u], h * height : (h + 1) * height, :]


def first_sum_kernel(table, source, r0, r1, s0, s1, kept):
    table = my_row(table)
    height = r0.shape[1]
    for h, (got, sent) in enumerate(((r0, s0), (r1, s1))):
        for u in range(4):
            place, block = table[8 * h + 2 * u], table[8 * h + 2 * u + 1]
            total = add_rounded(source[block, h * height : (h + 1) * height, :], got[place])
            if u < 2:
                sent[u] = total
            else:
                kept[h, u - 2] = total


def second_sum_kernel(table, kept, r0, r1, s0, s1, next_kept):
    table = my_row(table)
    for h, (got, sent) in enumerate(((r0, s0), (r1, s1))):
        go, stay = table[2 * h], table[2 * h + 1]
        sent[...] = add_rounded(kept[h, go], got[go])
        next_kept[h] = add_rounded(kept[h, stay], got[stay])


def third_sum_kernel(kept, r0, r1, s0, s1):
    s0[...] = add_rounded(kept[0], r0[...])
    s1[...] = add_rounded(kept[1], r1[...])


def gram_kernel(a, b, r0, r1, out, left, right):
    half = a.shape[0]
    out[:half, :] = add_rounded(a[...], r0[...])
    out[half:, :] = add_rounded(b[...], r1[...])
    g = out[...]
    for gram, side in ((left, 1), (right, 0)):
        gram[...] = lax.dot_general(
            g, g, (((side,), (side,)), ((), ())), preferred_element_type=jnp.float32
        )


def pick_kernel(table, source, out):
    for i in range(out.shape[0]):
        out[i] = source[table[i]]


def pick(table, source, flops=0):
    return pl.pallas_call(
        pick_kernel,
        out_shape=jax.ShapeDtypeStruct(table.shape + source.shape[1:], source.dtype),
        in_specs=[SMEM, VMEM],
        out_specs=VMEM,
        compiler_params=params(4),
        cost_estimate=pl.CostEstimate(
            flops=flops, bytes_accessed=4 * table.shape[0] * 65536, transcendentals=0
        ),
    )(table, source)


def output_kernel(source, out, sems):
    core = lax.axis_index("core")
    for p in range(2):

        @pl.when(core == p)
        def _():
            copies = [
                pltpu.make_async_copy(source.at[side_x * x + y], out.at[j], sems.at[j])
                for j, (x, y) in enumerate(chips[p])
            ]
            for copy in copies:
                copy.start()
            for copy in copies:
                copy.wait()


def square_iotas(n):
    return (
        lax.broadcasted_iota(jnp.int32, (n, n), 0),
        lax.broadcasted_iota(jnp.int32, (n, n), 1),
    )


def pack_kernel(stats, out):
    half = stats.shape[1] // 2
    i, j = square_iotas(half)
    row = lax.broadcasted_iota(jnp.int32, (8, 128), 0)
    for q in range(stats.shape[0]):
        low = stats[q, half:, half:]
        mixed = jnp.where(i <= j, stats[q, :half, :half], low).astype(jnp.bfloat16)
        side = stats[q, :half, half:].astype(jnp.bfloat16)
        diagonal = jnp.sum(jnp.where(i == j, low, 0.0), axis=0, keepdims=True)
        tail = jnp.where(
            row == 0, diagonal[:, :128], jnp.where(row == 1, diagonal[:, 128:], 0.0)
        ).astype(jnp.bfloat16)
        strips = (mixed[:, :128], mixed[:, 128:], side[:, :128], side[:, 128:])
        for c in range(16):
            out[c, q, :64, :] = strips[c // 4][64 * (c % 4) : 64 * (c % 4) + 64, :]
            out[c, q, 64:, :] = tail


def product(a, b):
    return jnp.dot(
        a.astype(jnp.bfloat16), b.astype(jnp.bfloat16), preferred_element_type=jnp.float32
    )


def unpack(chunks, s, mixed, stat):
    half = mixed.shape[0]
    for c in range(16):
        strip = chunks[c, s, :64, :].astype(jnp.float32)
        rows = slice(64 * (c % 4), 64 * (c % 4) + 64)
        at = c // 4
        if at < 2:
            mixed[rows, 128 * at : 128 * at + 128] = strip
        else:
            stat[rows, half + 128 * (at - 2) : half + 128 * (at - 2) + 128] = strip
    tail = chunks[0, s, 64:, :].astype(jnp.float32)
    diagonal = jnp.concatenate([tail[0:1, :], tail[1:2, :]], axis=1)
    m = mixed[...]
    flipped = m.T
    i, j = square_iotas(half)
    stat[:half, :half] = jnp.where(i <= j, m, flipped)
    stat[half:, half:] = jnp.where(i > j, m, jnp.where(i == j, diagonal, flipped))
    stat[half:, :half] = stat[:half, half:].T


def update_kernel(chunks, gradient, left, right, out, mixed, stat):
    order_n = out.shape[0]
    sides = (0, 1)
    for s in sides:
        unpack(chunks, s, mixed.at[s], stat.at[s])
    i, j = square_iotas(order_n)
    scale, quarter, square = [], [], []
    for s, gram in zip(sides, (left, right)):
        new_stat = decay_rate * stat[s] + (1.0 - decay_rate) * gram[...]
        rounded = new_stat.astype(jnp.bfloat16)
        new_stat = rounded.astype(jnp.float32)
        squares = jnp.sum(new_stat * new_stat, axis=0, keepdims=True)
        frob_norm = jnp.sqrt(jnp.sum(squares, axis=1, keepdims=True) + 1e-06)
        scale.append(root_gain * math.sqrt(order_n) / frob_norm)
        part = 0.25 * scale[s]
        quarter.append(part * new_stat)
        square.append((part * part) * product(rounded, rounded))
    e2 = [jnp.where(i == j, 0.5625, 0.0) - 2.5 * quarter[s] + square[s] for s in sides]
    e4 = [2.0 * e2[s] + product(e2[s], e2[s]) for s in sides]
    rest = [square[s] - 1.25 * quarter[s] for s in sides]
    roots = []
    for s in sides:
        root = jnp.where(i == j, e2[s] + 1.0, e2[s]) + product(e4[s], rest[s])
        roots.append((jnp.sqrt(jnp.sqrt(scale[s])) * root).astype(jnp.bfloat16))
    applied = jnp.dot(gradient[...], roots[1], preferred_element_type=jnp.float32)
    update = jnp.dot(
        roots[0], applied.astype(jnp.bfloat16), preferred_element_type=jnp.float32
    )
    out[...] = (update_gain * update).astype(jnp.bfloat16)


def shape(*dims):
    return jax.ShapeDtypeStruct(dims, jnp.bfloat16)


def cost(flops, moved):
    return pl.CostEstimate(flops=flops, bytes_accessed=moved, transcendentals=0)


def exchange(arrays, step):
    return [
        lax.ppermute(a, ("dp", "core"), pairs(portion, step)) for portion, a in enumerate(arrays)
    ]


def first_sent(grad, tables):
    n, order_n = grad.shape[1], grad.shape[2]
    return pl.pallas_call(
        choose_kernel,
        out_shape=[shape(3, n // 2, order_n)] * 2,
        in_specs=[SMEM, VMEM],
        out_specs=[VMEM] * 2,
        compiler_params=params(12),
        cost_estimate=cost(0, 6 * n * order_n),
    )(tables[0], grad)


def gradient_sum(grad, got, tables):
    n, order_n = grad.shape[1], grad.shape[2]
    half = n // 2
    *sent, kept = pl.pallas_call(
        first_sum_kernel,
        out_shape=[shape(2, half, order_n)] * 2 + [shape(2, 2, half, order_n)],
        in_specs=[SMEM] + [VMEM] * 3,
        out_specs=[VMEM] * 3,
        compiler_params=params(16),
        cost_estimate=cost(long_flops, 4 * 1024 * 1024),
    )(tables[1], grad, *got)
    *sent, kept = pl.pallas_call(
        second_sum_kernel,
        out_shape=[shape(half, order_n)] * 2 + [shape(2, half, order_n)],
        in_specs=[SMEM] + [VMEM] * 3,
        out_specs=[VMEM] * 3,
        compiler_params=params(12),
        cost_estimate=cost(0, 4 * 1024 * 1024),
    )(tables[2], kept, *exchange(sent, 1))
    sent = pl.pallas_call(
        third_sum_kernel,
        out_shape=[shape(half, order_n)] * 2,
        in_specs=[VMEM] * 3,
        out_specs=[VMEM] * 2,
        compiler_params=params(8),
        cost_estimate=cost(0, 4 * 1024 * 1024),
    )(kept, *exchange(sent, 2))
    square = jax.ShapeDtypeStruct((n, order_n), jnp.float32)
    return pl.pallas_call(
        gram_kernel,
        out_shape=[shape(n, order_n), square, square],
        in_specs=[VMEM] * 4,
        out_specs=[VMEM] * 3,
        compiler_params=params(16),
        cost_estimate=cost(long_flops // 2, 4 * 1024 * 1024),
    )(*sent, *exchange(sent, 3))


def body(grad_partial, statistics, owner_table):
    n_dp = lax.axis_size("dp")
    n_owner = lax.axis_size("z") * 2
    order_b = grad_partial.shape[3]
    slab = order_b // n_dp
    slots = statistics.shape[2]
    core = lax.axis_index("core")
    col = 2 * lax.axis_index("z") + core
    lane_item = home_tables()
    tables = [jnp.asarray(t.reshape(-1)) for t in tree_tables()]

    device = owner_table.reshape(-1)
    numbers = jnp.arange(device.shape[0], dtype=jnp.int32)
    earlier = numbers[None, :] < numbers[:, None]
    slot_of = jnp.sum(
        ((device[None, :] == device[:, None]) & earlier).astype(jnp.int32), axis=1
    )
    by_column = (device % n_owner).reshape(n_owner, 2 * blocks_col)
    place = ((device // n_owner) * slots + slot_of).reshape(n_owner, 2 * blocks_col)
    lane_from = jnp.sum(jnp.where(by_column == col, place, 0), axis=1)
    home = lax.dynamic_slice_in_dim(by_column, col, 1, axis=0)
    wanted = jnp.asarray(lane_item)[core]
    item_hot = wanted[:, None] == jnp.arange(2 * blocks_col)[None, :]
    item_from = jnp.sum(jnp.where(item_hot, home, 0), axis=1)

    packed = pl.pallas_call(
        pack_kernel,
        out_shape=shape(n_dp, slots, packed_rows, 128),
        in_specs=[VMEM],
        out_specs=VMEM,
        compiler_params=params(12),
        cost_estimate=cost(0, 3 * 1024 * 1024),
    )(statistics[0, 0])
    spread = lax.all_to_all(packed, "dp", split_axis=0, concat_axis=0, tiled=True)
    sent = first_sent(grad_partial[0], tables)
    spread, _ = lax.optimization_barrier((spread, sent))
    got = exchange(sent, 0)
    lanes = pick(lane_from, spread.reshape(slots * n_dp, packed_rows, 128), long_flops // 3)
    lanes = lax.all_to_all(lanes, ("z", "core"), split_axis=0, concat_axis=0, tiled=True)
    gradient, left, right = gradient_sum(grad_partial[0], got, tables)
    lanes = pick(item_from, lanes).reshape(n_dp, 2, packed_rows, 128)
    chunks = lax.all_to_all(lanes, "dp", split_axis=0, concat_axis=0, tiled=True)

    full = (order_b, order_b)
    update = pl.pallas_call(
        update_kernel,
        out_shape=shape(*full),
        in_specs=[VMEM] * 4,
        out_specs=VMEM,
        scratch_shapes=[
            pltpu.VMEM((2, order_b // 2, order_b // 2), jnp.float32),
            pltpu.VMEM((2,) + full, jnp.float32),
        ],
        compiler_params=params(40),
        cost_estimate=cost(16 * order_b**3, 6 * 1024 * 1024),
    )(chunks, gradient, left, right)
    rows = update.reshape(n_dp, slab, order_b)
    rows = lax.all_to_all(rows, "dp", split_axis=0, concat_axis=0, tiled=True)
    return pl.pallas_call(
        output_kernel,
        out_shape=shape(blocks_col, slab, order_b),
        in_specs=[VMEM],
        out_specs=pl.BlockSpec(memory_space=pl.ANY),
        scratch_shapes=[pltpu.SemaphoreType.DMA((blocks_col,))],
        compiler_params=params(4),
        cost_estimate=cost(0, 512 * 1024),
    )(rows)


def solution(mesh):
    n_dp, n_owner = mesh.devices.shape
    fine = Mesh(mesh.devices.reshape(n_dp, n_owner // 2, 2), ("dp", "z", "core"))
    column = ("z", "core")
    in_specs = (P("dp", column, None, None), P("dp", column, None, None, None), P())
    out_specs = P(column, "dp", None)
    return jax.shard_map(body, mesh=fine, in_specs=in_specs, out_specs=out_specs, check_vma=False)
```

```python
import functools
import math

import jax
import jax.numpy as jnp
import numpy as np
from jax import lax
from jax.experimental import pallas as pl
from jax.experimental.pallas import tpu as pltpu
from jax.sharding import Mesh
from jax.sharding import PartitionSpec as P

decay_rate = 0.9
update_gain = 16.0
root_gain = 1.5

side_x = 4
chips = (
    ((0, 0), (0, 2), (2, 0), (1, 1), (3, 3)),
    ((1, 0), (1, 2), (3, 0), (2, 1), (0, 3)),
)
blocks_col = len(chips[0])
packed_rows = 72

long_flops = 10**11

VMEM = pl.BlockSpec(memory_space=pltpu.VMEM)
SMEM = pl.BlockSpec(memory_space=pltpu.SMEM)
HBM = pl.BlockSpec(memory_space=pltpu.HBM)


def even(v):
    return v ^ 1


def odd(v):
    return side_x - 1 - v


def order(portion, core):
    first, later = (even, odd) if core == 0 else (odd, even)
    one, two = portion, 1 - portion
    return ((one, first), (one, later), (two, first), (two, later))


def pairs(portion, step):
    out = []
    for x in range(side_x):
        for y in range(side_x):
            for p in range(2):
                axis, pairing = order(portion, p)[step]
                to = (pairing(x), y) if axis == 0 else (x, pairing(y))
                out.append((2 * (side_x * x + y) + p, 2 * (side_x * to[0] + to[1]) + p))
    return out


def padded(items, count):
    assert len(items) <= count
    return (list(items) + [0] * count)[:count]


@functools.cache
def tree_tables():
    first, second, third = [], [], []
    for d in range(side_x * side_x):
        here = (d // side_x, d % side_x)
        for p in range(2):
            one, two, three = [], [], []
            for portion in range(2):
                steps = order(portion, p)
                axis, later = steps[1]
                at = [c[axis] for c in chips[p]]
                me = here[axis]
                kept = [j for j in range(blocks_col) if at[j] in (me, later(me))]
                one += padded([j for j in range(blocks_col) if j not in kept], 3)
                one += padded(kept, 3)
                go = [i for i, j in enumerate(kept) if at[j] == later(me)]
                stay = [i for i, j in enumerate(kept) if at[j] == me]
                for place in padded(go, 2) + padded(stay, 2):
                    two.append(place)
                mine = [kept[i] for i in stay]
                axis, later = steps[3]
                near = (here[axis], later(here[axis]))
                stay = [i for i, j in enumerate(mine) if chips[p][j][axis] in near]
                go = [i for i, j in enumerate(mine) if chips[p][j][axis] not in near]
                three += padded(go, 1) + padded(stay, 1)
            first.append(one)
            second.append(two)
            third.append(three)
    return [np.array(t, np.int32) for t in (first, second, third)]


@functools.cache
def home_tables():
    item = np.zeros((2, 2 * side_x * side_x), np.int32)
    for p in range(2):
        for j, (x, y) in enumerate(chips[p]):
            d = side_x * x + y
            item[p, 2 * d : 2 * d + 2] = (2 * j, 2 * j + 1)
    return item


def params(mib):
    return pltpu.CompilerParams(vmem_limit_bytes=mib * 1024 * 1024)


def add_rounded(a, b):
    return (a.astype(jnp.float32) + b.astype(jnp.float32)).astype(jnp.bfloat16)


def my_row(table):
    width = table.shape[0] // (2 * side_x * side_x)
    base = (2 * lax.axis_index("dp") + lax.axis_index("core")) * width
    return [table[base + k] for k in range(width)]


def choose_kernel(table, source, s0, s1, kept):
    table = my_row(table)
    height = s0.shape[1]
    for h, sent in enumerate((s0, s1)):
        rows = slice(h * height, (h + 1) * height)
        for u in range(3):
            sent[u] = source[table[6 * h + u], rows, :]
            kept[h, u] = source[table[6 * h + 3 + u], rows, :]


def first_sum_kernel(table, kept, r0, r1, s0, s1, next_kept):
    table = my_row(table)
    for h, (got, sent) in enumerate(((r0, s0), (r1, s1))):
        for u in range(4):
            place = table[4 * h + u]
            total = add_rounded(kept[h, place], got[place])
            if u < 2:
                sent[u] = total
            else:
                next_kept[h, u - 2] = total


def second_sum_kernel(table, kept, r0, r1, s0, s1, next_kept):
    table = my_row(table)
    for h, (got, sent) in enumerate(((r0, s0), (r1, s1))):
        go, stay = table[2 * h], table[2 * h + 1]
        sent[...] = add_rounded(kept[h, go], got[go])
        next_kept[h] = add_rounded(kept[h, stay], got[stay])


def third_sum_kernel(kept, r0, r1, s0, s1):
    s0[...] = add_rounded(kept[0], r0[...])
    s1[...] = add_rounded(kept[1], r1[...])


def gram_kernel(a, b, r0, r1, out, left, right):
    half = a.shape[0]
    out[:half, :] = add_rounded(a[...], r0[...])
    out[half:, :] = add_rounded(b[...], r1[...])
    g = out[...]
    for gram, side in ((left, 1), (right, 0)):
        product = lax.dot_general(
            g, g, (((side,), (side,)), ((), ())), preferred_element_type=jnp.float32
        )
        gram[...] = product.astype(jnp.bfloat16)


def pick_kernel(table, source, out, sems):
    copies = [
        pltpu.make_async_copy(source.at[table[i]], out.at[i], sems.at[i])
        for i in range(out.shape[0])
    ]
    for copy in copies:
        copy.start()
    for copy in copies:
        copy.wait()


def pick(table, source, flops=0):
    return pl.pallas_call(
        pick_kernel,
        out_shape=jax.ShapeDtypeStruct(table.shape + source.shape[1:], source.dtype),
        in_specs=[SMEM, VMEM],
        out_specs=HBM,
        scratch_shapes=[pltpu.SemaphoreType.DMA(table.shape)],
        compiler_params=params(4),
        cost_estimate=cost(flops, 1024 * 1024),
    )(table, source)


def output_kernel(source, out, sems):
    core = lax.axis_index("core")
    for p in range(2):

        @pl.when(core == p)
        def _():
            copies = [
                pltpu.make_async_copy(source.at[side_x * x + y], out.at[j], sems.at[j])
                for j, (x, y) in enumerate(chips[p])
            ]
            for copy in copies:
                copy.start()
            for copy in copies:
                copy.wait()


def square_iotas(n):
    return (
        lax.broadcasted_iota(jnp.int32, (n, n), 0),
        lax.broadcasted_iota(jnp.int32, (n, n), 1),
    )


def pack_kernel(stats, out, quarters, packed, in_sems, out_sems):
    half = stats.shape[1] // 2
    i, j = square_iotas(half)
    row = lax.broadcasted_iota(jnp.int32, (8, 128), 0)
    corners = ((0, 0), (0, half), (half, half))
    slots = range(stats.shape[0])
    loads = [
        [
            pltpu.make_async_copy(
                stats.at[q, pl.ds(at, half), pl.ds(left, half)],
                quarters.at[q, k],
                in_sems.at[3 * q + k],
            )
            for k, (at, left) in enumerate(corners)
        ]
        for q in slots
    ]
    stores = [
        pltpu.make_async_copy(packed.at[q], out.at[:, q], out_sems.at[q]) for q in slots
    ]
    for q in slots:
        for load in loads[q]:
            load.start()
    for q in slots:
        for load in loads[q]:
            load.wait()
        low = quarters[q, 2]
        mixed = jnp.where(i <= j, quarters[q, 0], low).astype(jnp.bfloat16)
        side = quarters[q, 1].astype(jnp.bfloat16)
        diagonal = jnp.sum(jnp.where(i == j, low, 0.0), axis=0, keepdims=True)
        tail = jnp.where(
            row == 0, diagonal[:, :128], jnp.where(row == 1, diagonal[:, 128:], 0.0)
        ).astype(jnp.bfloat16)
        strips = (mixed[:, :128], mixed[:, 128:], side[:, :128], side[:, 128:])
        for c in range(16):
            packed[q, c, :64, :] = strips[c // 4][64 * (c % 4) : 64 * (c % 4) + 64, :]
            packed[q, c, 64:, :] = tail
        stores[q].start()
    for q in slots:
        stores[q].wait()


def product(a, b):
    return jnp.dot(
        a.astype(jnp.bfloat16), b.astype(jnp.bfloat16), preferred_element_type=jnp.float32
    )


def unpack(chunks, s, mixed, stat):
    half = mixed.shape[0]
    for c in range(16):
        strip = chunks[c, s, :64, :].astype(jnp.float32)
        rows = slice(64 * (c % 4), 64 * (c % 4) + 64)
        at = c // 4
        if at < 2:
            mixed[rows, 128 * at : 128 * at + 128] = strip
        else:
            stat[rows, half + 128 * (at - 2) : half + 128 * (at - 2) + 128] = strip
    tail = chunks[0, s, 64:, :].astype(jnp.float32)
    diagonal = jnp.concatenate([tail[0:1, :], tail[1:2, :]], axis=1)
    m = mixed[...]
    flipped = m.T
    i, j = square_iotas(half)
    stat[:half, :half] = jnp.where(i <= j, m, flipped)
    stat[half:, half:] = jnp.where(i > j, m, jnp.where(i == j, diagonal, flipped))
    stat[half:, :half] = stat[:half, half:].T


def update_kernel(chunks, gradient, left, right, out, mixed, stat):
    order_n = out.shape[0]
    sides = (0, 1)
    for s in sides:
        unpack(chunks, s, mixed.at[s], stat.at[s])
    i, j = square_iotas(order_n)
    scale, quarter, square = [], [], []
    for s, gram in zip(sides, (left, right)):
        new_stat = decay_rate * stat[s] + (1.0 - decay_rate) * gram[...].astype(jnp.float32)
        rounded = new_stat.astype(jnp.bfloat16)
        new_stat = rounded.astype(jnp.float32)
        squares = jnp.sum(new_stat * new_stat, axis=0, keepdims=True)
        frob_norm = jnp.sqrt(jnp.sum(squares, axis=1, keepdims=True) + 1e-06)
        scale.append(root_gain * math.sqrt(order_n) / frob_norm)
        part = 0.25 * scale[s]
        quarter.append(part * new_stat)
        square.append((part * part) * product(rounded, rounded))
    e2 = [jnp.where(i == j, 0.5625, 0.0) - 2.5 * quarter[s] + square[s] for s in sides]
    e4 = [2.0 * e2[s] + product(e2[s], e2[s]) for s in sides]
    rest = [square[s] - 1.25 * quarter[s] for s in sides]
    roots = []
    for s in sides:
        root = jnp.where(i == j, e2[s] + 1.0, e2[s]) + product(e4[s], rest[s])
        roots.append((jnp.sqrt(jnp.sqrt(scale[s])) * root).astype(jnp.bfloat16))
    applied = jnp.dot(gradient[...], roots[1], preferred_element_type=jnp.float32)
    update = jnp.dot(
        roots[0], applied.astype(jnp.bfloat16), preferred_element_type=jnp.float32
    )
    out[...] = (update_gain * update).astype(jnp.bfloat16)


def shape(*dims):
    return jax.ShapeDtypeStruct(dims, jnp.bfloat16)


def cost(flops, moved):
    return pl.CostEstimate(flops=flops, bytes_accessed=moved, transcendentals=0)


def exchange(arrays, step):
    return [
        lax.ppermute(a, ("dp", "core"), pairs(portion, step)) for portion, a in enumerate(arrays)
    ]


def first_sent(grad, tables):
    n, order_n = grad.shape[1], grad.shape[2]
    return pl.pallas_call(
        choose_kernel,
        out_shape=[shape(3, n // 2, order_n)] * 2 + [shape(2, 3, n // 2, order_n)],
        in_specs=[SMEM, VMEM],
        out_specs=[VMEM] * 3,
        compiler_params=params(16),
        cost_estimate=cost(0, 12 * n * order_n),
    )(tables[0], grad)


def gradient_sum(kept, got, tables):
    half, order_n = kept.shape[2], kept.shape[3]
    n = 2 * half
    *sent, kept = pl.pallas_call(
        first_sum_kernel,
        out_shape=[shape(2, half, order_n)] * 2 + [shape(2, 2, half, order_n)],
        in_specs=[SMEM] + [VMEM] * 3,
        out_specs=[VMEM] * 3,
        compiler_params=params(16),
        cost_estimate=cost(long_flops, 4 * 1024 * 1024),
    )(tables[1], kept, *got)
    *sent, kept = pl.pallas_call(
        second_sum_kernel,
        out_shape=[shape(half, order_n)] * 2 + [shape(2, half, order_n)],
        in_specs=[SMEM] + [VMEM] * 3,
        out_specs=[VMEM] * 3,
        compiler_params=params(12),
        cost_estimate=cost(0, 4 * 1024 * 1024),
    )(tables[2], kept, *exchange(sent, 1))
    sent = pl.pallas_call(
        third_sum_kernel,
        out_shape=[shape(half, order_n)] * 2,
        in_specs=[VMEM] * 3,
        out_specs=[VMEM] * 2,
        compiler_params=params(8),
        cost_estimate=cost(0, 4 * 1024 * 1024),
    )(kept, *exchange(sent, 2))
    return pl.pallas_call(
        gram_kernel,
        out_shape=[shape(n, order_n)] * 3,
        in_specs=[VMEM] * 4,
        out_specs=[VMEM] * 3,
        compiler_params=params(16),
        cost_estimate=cost(long_flops // 2, 4 * 1024 * 1024),
    )(*sent, *exchange(sent, 3))


def body(grad_partial, statistics, owner_table):
    n_dp = lax.axis_size("dp")
    n_owner = lax.axis_size("z") * 2
    order_b = grad_partial.shape[3]
    slab = order_b // n_dp
    slots = statistics.shape[2]
    core = lax.axis_index("core")
    col = 2 * lax.axis_index("z") + core
    lane_item = home_tables()
    tables = [jnp.asarray(t.reshape(-1)) for t in tree_tables()]

    device = owner_table.reshape(-1)
    numbers = jnp.arange(device.shape[0], dtype=jnp.int32)
    earlier = numbers[None, :] < numbers[:, None]
    slot_of = jnp.sum(
        ((device[None, :] == device[:, None]) & earlier).astype(jnp.int32), axis=1
    )
    by_column = (device % n_owner).reshape(n_owner, 2 * blocks_col)
    place = ((device // n_owner) * slots + slot_of).reshape(n_owner, 2 * blocks_col)
    lane_from = jnp.sum(jnp.where(by_column == col, place, 0), axis=1)
    home = lax.dynamic_slice_in_dim(by_column, col, 1, axis=0)
    wanted = jnp.asarray(lane_item)[core]
    item_hot = wanted[:, None] == jnp.arange(2 * blocks_col)[None, :]
    item_from = jnp.sum(jnp.where(item_hot, home, 0), axis=1)

    packed = pl.pallas_call(
        pack_kernel,
        out_shape=shape(n_dp, slots, packed_rows, 128),
        in_specs=[HBM],
        out_specs=HBM,
        scratch_shapes=[
            pltpu.VMEM((slots, 3, order_b // 2, order_b // 2), jnp.float32),
            pltpu.VMEM((slots, n_dp, packed_rows, 128), jnp.bfloat16),
            pltpu.SemaphoreType.DMA((3 * slots,)),
            pltpu.SemaphoreType.DMA((slots,)),
        ],
        compiler_params=params(12),
        cost_estimate=cost(0, 3 * 1024 * 1024),
    )(statistics[0, 0])
    spread = lax.all_to_all(packed, "dp", split_axis=0, concat_axis=0, tiled=True)
    *sent, kept = first_sent(grad_partial[0], tables)
    spread, _ = lax.optimization_barrier((spread, sent))
    got = exchange(sent, 0)
    lanes = pick(lane_from, spread.reshape(slots * n_dp, packed_rows, 128), long_flops // 3)
    lanes = lax.all_to_all(lanes, ("z", "core"), split_axis=0, concat_axis=0, tiled=True)
    gradient, left, right = gradient_sum(kept, got, tables)
    lanes = pick(item_from, lanes).reshape(n_dp, 2, packed_rows, 128)
    chunks = lax.all_to_all(lanes, "dp", split_axis=0, concat_axis=0, tiled=True)

    full = (order_b, order_b)
    update = pl.pallas_call(
        update_kernel,
        out_shape=shape(*full),
        in_specs=[VMEM] * 4,
        out_specs=VMEM,
        scratch_shapes=[
            pltpu.VMEM((2, order_b // 2, order_b // 2), jnp.float32),
            pltpu.VMEM((2,) + full, jnp.float32),
        ],
        compiler_params=params(40),
        cost_estimate=cost(16 * order_b**3, 6 * 1024 * 1024),
    )(chunks, gradient, left, right)
    rows = update.reshape(n_dp, slab, order_b)
    rows = lax.all_to_all(rows, "dp", split_axis=0, concat_axis=0, tiled=True)
    return pl.pallas_call(
        output_kernel,
        out_shape=shape(blocks_col, slab, order_b),
        in_specs=[VMEM],
        out_specs=HBM,
        scratch_shapes=[pltpu.SemaphoreType.DMA((blocks_col,))],
        compiler_params=params(4),
        cost_estimate=cost(0, 512 * 1024),
    )(rows)


def solution(mesh):
    n_dp, n_owner = mesh.devices.shape
    fine = Mesh(mesh.devices.reshape(n_dp, n_owner // 2, 2), ("dp", "z", "core"))
    column = ("z", "core")
    in_specs = (P("dp", column, None, None), P("dp", column, None, None, None), P())
    out_specs = P(column, "dp", None)
    return jax.shard_map(body, mesh=fine, in_specs=in_specs, out_specs=out_specs, check_vma=False)
```

```python
import functools
import math

import jax
import jax.numpy as jnp
import numpy as np
from jax import lax
from jax.experimental import pallas as pl
from jax.experimental.pallas import tpu as pltpu
from jax.sharding import Mesh
from jax.sharding import PartitionSpec as P

decay_rate = 0.9
update_gain = 16.0
root_gain = 1.5

side_x = 4
chips = (
    ((0, 0), (0, 2), (2, 0), (1, 1), (3, 3)),
    ((1, 0), (1, 2), (3, 0), (2, 1), (0, 3)),
)
blocks_col = len(chips[0])
packed_rows = 72

long_flops = 10**11

most_mib = 60

VMEM = pl.BlockSpec(memory_space=pltpu.VMEM)
SMEM = pl.BlockSpec(memory_space=pltpu.SMEM)
HBM = pl.BlockSpec(memory_space=pltpu.HBM)


def even(v):
    return v ^ 1


def odd(v):
    return side_x - 1 - v


def order(portion, core):
    first, later = (even, odd) if core == 0 else (odd, even)
    one, two = portion, 1 - portion
    return ((one, first), (one, later), (two, first), (two, later))


def pairs(portion, step):
    out = []
    for x in range(side_x):
        for y in range(side_x):
            for p in range(2):
                axis, pairing = order(portion, p)[step]
                to = (pairing(x), y) if axis == 0 else (x, pairing(y))
                out.append((2 * (side_x * x + y) + p, 2 * (side_x * to[0] + to[1]) + p))
    return out


def padded(items, count):
    assert len(items) <= count
    return (list(items) + [0] * count)[:count]


@functools.cache
def tree_tables():
    first, second, third = [], [], []
    for d in range(side_x * side_x):
        here = (d // side_x, d % side_x)
        for p in range(2):
            one, two, three = [], [], []
            for portion in range(2):
                steps = order(portion, p)
                axis, later = steps[1]
                at = [c[axis] for c in chips[p]]
                me = here[axis]
                kept = [j for j in range(blocks_col) if at[j] in (me, later(me))]
                one += padded([j for j in range(blocks_col) if j not in kept], 3)
                one += padded(kept, 3)
                go = [i for i, j in enumerate(kept) if at[j] == later(me)]
                stay = [i for i, j in enumerate(kept) if at[j] == me]
                for place in padded(go, 2) + padded(stay, 2):
                    two.append(place)
                mine = [kept[i] for i in stay]
                axis, later = steps[3]
                near = (here[axis], later(here[axis]))
                stay = [i for i, j in enumerate(mine) if chips[p][j][axis] in near]
                go = [i for i, j in enumerate(mine) if chips[p][j][axis] not in near]
                three += padded(go, 1) + padded(stay, 1)
            first.append(one)
            second.append(two)
            third.append(three)
    return [np.array(t, np.int32) for t in (first, second, third)]


@functools.cache
def home_tables():
    item = np.zeros((2, 2 * side_x * side_x), np.int32)
    for p in range(2):
        for j, (x, y) in enumerate(chips[p]):
            d = side_x * x + y
            item[p, 2 * d : 2 * d + 2] = (2 * j, 2 * j + 1)
    return item


def params(mib):
    return pltpu.CompilerParams(vmem_limit_bytes=mib * 1024 * 1024)


def add_rounded(a, b):
    return (a.astype(jnp.float32) + b.astype(jnp.float32)).astype(jnp.bfloat16)


def my_row(table):
    width = table.shape[0] // (2 * side_x * side_x)
    base = (2 * lax.axis_index("dp") + lax.axis_index("core")) * width
    return [table[base + k] for k in range(width)]


def choose_kernel(table, source, s0, s1):
    table = my_row(table)
    height = s0.shape[1]
    for h, sent in enumerate((s0, s1)):
        for u in range(3):
            sent[u] = source[table[6 * h + u], h * height : (h + 1) * height, :]


def first_sum_kernel(sent_table, table, source, r0, r1, s0, s1, next_kept, kept, sems):
    sent_table, table = my_row(sent_table), my_row(table)
    height = r0.shape[1]
    loads = [
        pltpu.make_async_copy(
            source.at[sent_table[6 * h + 3 + u], pl.ds(h * height, height), :],
            kept.at[h, u],
            sems.at[3 * h + u],
        )
        for h in range(2)
        for u in range(3)
    ]
    for load in loads:
        load.start()
    for h, (got, sent) in enumerate(((r0, s0), (r1, s1))):
        for load in loads[3 * h : 3 * h + 3]:
            load.wait()
        for u in range(4):
            place = table[4 * h + u]
            total = add_rounded(kept[h, place], got[place])
            if u < 2:
                sent[u] = total
            else:
                next_kept[h, u - 2] = total


def second_sum_kernel(table, kept, r0, r1, s0, s1, next_kept):
    table = my_row(table)
    for h, (got, sent) in enumerate(((r0, s0), (r1, s1))):
        go, stay = table[2 * h], table[2 * h + 1]
        sent[...] = add_rounded(kept[h, go], got[go])
        next_kept[h] = add_rounded(kept[h, stay], got[stay])


def third_sum_kernel(kept, r0, r1, s0, s1):
    s0[...] = add_rounded(kept[0], r0[...])
    s1[...] = add_rounded(kept[1], r1[...])


def gram_kernel(a, b, r0, r1, out, left, right):
    half = a.shape[0]
    out[:half, :] = add_rounded(a[...], r0[...])
    out[half:, :] = add_rounded(b[...], r1[...])
    g = out[...]
    for gram, side in ((left, 1), (right, 0)):
        product = lax.dot_general(
            g, g, (((side,), (side,)), ((), ())), preferred_element_type=jnp.float32
        )
        gram[...] = product.astype(jnp.bfloat16)


def pick_kernel(table, source, out):
    for i in range(out.shape[0]):
        out[i] = source[table[i]]


def pick(table, source, flops=0):
    return pl.pallas_call(
        pick_kernel,
        out_shape=jax.ShapeDtypeStruct(table.shape + source.shape[1:], source.dtype),
        in_specs=[SMEM, VMEM],
        out_specs=VMEM,
        compiler_params=params(4),
        cost_estimate=cost(flops, 4 * 1024 * 1024),
    )(table, source)


def output_kernel(source, out, sems):
    core = lax.axis_index("core")
    for p in range(2):

        @pl.when(core == p)
        def _():
            copies = [
                pltpu.make_async_copy(source.at[side_x * x + y], out.at[j], sems.at[j])
                for j, (x, y) in enumerate(chips[p])
            ]
            for copy in copies:
                copy.start()
            for copy in copies:
                copy.wait()


def square_iotas(n):
    return (
        lax.broadcasted_iota(jnp.int32, (n, n), 0),
        lax.broadcasted_iota(jnp.int32, (n, n), 1),
    )


def pack_kernel(stats, out, quarters, packed, in_sems, out_sems):
    half = stats.shape[1] // 2
    i, j = square_iotas(half)
    row = lax.broadcasted_iota(jnp.int32, (8, 128), 0)
    corners = ((0, 0), (0, half), (half, half))
    slots = range(stats.shape[0])
    loads = [
        [
            pltpu.make_async_copy(
                stats.at[q, pl.ds(at, half), pl.ds(left, half)],
                quarters.at[q, k],
                in_sems.at[3 * q + k],
            )
            for k, (at, left) in enumerate(corners)
        ]
        for q in slots
    ]
    stores = [
        pltpu.make_async_copy(packed.at[q], out.at[:, q], out_sems.at[q]) for q in slots
    ]
    for q in slots:
        for load in loads[q]:
            load.start()
    for q in slots:
        for load in loads[q]:
            load.wait()
        low = quarters[q, 2]
        mixed = jnp.where(i <= j, quarters[q, 0], low).astype(jnp.bfloat16)
        side = quarters[q, 1].astype(jnp.bfloat16)
        diagonal = jnp.sum(jnp.where(i == j, low, 0.0), axis=0, keepdims=True)
        tail = jnp.where(
            row == 0, diagonal[:, :128], jnp.where(row == 1, diagonal[:, 128:], 0.0)
        ).astype(jnp.bfloat16)
        strips = (mixed[:, :128], mixed[:, 128:], side[:, :128], side[:, 128:])
        for c in range(16):
            packed[q, c, :64, :] = strips[c // 4][64 * (c % 4) : 64 * (c % 4) + 64, :]
            packed[q, c, 64:, :] = tail
        stores[q].start()
    for q in slots:
        stores[q].wait()


def product(a, b):
    return jnp.dot(
        a.astype(jnp.bfloat16), b.astype(jnp.bfloat16), preferred_element_type=jnp.float32
    )


def unpack(chunks, s, mixed, stat):
    half = mixed.shape[0]
    for c in range(16):
        strip = chunks[c, s, :64, :].astype(jnp.float32)
        rows = slice(64 * (c % 4), 64 * (c % 4) + 64)
        at = c // 4
        if at < 2:
            mixed[rows, 128 * at : 128 * at + 128] = strip
        else:
            stat[rows, half + 128 * (at - 2) : half + 128 * (at - 2) + 128] = strip
    tail = chunks[0, s, 64:, :].astype(jnp.float32)
    diagonal = jnp.concatenate([tail[0:1, :], tail[1:2, :]], axis=1)
    m = mixed[...]
    flipped = m.T
    i, j = square_iotas(half)
    stat[:half, :half] = jnp.where(i <= j, m, flipped)
    stat[half:, half:] = jnp.where(i > j, m, jnp.where(i == j, diagonal, flipped))
    stat[half:, :half] = stat[:half, half:].T


def update_kernel(chunks, gradient, left, right, out, mixed, stat):
    order_n = out.shape[0]
    sides = (0, 1)
    for s in sides:
        unpack(chunks, s, mixed.at[s], stat.at[s])
    i, j = square_iotas(order_n)
    scale, quarter, square = [], [], []
    for s, gram in zip(sides, (left, right)):
        new_stat = decay_rate * stat[s] + (1.0 - decay_rate) * gram[...].astype(jnp.float32)
        rounded = new_stat.astype(jnp.bfloat16)
        new_stat = rounded.astype(jnp.float32)
        squares = jnp.sum(new_stat * new_stat, axis=0, keepdims=True)
        frob_norm = jnp.sqrt(jnp.sum(squares, axis=1, keepdims=True) + 1e-06)
        scale.append(root_gain * math.sqrt(order_n) / frob_norm)
        part = 0.25 * scale[s]
        quarter.append(part * new_stat)
        square.append((part * part) * product(rounded, rounded))
    e2 = [jnp.where(i == j, 0.5625, 0.0) - 2.5 * quarter[s] + square[s] for s in sides]
    e4 = [2.0 * e2[s] + product(e2[s], e2[s]) for s in sides]
    rest = [square[s] - 1.25 * quarter[s] for s in sides]
    roots = []
    for s in sides:
        root = jnp.where(i == j, e2[s] + 1.0, e2[s]) + product(e4[s], rest[s])
        roots.append((jnp.sqrt(jnp.sqrt(scale[s])) * root).astype(jnp.bfloat16))
    applied = jnp.dot(gradient[...], roots[1], preferred_element_type=jnp.float32)
    update = jnp.dot(
        roots[0], applied.astype(jnp.bfloat16), preferred_element_type=jnp.float32
    )
    out[...] = (update_gain * update).astype(jnp.bfloat16)


def shape(*dims):
    return jax.ShapeDtypeStruct(dims, jnp.bfloat16)


def cost(flops, moved):
    return pl.CostEstimate(flops=flops, bytes_accessed=moved, transcendentals=0)


def exchange(arrays, step):
    return [
        lax.ppermute(a, ("dp", "core"), pairs(portion, step)) for portion, a in enumerate(arrays)
    ]


def first_sent(grad, tables):
    n, order_n = grad.shape[1], grad.shape[2]
    return pl.pallas_call(
        choose_kernel,
        out_shape=[shape(3, n // 2, order_n)] * 2,
        in_specs=[SMEM, VMEM],
        out_specs=[VMEM] * 2,
        compiler_params=params(most_mib),
        cost_estimate=cost(0, 12 * n * order_n),
    )(tables[0], grad)


def gradient_sum(grad, got, tables):
    n, order_n = grad.shape[1], grad.shape[2]
    half = n // 2
    *sent, kept = pl.pallas_call(
        first_sum_kernel,
        out_shape=[shape(2, half, order_n)] * 2 + [shape(2, 2, half, order_n)],
        in_specs=[SMEM, SMEM, HBM, VMEM, VMEM],
        out_specs=[VMEM] * 3,
        scratch_shapes=[
            pltpu.VMEM((2, 3, half, order_n), jnp.bfloat16),
            pltpu.SemaphoreType.DMA((6,)),
        ],
        compiler_params=params(16),
        cost_estimate=cost(long_flops, 4 * 1024 * 1024),
    )(tables[0], tables[1], grad, *got)
    *sent, kept = pl.pallas_call(
        second_sum_kernel,
        out_shape=[shape(half, order_n)] * 2 + [shape(2, half, order_n)],
        in_specs=[SMEM] + [VMEM] * 3,
        out_specs=[VMEM] * 3,
        compiler_params=params(12),
        cost_estimate=cost(0, 4 * 1024 * 1024),
    )(tables[2], kept, *exchange(sent, 1))
    sent = pl.pallas_call(
        third_sum_kernel,
        out_shape=[shape(half, order_n)] * 2,
        in_specs=[VMEM] * 3,
        out_specs=[VMEM] * 2,
        compiler_params=params(8),
        cost_estimate=cost(0, 4 * 1024 * 1024),
    )(kept, *exchange(sent, 2))
    return pl.pallas_call(
        gram_kernel,
        out_shape=[shape(n, order_n)] * 3,
        in_specs=[VMEM] * 4,
        out_specs=[VMEM] * 3,
        compiler_params=params(16),
        cost_estimate=cost(long_flops // 2, 4 * 1024 * 1024),
    )(*sent, *exchange(sent, 3))


def body(grad_partial, statistics, owner_table):
    n_dp = lax.axis_size("dp")
    n_owner = lax.axis_size("z") * 2
    order_b = grad_partial.shape[3]
    slab = order_b // n_dp
    slots = statistics.shape[2]
    core = lax.axis_index("core")
    col = 2 * lax.axis_index("z") + core
    lane_item = home_tables()
    tables = [jnp.asarray(t.reshape(-1)) for t in tree_tables()]

    device = owner_table.reshape(-1)
    numbers = jnp.arange(device.shape[0], dtype=jnp.int32)
    earlier = numbers[None, :] < numbers[:, None]
    slot_of = jnp.sum(
        ((device[None, :] == device[:, None]) & earlier).astype(jnp.int32), axis=1
    )
    by_column = (device % n_owner).reshape(n_owner, 2 * blocks_col)
    place = ((device // n_owner) * slots + slot_of).reshape(n_owner, 2 * blocks_col)
    lane_from = jnp.sum(jnp.where(by_column == col, place, 0), axis=1)
    home = lax.dynamic_slice_in_dim(by_column, col, 1, axis=0)
    wanted = jnp.asarray(lane_item)[core]
    item_hot = wanted[:, None] == jnp.arange(2 * blocks_col)[None, :]
    item_from = jnp.sum(jnp.where(item_hot, home, 0), axis=1)

    packed = pl.pallas_call(
        pack_kernel,
        out_shape=shape(n_dp, slots, packed_rows, 128),
        in_specs=[HBM],
        out_specs=HBM,
        scratch_shapes=[
            pltpu.VMEM((slots, 3, order_b // 2, order_b // 2), jnp.float32),
            pltpu.VMEM((slots, n_dp, packed_rows, 128), jnp.bfloat16),
            pltpu.SemaphoreType.DMA((3 * slots,)),
            pltpu.SemaphoreType.DMA((slots,)),
        ],
        compiler_params=params(most_mib),
        cost_estimate=cost(0, 3 * 1024 * 1024),
    )(statistics[0, 0])
    spread = lax.all_to_all(packed, "dp", split_axis=0, concat_axis=0, tiled=True)
    sent = first_sent(grad_partial[0], tables)
    spread, _ = lax.optimization_barrier((spread, sent))
    got = exchange(sent, 0)
    lanes = pick(lane_from, spread.reshape(slots * n_dp, packed_rows, 128), long_flops // 3)
    lanes = lax.all_to_all(lanes, ("z", "core"), split_axis=0, concat_axis=0, tiled=True)
    gradient, left, right = gradient_sum(grad_partial[0], got, tables)
    lanes = pick(item_from, lanes).reshape(n_dp, 2, packed_rows, 128)
    chunks = lax.all_to_all(lanes, "dp", split_axis=0, concat_axis=0, tiled=True)

    full = (order_b, order_b)
    update = pl.pallas_call(
        update_kernel,
        out_shape=shape(*full),
        in_specs=[VMEM] * 4,
        out_specs=VMEM,
        scratch_shapes=[
            pltpu.VMEM((2, order_b // 2, order_b // 2), jnp.float32),
            pltpu.VMEM((2,) + full, jnp.float32),
        ],
        compiler_params=params(40),
        cost_estimate=cost(16 * order_b**3, 6 * 1024 * 1024),
    )(chunks, gradient, left, right)
    rows = update.reshape(n_dp, slab, order_b)
    rows = lax.all_to_all(rows, "dp", split_axis=0, concat_axis=0, tiled=True)
    return pl.pallas_call(
        output_kernel,
        out_shape=shape(blocks_col, slab, order_b),
        in_specs=[VMEM],
        out_specs=HBM,
        scratch_shapes=[pltpu.SemaphoreType.DMA((blocks_col,))],
        compiler_params=params(4),
        cost_estimate=cost(0, 512 * 1024),
    )(rows)


def solution(mesh):
    n_dp, n_owner = mesh.devices.shape
    fine = Mesh(mesh.devices.reshape(n_dp, n_owner // 2, 2), ("dp", "z", "core"))
    column = ("z", "core")
    in_specs = (P("dp", column, None, None), P("dp", column, None, None, None), P())
    out_specs = P(column, "dp", None)
    return jax.shard_map(body, mesh=fine, in_specs=in_specs, out_specs=out_specs, check_vma=False)
```

```python
import functools
import math

import jax
import jax.numpy as jnp
import numpy as np
from jax import lax
from jax.experimental import pallas as pl
from jax.experimental.pallas import tpu as pltpu
from jax.sharding import Mesh
from jax.sharding import PartitionSpec as P

decay_rate = 0.9
update_gain = 16.0
root_gain = 1.5

side_x = 4
chips = (
    ((0, 0), (0, 2), (2, 0), (1, 1), (3, 3)),
    ((1, 0), (1, 2), (3, 0), (2, 1), (0, 3)),
)
blocks_col = len(chips[0])
packed_rows = 72

long_flops = 10**11

most_mib = 60

VMEM = pl.BlockSpec(memory_space=pltpu.VMEM)
SMEM = pl.BlockSpec(memory_space=pltpu.SMEM)
HBM = pl.BlockSpec(memory_space=pltpu.HBM)


def even(v):
    return v ^ 1


def odd(v):
    return side_x - 1 - v


def order(portion, core):
    first, later = (even, odd) if core == portion else (odd, even)
    one, two = portion, 1 - portion
    return ((one, first), (one, later), (two, first), (two, later))


def pairs(portion, step):
    out = []
    for x in range(side_x):
        for y in range(side_x):
            for p in range(2):
                axis, pairing = order(portion, p)[step]
                to = (pairing(x), y) if axis == 0 else (x, pairing(y))
                out.append((2 * (side_x * x + y) + p, 2 * (side_x * to[0] + to[1]) + p))
    return out


def padded(items, count):
    assert len(items) <= count
    return (list(items) + [0] * count)[:count]


@functools.cache
def tree_tables():
    first, second, third = [], [], []
    for d in range(side_x * side_x):
        here = (d // side_x, d % side_x)
        for p in range(2):
            one, two, three = [], [], []
            for portion in range(2):
                steps = order(portion, p)
                axis, later = steps[1]
                at = [c[axis] for c in chips[p]]
                me = here[axis]
                kept = [j for j in range(blocks_col) if at[j] in (me, later(me))]
                one += padded([j for j in range(blocks_col) if j not in kept], 3)
                one += padded(kept, 3)
                go = [i for i, j in enumerate(kept) if at[j] == later(me)]
                stay = [i for i, j in enumerate(kept) if at[j] == me]
                for place in padded(go, 2) + padded(stay, 2):
                    two.append(place)
                mine = [kept[i] for i in stay]
                axis, later = steps[3]
                near = (here[axis], later(here[axis]))
                stay = [i for i, j in enumerate(mine) if chips[p][j][axis] in near]
                go = [i for i, j in enumerate(mine) if chips[p][j][axis] not in near]
                three += padded(go, 1) + padded(stay, 1)
            first.append(one)
            second.append(two)
            third.append(three)
    return [np.array(t, np.int32) for t in (first, second, third)]


@functools.cache
def home_tables():
    item = np.zeros((2, 2 * side_x * side_x), np.int32)
    for p in range(2):
        for j, (x, y) in enumerate(chips[p]):
            d = side_x * x + y
            item[p, 2 * d : 2 * d + 2] = (2 * j, 2 * j + 1)
    return item


def params(mib):
    return pltpu.CompilerParams(vmem_limit_bytes=mib * 1024 * 1024)


def add_rounded(a, b):
    return (a.astype(jnp.float32) + b.astype(jnp.float32)).astype(jnp.bfloat16)


def my_row(table):
    width = table.shape[0] // (2 * side_x * side_x)
    base = (2 * lax.axis_index("dp") + lax.axis_index("core")) * width
    return [table[base + k] for k in range(width)]


def choose_kernel(table, source, s0, s1, k0, k1):
    table = my_row(table)
    height = s0.shape[1]
    for h, (sent, kept) in enumerate(((s0, k0), (s1, k1))):
        rows = slice(h * height, (h + 1) * height)
        for u in range(3):
            sent[u] = source[table[6 * h + u], rows, :]
            kept[u] = source[table[6 * h + 3 + u], rows, :]


def first_sum_kernel(portion, table, kept, got, sent, next_kept):
    table = my_row(table)
    for u in range(4):
        place = table[4 * portion + u]
        total = add_rounded(kept[place], got[place])
        if u < 2:
            sent[u] = total
        else:
            next_kept[u - 2] = total


def second_sum_kernel(portion, table, kept, got, sent, next_kept):
    table = my_row(table)
    go, stay = table[2 * portion], table[2 * portion + 1]
    sent[...] = add_rounded(kept[go], got[go])
    next_kept[...] = add_rounded(kept[stay], got[stay])


def third_sum_kernel(kept, got, sent):
    sent[...] = add_rounded(kept[...], got[...])


def gram_kernel(a, b, r0, r1, out, left, right):
    half = a.shape[0]
    out[:half, :] = add_rounded(a[...], r0[...])
    out[half:, :] = add_rounded(b[...], r1[...])
    g = out[...]
    for gram, side in ((left, 1), (right, 0)):
        product = lax.dot_general(
            g, g, (((side,), (side,)), ((), ())), preferred_element_type=jnp.float32
        )
        gram[...] = product.astype(jnp.bfloat16)


def pick_kernel(table, source, out):
    for i in range(out.shape[0]):
        out[i] = source[table[i]]


def pick(table, source, flops=0):
    return pl.pallas_call(
        pick_kernel,
        out_shape=jax.ShapeDtypeStruct(table.shape + source.shape[1:], source.dtype),
        in_specs=[SMEM, VMEM],
        out_specs=VMEM,
        compiler_params=params(4),
        cost_estimate=cost(flops, 4 * 1024 * 1024),
    )(table, source)


def output_kernel(source, out, sems):
    core = lax.axis_index("core")
    for p in range(2):

        @pl.when(core == p)
        def _():
            copies = [
                pltpu.make_async_copy(source.at[side_x * x + y], out.at[j], sems.at[j])
                for j, (x, y) in enumerate(chips[p])
            ]
            for copy in copies:
                copy.start()
            for copy in copies:
                copy.wait()


def square_iotas(n):
    return (
        lax.broadcasted_iota(jnp.int32, (n, n), 0),
        lax.broadcasted_iota(jnp.int32, (n, n), 1),
    )


def pack_kernel(stats, out, quarters, packed, in_sems, out_sems):
    half = stats.shape[1] // 2
    i, j = square_iotas(half)
    row = lax.broadcasted_iota(jnp.int32, (8, 128), 0)
    corners = ((0, 0), (0, half), (half, half))
    slots = range(stats.shape[0])
    loads = [
        [
            pltpu.make_async_copy(
                stats.at[q, pl.ds(at, half), pl.ds(left, half)],
                quarters.at[q, k],
                in_sems.at[3 * q + k],
            )
            for k, (at, left) in enumerate(corners)
        ]
        for q in slots
    ]
    stores = [
        pltpu.make_async_copy(packed.at[q], out.at[:, q], out_sems.at[q]) for q in slots
    ]
    for q in slots:
        for load in loads[q]:
            load.start()
    for q in slots:
        for load in loads[q]:
            load.wait()
        low = quarters[q, 2]
        mixed = jnp.where(i <= j, quarters[q, 0], low).astype(jnp.bfloat16)
        side = quarters[q, 1].astype(jnp.bfloat16)
        diagonal = jnp.sum(jnp.where(i == j, low, 0.0), axis=0, keepdims=True)
        tail = jnp.where(
            row == 0, diagonal[:, :128], jnp.where(row == 1, diagonal[:, 128:], 0.0)
        ).astype(jnp.bfloat16)
        strips = (mixed[:, :128], mixed[:, 128:], side[:, :128], side[:, 128:])
        for c in range(16):
            packed[q, c, :64, :] = strips[c // 4][64 * (c % 4) : 64 * (c % 4) + 64, :]
            packed[q, c, 64:, :] = tail
        stores[q].start()
    for q in slots:
        stores[q].wait()


def product(a, b):
    return jnp.dot(
        a.astype(jnp.bfloat16), b.astype(jnp.bfloat16), preferred_element_type=jnp.float32
    )


def unpack(chunks, s, mixed, stat):
    half = mixed.shape[0]
    for c in range(16):
        strip = chunks[c, s, :64, :].astype(jnp.float32)
        rows = slice(64 * (c % 4), 64 * (c % 4) + 64)
        at = c // 4
        if at < 2:
            mixed[rows, 128 * at : 128 * at + 128] = strip
        else:
            stat[rows, half + 128 * (at - 2) : half + 128 * (at - 2) + 128] = strip
    tail = chunks[0, s, 64:, :].astype(jnp.float32)
    diagonal = jnp.concatenate([tail[0:1, :], tail[1:2, :]], axis=1)
    m = mixed[...]
    flipped = m.T
    i, j = square_iotas(half)
    stat[:half, :half] = jnp.where(i <= j, m, flipped)
    stat[half:, half:] = jnp.where(i > j, m, jnp.where(i == j, diagonal, flipped))
    stat[half:, :half] = stat[:half, half:].T


def update_kernel(chunks, gradient, left, right, out, mixed, stat):
    order_n = out.shape[0]
    sides = (0, 1)
    for s in sides:
        unpack(chunks, s, mixed.at[s], stat.at[s])
    i, j = square_iotas(order_n)
    scale, quarter, square = [], [], []
    for s, gram in zip(sides, (left, right)):
        new_stat = decay_rate * stat[s] + (1.0 - decay_rate) * gram[...].astype(jnp.float32)
        rounded = new_stat.astype(jnp.bfloat16)
        new_stat = rounded.astype(jnp.float32)
        squares = jnp.sum(new_stat * new_stat, axis=0, keepdims=True)
        frob_norm = jnp.sqrt(jnp.sum(squares, axis=1, keepdims=True) + 1e-06)
        scale.append(root_gain * math.sqrt(order_n) / frob_norm)
        part = 0.25 * scale[s]
        quarter.append(part * new_stat)
        square.append((part * part) * product(rounded, rounded))
    e2 = [jnp.where(i == j, 0.5625, 0.0) - 2.5 * quarter[s] + square[s] for s in sides]
    e4 = [2.0 * e2[s] + product(e2[s], e2[s]) for s in sides]
    rest = [square[s] - 1.25 * quarter[s] for s in sides]
    roots = []
    for s in sides:
        root = jnp.where(i == j, e2[s] + 1.0, e2[s]) + product(e4[s], rest[s])
        roots.append((jnp.sqrt(jnp.sqrt(scale[s])) * root).astype(jnp.bfloat16))
    applied = jnp.dot(gradient[...], roots[1], preferred_element_type=jnp.float32)
    update = jnp.dot(
        roots[0], applied.astype(jnp.bfloat16), preferred_element_type=jnp.float32
    )
    out[...] = (update_gain * update).astype(jnp.bfloat16)


def shape(*dims):
    return jax.ShapeDtypeStruct(dims, jnp.bfloat16)


def cost(flops, moved):
    return pl.CostEstimate(flops=flops, bytes_accessed=moved, transcendentals=0)


def exchange(array, portion, step):
    return lax.ppermute(array, ("dp", "core"), pairs(portion, step))


def first_sent(grad, tables):
    n, order_n = grad.shape[1], grad.shape[2]
    return pl.pallas_call(
        choose_kernel,
        out_shape=[shape(3, n // 2, order_n)] * 4,
        in_specs=[SMEM, VMEM],
        out_specs=[VMEM] * 4,
        compiler_params=params(most_mib),
        cost_estimate=cost(0, 12 * n * order_n),
    )(tables[0], grad)


def gradient_sum(kept, got, tables):
    half, order_n = kept[0].shape[1], kept[0].shape[2]
    n = 2 * half
    small = 1024 * 1024
    sent, kept, got = [None, None], list(kept), list(got)
    for h in range(2):
        if h == 1:
            got[1], _ = lax.optimization_barrier((got[1], sent[0]))
        sent[h], kept[h] = pl.pallas_call(
            functools.partial(first_sum_kernel, h),
            out_shape=[shape(2, half, order_n)] * 2,
            in_specs=[SMEM, VMEM, VMEM],
            out_specs=[VMEM] * 2,
            compiler_params=params(8),
            cost_estimate=cost(long_flops if h == 0 else 0, 2 * small),
        )(tables[1], kept[h], got[h])
    for h in range(2):
        sent[h], kept[h] = pl.pallas_call(
            functools.partial(second_sum_kernel, h),
            out_shape=[shape(half, order_n)] * 2,
            in_specs=[SMEM, VMEM, VMEM],
            out_specs=[VMEM] * 2,
            compiler_params=params(8),
            cost_estimate=cost(0, small),
        )(tables[2], kept[h], exchange(sent[h], h, 1))
    for h in range(2):
        sent[h] = pl.pallas_call(
            third_sum_kernel,
            out_shape=shape(half, order_n),
            in_specs=[VMEM] * 2,
            out_specs=VMEM,
            compiler_params=params(8),
            cost_estimate=cost(0, small),
        )(kept[h], exchange(sent[h], h, 2))
    got = [exchange(sent[h], h, 3) for h in range(2)]
    return pl.pallas_call(
        gram_kernel,
        out_shape=[shape(n, order_n)] * 3,
        in_specs=[VMEM] * 4,
        out_specs=[VMEM] * 3,
        compiler_params=params(16),
        cost_estimate=cost(long_flops // 2, 4 * small),
    )(*sent, *got)


def body(grad_partial, statistics, owner_table):
    n_dp = lax.axis_size("dp")
    n_owner = lax.axis_size("z") * 2
    order_b = grad_partial.shape[3]
    slab = order_b // n_dp
    slots = statistics.shape[2]
    core = lax.axis_index("core")
    col = 2 * lax.axis_index("z") + core
    lane_item = home_tables()
    tables = [jnp.asarray(t.reshape(-1)) for t in tree_tables()]

    device = owner_table.reshape(-1)
    numbers = jnp.arange(device.shape[0], dtype=jnp.int32)
    earlier = numbers[None, :] < numbers[:, None]
    slot_of = jnp.sum(
        ((device[None, :] == device[:, None]) & earlier).astype(jnp.int32), axis=1
    )
    by_column = (device % n_owner).reshape(n_owner, 2 * blocks_col)
    place = ((device // n_owner) * slots + slot_of).reshape(n_owner, 2 * blocks_col)
    lane_from = jnp.sum(jnp.where(by_column == col, place, 0), axis=1)
    home = lax.dynamic_slice_in_dim(by_column, col, 1, axis=0)
    wanted = jnp.asarray(lane_item)[core]
    item_hot = wanted[:, None] == jnp.arange(2 * blocks_col)[None, :]
    item_from = jnp.sum(jnp.where(item_hot, home, 0), axis=1)

    packed = pl.pallas_call(
        pack_kernel,
        out_shape=shape(n_dp, slots, packed_rows, 128),
        in_specs=[HBM],
        out_specs=HBM,
        scratch_shapes=[
            pltpu.VMEM((slots, 3, order_b // 2, order_b // 2), jnp.float32),
            pltpu.VMEM((slots, n_dp, packed_rows, 128), jnp.bfloat16),
            pltpu.SemaphoreType.DMA((3 * slots,)),
            pltpu.SemaphoreType.DMA((slots,)),
        ],
        compiler_params=params(most_mib),
        cost_estimate=cost(0, 3 * 1024 * 1024),
    )(statistics[0, 0])
    spread = lax.all_to_all(packed, "dp", split_axis=0, concat_axis=0, tiled=True)
    *sent, k0, k1 = first_sent(grad_partial[0], tables)
    spread, _ = lax.optimization_barrier((spread, sent))
    got = [exchange(a, portion, 0) for portion, a in enumerate(sent)]
    lanes = pick(lane_from, spread.reshape(slots * n_dp, packed_rows, 128), long_flops // 3)
    lanes = lax.all_to_all(lanes, ("z", "core"), split_axis=0, concat_axis=0, tiled=True)
    gradient, left, right = gradient_sum((k0, k1), got, tables)
    lanes = pick(item_from, lanes).reshape(n_dp, 2, packed_rows, 128)
    chunks = lax.all_to_all(lanes, "dp", split_axis=0, concat_axis=0, tiled=True)

    full = (order_b, order_b)
    update = pl.pallas_call(
        update_kernel,
        out_shape=shape(*full),
        in_specs=[VMEM] * 4,
        out_specs=VMEM,
        scratch_shapes=[
            pltpu.VMEM((2, order_b // 2, order_b // 2), jnp.float32),
            pltpu.VMEM((2,) + full, jnp.float32),
        ],
        compiler_params=params(40),
        cost_estimate=cost(16 * order_b**3, 6 * 1024 * 1024),
    )(chunks, gradient, left, right)
    rows = update.reshape(n_dp, slab, order_b)
    rows = lax.all_to_all(rows, "dp", split_axis=0, concat_axis=0, tiled=True)
    return pl.pallas_call(
        output_kernel,
        out_shape=shape(blocks_col, slab, order_b),
        in_specs=[VMEM],
        out_specs=HBM,
        scratch_shapes=[pltpu.SemaphoreType.DMA((blocks_col,))],
        compiler_params=params(4),
        cost_estimate=cost(0, 512 * 1024),
    )(rows)


def solution(mesh):
    n_dp, n_owner = mesh.devices.shape
    fine = Mesh(mesh.devices.reshape(n_dp, n_owner // 2, 2), ("dp", "z", "core"))
    column = ("z", "core")
    in_specs = (P("dp", column, None, None), P("dp", column, None, None, None), P())
    out_specs = P(column, "dp", None)
    return jax.shard_map(body, mesh=fine, in_specs=in_specs, out_specs=out_specs, check_vma=False)
```

```python
import functools
import math

import jax
import jax.numpy as jnp
import numpy as np
from jax import lax
from jax.experimental import pallas as pl
from jax.experimental.pallas import tpu as pltpu
from jax.sharding import Mesh
from jax.sharding import PartitionSpec as P

decay_rate = 0.9
update_gain = 16.0
root_gain = 1.5

side_x = 4
chips = (
    ((0, 0), (0, 2), (2, 0), (1, 1), (3, 3)),
    ((1, 0), (1, 2), (3, 0), (2, 1), (0, 3)),
)
blocks_col = len(chips[0])
packed_rows = 72

long_flops = 10**11

most_mib = 60
sum_mib = 61.5

VMEM = pl.BlockSpec(memory_space=pltpu.VMEM)
SMEM = pl.BlockSpec(memory_space=pltpu.SMEM)
HBM = pl.BlockSpec(memory_space=pltpu.HBM)


def even(v):
    return v ^ 1


def odd(v):
    return side_x - 1 - v


def order(portion, core):
    first, later = (even, odd) if core == portion else (odd, even)
    one, two = portion, 1 - portion
    return ((one, first), (one, later), (two, first), (two, later))


def pairs(portion, step):
    out = []
    for x in range(side_x):
        for y in range(side_x):
            for p in range(2):
                axis, pairing = order(portion, p)[step]
                to = (pairing(x), y) if axis == 0 else (x, pairing(y))
                out.append((2 * (side_x * x + y) + p, 2 * (side_x * to[0] + to[1]) + p))
    return out


def padded(items, count):
    assert len(items) <= count
    return (list(items) + [0] * count)[:count]


@functools.cache
def tree_tables():
    first, second, third = [], [], []
    for d in range(side_x * side_x):
        here = (d // side_x, d % side_x)
        for p in range(2):
            one, two, three = [], [], []
            for portion in range(2):
                steps = order(portion, p)
                axis, later = steps[1]
                at = [c[axis] for c in chips[p]]
                me = here[axis]
                kept = [j for j in range(blocks_col) if at[j] in (me, later(me))]
                one += padded([j for j in range(blocks_col) if j not in kept], 3)
                one += padded(kept, 3)
                go = [i for i, j in enumerate(kept) if at[j] == later(me)]
                stay = [i for i, j in enumerate(kept) if at[j] == me]
                for place in padded(go, 2) + padded(stay, 2):
                    two.append(place)
                mine = [kept[i] for i in stay]
                axis, later = steps[3]
                near = (here[axis], later(here[axis]))
                stay = [i for i, j in enumerate(mine) if chips[p][j][axis] in near]
                go = [i for i, j in enumerate(mine) if chips[p][j][axis] not in near]
                three += padded(go, 1) + padded(stay, 1)
            first.append(one)
            second.append(two)
            third.append(three)
    return [np.array(t, np.int32) for t in (first, second, third)]


@functools.cache
def home_tables():
    item = np.zeros((2, 2 * side_x * side_x), np.int32)
    for p in range(2):
        for j, (x, y) in enumerate(chips[p]):
            d = side_x * x + y
            item[p, 2 * d : 2 * d + 2] = (2 * j, 2 * j + 1)
    return item


def params(mib):
    return pltpu.CompilerParams(vmem_limit_bytes=int(mib * 1024 * 1024))


def add_rounded(a, b):
    return (a.astype(jnp.float32) + b.astype(jnp.float32)).astype(jnp.bfloat16)


def my_row(table):
    width = table.shape[0] // (2 * side_x * side_x)
    base = (2 * lax.axis_index("dp") + lax.axis_index("core")) * width
    return [table[base + k] for k in range(width)]


def choose_kernel(table, source, s0, s1):
    table = my_row(table)
    height = s0.shape[1]
    for h, sent in enumerate((s0, s1)):
        for u in range(3):
            sent[u] = source[table[6 * h + u], h * height : (h + 1) * height, :]


def first_sum_kernel(portion, units, table, source, got, sent, next_kept, kept, sems):
    units, table = my_row(units), my_row(table)
    height = got.shape[1]
    loads = [
        pltpu.make_async_copy(
            source.at[units[6 * portion + 3 + u], pl.ds(portion * height, height), :],
            kept.at[u],
            sems.at[u],
        )
        for u in range(3)
    ]
    for load in loads:
        load.start()
    for load in loads:
        load.wait()
    for u in range(4):
        place = table[4 * portion + u]
        total = add_rounded(kept[place], got[place])
        if u < 2:
            sent[u] = total
        else:
            next_kept[u - 2] = total


def second_sum_kernel(portion, table, kept, got, sent, next_kept):
    table = my_row(table)
    go, stay = table[2 * portion], table[2 * portion + 1]
    sent[...] = add_rounded(kept[go], got[go])
    next_kept[...] = add_rounded(kept[stay], got[stay])


def third_sum_kernel(kept, got, sent):
    sent[...] = add_rounded(kept[...], got[...])


def gram_kernel(a, b, r0, r1, out, left, right):
    half = a.shape[0]
    out[:half, :] = add_rounded(a[...], r0[...])
    out[half:, :] = add_rounded(b[...], r1[...])
    g = out[...]
    for gram, side in ((left, 1), (right, 0)):
        product = lax.dot_general(
            g, g, (((side,), (side,)), ((), ())), preferred_element_type=jnp.float32
        )
        gram[...] = product.astype(jnp.bfloat16)


def pick_kernel(table, source, out):
    for i in range(out.shape[0]):
        out[i] = source[table[i]]


def pick(table, source, flops=0):
    return pl.pallas_call(
        pick_kernel,
        out_shape=jax.ShapeDtypeStruct(table.shape + source.shape[1:], source.dtype),
        in_specs=[SMEM, VMEM],
        out_specs=VMEM,
        compiler_params=params(4),
        cost_estimate=cost(flops, 4 * 1024 * 1024),
    )(table, source)


def output_kernel(source, out, sems):
    core = lax.axis_index("core")
    for p in range(2):

        @pl.when(core == p)
        def _():
            copies = [
                pltpu.make_async_copy(source.at[side_x * x + y], out.at[j], sems.at[j])
                for j, (x, y) in enumerate(chips[p])
            ]
            for copy in copies:
                copy.start()
            for copy in copies:
                copy.wait()


def square_iotas(n):
    return (
        lax.broadcasted_iota(jnp.int32, (n, n), 0),
        lax.broadcasted_iota(jnp.int32, (n, n), 1),
    )


def pack_kernel(stats, out, quarters, packed, in_sems, out_sems):
    half = stats.shape[1] // 2
    i, j = square_iotas(half)
    row = lax.broadcasted_iota(jnp.int32, (8, 128), 0)
    corners = ((0, 0), (0, half), (half, half))
    slots = range(stats.shape[0])
    loads = [
        [
            pltpu.make_async_copy(
                stats.at[q, pl.ds(at, half), pl.ds(left, half)],
                quarters.at[q, k],
                in_sems.at[3 * q + k],
            )
            for k, (at, left) in enumerate(corners)
        ]
        for q in slots
    ]
    stores = [
        pltpu.make_async_copy(packed.at[q], out.at[:, q], out_sems.at[q]) for q in slots
    ]
    for q in slots:
        for load in loads[q]:
            load.start()
    for q in slots:
        for load in loads[q]:
            load.wait()
        low = quarters[q, 2]
        mixed = jnp.where(i <= j, quarters[q, 0], low).astype(jnp.bfloat16)
        side = quarters[q, 1].astype(jnp.bfloat16)
        diagonal = jnp.sum(jnp.where(i == j, low, 0.0), axis=0, keepdims=True)
        tail = jnp.where(
            row == 0, diagonal[:, :128], jnp.where(row == 1, diagonal[:, 128:], 0.0)
        ).astype(jnp.bfloat16)
        strips = (mixed[:, :128], mixed[:, 128:], side[:, :128], side[:, 128:])
        for c in range(16):
            packed[q, c, :64, :] = strips[c // 4][64 * (c % 4) : 64 * (c % 4) + 64, :]
            packed[q, c, 64:, :] = tail
        stores[q].start()
    for q in slots:
        stores[q].wait()


def product(a, b):
    return jnp.dot(
        a.astype(jnp.bfloat16), b.astype(jnp.bfloat16), preferred_element_type=jnp.float32
    )


def unpack(chunks, s, mixed, stat):
    half = mixed.shape[0]
    for c in range(16):
        strip = chunks[c, s, :64, :].astype(jnp.float32)
        rows = slice(64 * (c % 4), 64 * (c % 4) + 64)
        at = c // 4
        if at < 2:
            mixed[rows, 128 * at : 128 * at + 128] = strip
        else:
            stat[rows, half + 128 * (at - 2) : half + 128 * (at - 2) + 128] = strip
    tail = chunks[0, s, 64:, :].astype(jnp.float32)
    diagonal = jnp.concatenate([tail[0:1, :], tail[1:2, :]], axis=1)
    m = mixed[...]
    flipped = m.T
    i, j = square_iotas(half)
    stat[:half, :half] = jnp.where(i <= j, m, flipped)
    stat[half:, half:] = jnp.where(i > j, m, jnp.where(i == j, diagonal, flipped))
    stat[half:, :half] = stat[:half, half:].T


def update_kernel(chunks, gradient, left, right, out, mixed, stat):
    order_n = out.shape[0]
    sides = (0, 1)
    for s in sides:
        unpack(chunks, s, mixed.at[s], stat.at[s])
    i, j = square_iotas(order_n)
    scale, quarter, square = [], [], []
    for s, gram in zip(sides, (left, right)):
        new_stat = decay_rate * stat[s] + (1.0 - decay_rate) * gram[...].astype(jnp.float32)
        rounded = new_stat.astype(jnp.bfloat16)
        new_stat = rounded.astype(jnp.float32)
        squares = jnp.sum(new_stat * new_stat, axis=0, keepdims=True)
        frob_norm = jnp.sqrt(jnp.sum(squares, axis=1, keepdims=True) + 1e-06)
        scale.append(root_gain * math.sqrt(order_n) / frob_norm)
        part = 0.25 * scale[s]
        quarter.append(part * new_stat)
        square.append((part * part) * product(rounded, rounded))
    e2 = [jnp.where(i == j, 0.5625, 0.0) - 2.5 * quarter[s] + square[s] for s in sides]
    e4 = [2.0 * e2[s] + product(e2[s], e2[s]) for s in sides]
    rest = [square[s] - 1.25 * quarter[s] for s in sides]
    roots = []
    for s in sides:
        root = jnp.where(i == j, e2[s] + 1.0, e2[s]) + product(e4[s], rest[s])
        roots.append((jnp.sqrt(jnp.sqrt(scale[s])) * root).astype(jnp.bfloat16))
    applied = jnp.dot(gradient[...], roots[1], preferred_element_type=jnp.float32)
    update = jnp.dot(
        roots[0], applied.astype(jnp.bfloat16), preferred_element_type=jnp.float32
    )
    out[...] = (update_gain * update).astype(jnp.bfloat16)


def shape(*dims):
    return jax.ShapeDtypeStruct(dims, jnp.bfloat16)


def cost(flops, moved):
    return pl.CostEstimate(flops=flops, bytes_accessed=moved, transcendentals=0)


def exchange(array, portion, step):
    return lax.ppermute(array, ("dp", "core"), pairs(portion, step))


def first_sent(grad, tables):
    n, order_n = grad.shape[1], grad.shape[2]
    return pl.pallas_call(
        choose_kernel,
        out_shape=[shape(3, n // 2, order_n)] * 2,
        in_specs=[SMEM, VMEM],
        out_specs=[VMEM] * 2,
        compiler_params=params(most_mib),
        cost_estimate=cost(0, 12 * n * order_n),
    )(tables[0], grad)


def gradient_sum(grad, got, tables):
    n, order_n = grad.shape[1], grad.shape[2]
    half = n // 2
    small = 1024 * 1024
    sent, kept, got = [None, None], [None, None], list(got)
    for h in range(2):
        if h == 1:
            got[1], _ = lax.optimization_barrier((got[1], sent[0]))
        sent[h], kept[h] = pl.pallas_call(
            functools.partial(first_sum_kernel, h),
            out_shape=[shape(2, half, order_n)] * 2,
            in_specs=[SMEM, SMEM, HBM, VMEM],
            out_specs=[VMEM] * 2,
            scratch_shapes=[
                pltpu.VMEM((3, half, order_n), jnp.bfloat16),
                pltpu.SemaphoreType.DMA((3,)),
            ],
            compiler_params=params(sum_mib),
            cost_estimate=cost(long_flops if h == 0 else 0, 2 * small),
        )(tables[0], tables[1], grad, got[h])
    for h in range(2):
        sent[h], kept[h] = pl.pallas_call(
            functools.partial(second_sum_kernel, h),
            out_shape=[shape(half, order_n)] * 2,
            in_specs=[SMEM, VMEM, VMEM],
            out_specs=[VMEM] * 2,
            compiler_params=params(8),
            cost_estimate=cost(0, small),
        )(tables[2], kept[h], exchange(sent[h], h, 1))
    for h in range(2):
        sent[h] = pl.pallas_call(
            third_sum_kernel,
            out_shape=shape(half, order_n),
            in_specs=[VMEM] * 2,
            out_specs=VMEM,
            compiler_params=params(8),
            cost_estimate=cost(0, small),
        )(kept[h], exchange(sent[h], h, 2))
    got = [exchange(sent[h], h, 3) for h in range(2)]
    return pl.pallas_call(
        gram_kernel,
        out_shape=[shape(n, order_n)] * 3,
        in_specs=[VMEM] * 4,
        out_specs=[VMEM] * 3,
        compiler_params=params(16),
        cost_estimate=cost(long_flops // 2, 4 * small),
    )(*sent, *got)


def body(grad_partial, statistics, owner_table):
    n_dp = lax.axis_size("dp")
    n_owner = lax.axis_size("z") * 2
    order_b = grad_partial.shape[3]
    slab = order_b // n_dp
    slots = statistics.shape[2]
    core = lax.axis_index("core")
    col = 2 * lax.axis_index("z") + core
    lane_item = home_tables()
    tables = [jnp.asarray(t.reshape(-1)) for t in tree_tables()]

    device = owner_table.reshape(-1)
    numbers = jnp.arange(device.shape[0], dtype=jnp.int32)
    earlier = numbers[None, :] < numbers[:, None]
    slot_of = jnp.sum(
        ((device[None, :] == device[:, None]) & earlier).astype(jnp.int32), axis=1
    )
    by_column = (device % n_owner).reshape(n_owner, 2 * blocks_col)
    place = ((device // n_owner) * slots + slot_of).reshape(n_owner, 2 * blocks_col)
    lane_from = jnp.sum(jnp.where(by_column == col, place, 0), axis=1)
    home = lax.dynamic_slice_in_dim(by_column, col, 1, axis=0)
    wanted = jnp.asarray(lane_item)[core]
    item_hot = wanted[:, None] == jnp.arange(2 * blocks_col)[None, :]
    item_from = jnp.sum(jnp.where(item_hot, home, 0), axis=1)

    packed = pl.pallas_call(
        pack_kernel,
        out_shape=shape(n_dp, slots, packed_rows, 128),
        in_specs=[HBM],
        out_specs=HBM,
        scratch_shapes=[
            pltpu.VMEM((slots, 3, order_b // 2, order_b // 2), jnp.float32),
            pltpu.VMEM((slots, n_dp, packed_rows, 128), jnp.bfloat16),
            pltpu.SemaphoreType.DMA((3 * slots,)),
            pltpu.SemaphoreType.DMA((slots,)),
        ],
        compiler_params=params(most_mib),
        cost_estimate=cost(0, 3 * 1024 * 1024),
    )(statistics[0, 0])
    spread = lax.all_to_all(packed, "dp", split_axis=0, concat_axis=0, tiled=True)
    sent = first_sent(grad_partial[0], tables)
    spread, _ = lax.optimization_barrier((spread, sent))
    got = [exchange(a, portion, 0) for portion, a in enumerate(sent)]
    lanes = pick(lane_from, spread.reshape(slots * n_dp, packed_rows, 128), long_flops // 3)
    lanes = lax.all_to_all(lanes, ("z", "core"), split_axis=0, concat_axis=0, tiled=True)
    gradient, left, right = gradient_sum(grad_partial[0], got, tables)
    lanes = pick(item_from, lanes).reshape(n_dp, 2, packed_rows, 128)
    chunks = lax.all_to_all(lanes, "dp", split_axis=0, concat_axis=0, tiled=True)

    full = (order_b, order_b)
    update = pl.pallas_call(
        update_kernel,
        out_shape=shape(*full),
        in_specs=[VMEM] * 4,
        out_specs=VMEM,
        scratch_shapes=[
            pltpu.VMEM((2, order_b // 2, order_b // 2), jnp.float32),
            pltpu.VMEM((2,) + full, jnp.float32),
        ],
        compiler_params=params(40),
        cost_estimate=cost(16 * order_b**3, 6 * 1024 * 1024),
    )(chunks, gradient, left, right)
    rows = update.reshape(n_dp, slab, order_b)
    rows = lax.all_to_all(rows, "dp", split_axis=0, concat_axis=0, tiled=True)
    return pl.pallas_call(
        output_kernel,
        out_shape=shape(blocks_col, slab, order_b),
        in_specs=[VMEM],
        out_specs=HBM,
        scratch_shapes=[pltpu.SemaphoreType.DMA((blocks_col,))],
        compiler_params=params(4),
        cost_estimate=cost(0, 512 * 1024),
    )(rows)


def solution(mesh):
    n_dp, n_owner = mesh.devices.shape
    fine = Mesh(mesh.devices.reshape(n_dp, n_owner // 2, 2), ("dp", "z", "core"))
    column = ("z", "core")
    in_specs = (P("dp", column, None, None), P("dp", column, None, None, None), P())
    out_specs = P(column, "dp", None)
    return jax.shard_map(body, mesh=fine, in_specs=in_specs, out_specs=out_specs, check_vma=False)
```

```python
import functools
import math

import jax
import jax.numpy as jnp
import numpy as np
from jax import lax
from jax.experimental import pallas as pl
from jax.experimental.pallas import tpu as pltpu
from jax.sharding import Mesh
from jax.sharding import PartitionSpec as P

decay_rate = 0.9
update_gain = 16.0
root_gain = 1.5

side_x = 4
chips = (
    ((0, 0), (0, 2), (2, 0), (1, 1), (3, 3)),
    ((1, 0), (1, 2), (3, 0), (2, 1), (0, 3)),
)
blocks_col = len(chips[0])
packed_rows = 72

long_flops = 10**11

most_mib = 60

VMEM = pl.BlockSpec(memory_space=pltpu.VMEM)
SMEM = pl.BlockSpec(memory_space=pltpu.SMEM)
HBM = pl.BlockSpec(memory_space=pltpu.HBM)


def even(v):
    return v ^ 1


def odd(v):
    return side_x - 1 - v


def order(portion, core):
    first, later = (even, odd) if core == portion else (odd, even)
    one, two = portion, 1 - portion
    return ((one, first), (one, later), (two, first), (two, later))


def pairs(portion, step):
    out = []
    for x in range(side_x):
        for y in range(side_x):
            for p in range(2):
                axis, pairing = order(portion, p)[step]
                to = (pairing(x), y) if axis == 0 else (x, pairing(y))
                out.append((2 * (side_x * x + y) + p, 2 * (side_x * to[0] + to[1]) + p))
    return out


def padded(items, count):
    assert len(items) <= count
    return (list(items) + [0] * count)[:count]


@functools.cache
def tree_tables():
    first, second, third = [], [], []
    for d in range(side_x * side_x):
        here = (d // side_x, d % side_x)
        for p in range(2):
            one, two, three = [], [], []
            for portion in range(2):
                steps = order(portion, p)
                axis, later = steps[1]
                at = [c[axis] for c in chips[p]]
                me = here[axis]
                kept = [j for j in range(blocks_col) if at[j] in (me, later(me))]
                one += padded([j for j in range(blocks_col) if j not in kept], 3)
                one += padded(kept, 3)
                go = [i for i, j in enumerate(kept) if at[j] == later(me)]
                stay = [i for i, j in enumerate(kept) if at[j] == me]
                for place in padded(go, 2) + padded(stay, 2):
                    two.append(place)
                mine = [kept[i] for i in stay]
                axis, later = steps[3]
                near = (here[axis], later(here[axis]))
                stay = [i for i, j in enumerate(mine) if chips[p][j][axis] in near]
                go = [i for i, j in enumerate(mine) if chips[p][j][axis] not in near]
                three += padded(go, 1) + padded(stay, 1)
            first.append(one)
            second.append(two)
            third.append(three)
    return [np.array(t, np.int32) for t in (first, second, third)]


@functools.cache
def home_tables():
    item = np.zeros((2, 2 * side_x * side_x), np.int32)
    for p in range(2):
        for j, (x, y) in enumerate(chips[p]):
            d = side_x * x + y
            item[p, 2 * d : 2 * d + 2] = (2 * j, 2 * j + 1)
    return item


def params(mib):
    return pltpu.CompilerParams(vmem_limit_bytes=mib * 1024 * 1024)


def add_rounded(a, b):
    return (a.astype(jnp.float32) + b.astype(jnp.float32)).astype(jnp.bfloat16)


def my_row(table):
    width = table.shape[0] // (2 * side_x * side_x)
    base = (2 * lax.axis_index("dp") + lax.axis_index("core")) * width
    return [table[base + k] for k in range(width)]


def choose_kernel(table, source, s0, s1, k0, k1):
    table = my_row(table)
    height = s0.shape[1]
    for h, (sent, kept) in enumerate(((s0, k0), (s1, k1))):
        rows = slice(h * height, (h + 1) * height)
        for u in range(3):
            sent[u] = source[table[6 * h + u], rows, :]
            kept[u] = source[table[6 * h + 3 + u], rows, :]


def first_sum_kernel(portion, table, kept, got, sent, next_kept):
    table = my_row(table)
    for u in range(4):
        place = table[4 * portion + u]
        total = add_rounded(kept[place], got[place])
        if u < 2:
            sent[u] = total
        else:
            next_kept[u - 2] = total


def second_sum_kernel(portion, table, kept, got, sent, next_kept):
    table = my_row(table)
    go, stay = table[2 * portion], table[2 * portion + 1]
    sent[...] = add_rounded(kept[go], got[go])
    next_kept[...] = add_rounded(kept[stay], got[stay])


def third_sum_kernel(kept, got, sent):
    sent[...] = add_rounded(kept[...], got[...])


def gram_kernel(a, b, r0, r1, out, left, right):
    half = a.shape[0]
    out[:half, :] = add_rounded(a[...], r0[...])
    out[half:, :] = add_rounded(b[...], r1[...])
    g = out[...]
    for gram, side in ((left, 1), (right, 0)):
        product = lax.dot_general(
            g, g, (((side,), (side,)), ((), ())), preferred_element_type=jnp.float32
        )
        gram[...] = product.astype(jnp.bfloat16)


def pick_kernel(table, source, out, staged, sems):
    group = out.shape[0] // 4
    stores = []
    for g in range(4):
        rows = pl.ds(g * group, group)
        for i in range(g * group, (g + 1) * group):
            staged[i] = source[table[i]]
        stores.append(pltpu.make_async_copy(staged.at[rows], out.at[rows], sems.at[g]))
        stores[g].start()
    for store in stores:
        store.wait()


def pick(table, source, flops=0):
    out = table.shape + source.shape[1:]
    return pl.pallas_call(
        pick_kernel,
        out_shape=jax.ShapeDtypeStruct(out, source.dtype),
        in_specs=[SMEM, VMEM],
        out_specs=HBM,
        scratch_shapes=[pltpu.VMEM(out, source.dtype), pltpu.SemaphoreType.DMA((4,))],
        compiler_params=params(4),
        cost_estimate=cost(flops, 4 * 1024 * 1024),
    )(table, source)


def output_kernel(source, out, sems):
    core = lax.axis_index("core")
    for p in range(2):

        @pl.when(core == p)
        def _():
            copies = [
                pltpu.make_async_copy(source.at[side_x * x + y], out.at[j], sems.at[j])
                for j, (x, y) in enumerate(chips[p])
            ]
            for copy in copies:
                copy.start()
            for copy in copies:
                copy.wait()


def square_iotas(n):
    return (
        lax.broadcasted_iota(jnp.int32, (n, n), 0),
        lax.broadcasted_iota(jnp.int32, (n, n), 1),
    )


def pack_kernel(stats, out, quarters, packed, in_sems, out_sems):
    half = stats.shape[1] // 2
    i, j = square_iotas(half)
    row = lax.broadcasted_iota(jnp.int32, (8, 128), 0)
    corners = ((0, 0), (0, half), (half, half))
    slots = range(stats.shape[0])
    loads = [
        [
            pltpu.make_async_copy(
                stats.at[q, pl.ds(at, half), pl.ds(left, half)],
                quarters.at[q, k],
                in_sems.at[3 * q + k],
            )
            for k, (at, left) in enumerate(corners)
        ]
        for q in slots
    ]
    stores = [
        pltpu.make_async_copy(packed.at[q], out.at[:, q], out_sems.at[q]) for q in slots
    ]
    for q in slots:
        for load in loads[q]:
            load.start()
    for q in slots:
        for load in loads[q]:
            load.wait()
        low = quarters[q, 2]
        mixed = jnp.where(i <= j, quarters[q, 0], low).astype(jnp.bfloat16)
        side = quarters[q, 1].astype(jnp.bfloat16)
        diagonal = jnp.sum(jnp.where(i == j, low, 0.0), axis=0, keepdims=True)
        tail = jnp.where(
            row == 0, diagonal[:, :128], jnp.where(row == 1, diagonal[:, 128:], 0.0)
        ).astype(jnp.bfloat16)
        strips = (mixed[:, :128], mixed[:, 128:], side[:, :128], side[:, 128:])
        for c in range(16):
            packed[q, c, :64, :] = strips[c // 4][64 * (c % 4) : 64 * (c % 4) + 64, :]
            packed[q, c, 64:, :] = tail
        stores[q].start()
    for q in slots:
        stores[q].wait()


def product(a, b):
    return jnp.dot(
        a.astype(jnp.bfloat16), b.astype(jnp.bfloat16), preferred_element_type=jnp.float32
    )


def add_statistic(chunks, s, gram, mixed, side, stat):
    half = mixed.shape[0]
    for c in range(16):
        strip = chunks[c, s, :64, :].astype(jnp.float32)
        rows = slice(64 * (c % 4), 64 * (c % 4) + 64)
        cols = slice(128 * (c // 4 % 2), 128 * (c // 4 % 2) + 128)
        if c < 8:
            mixed[rows, cols] = strip
        else:
            side[rows, cols] = strip
    tail = chunks[0, s, 64:, :].astype(jnp.float32)
    diagonal = jnp.concatenate([tail[0:1, :], tail[1:2, :]], axis=1)
    m = mixed[...]
    flipped = m.T
    i, j = square_iotas(half)
    upper, lower = slice(0, half), slice(half, 2 * half)
    low = jnp.where(i > j, m, jnp.where(i == j, diagonal, flipped))
    total = 0.0
    for old, rows, cols in (
        (jnp.where(i <= j, m, flipped), upper, upper),
        (low, lower, lower),
        (side[...], upper, lower),
    ):
        added = decay_rate * old + (1.0 - decay_rate) * gram[rows, cols].astype(jnp.float32)
        rounded = added.astype(jnp.bfloat16)
        stat[rows, cols] = rounded
        wide = rounded.astype(jnp.float32)
        squares = jnp.sum(wide * wide, axis=0, keepdims=True)
        if rows is not cols:
            stat[cols, rows] = wide.T.astype(jnp.bfloat16)
            squares = 2.0 * squares
        total = total + squares
    return total


def update_kernel(chunks, gradient, left, right, out, mixed, side, stat):
    order_n = out.shape[0]
    sides = (0, 1)
    i, j = square_iotas(order_n)
    scale, quarter, square = [], [], []
    for s, gram in zip(sides, (left, right)):
        squares = add_statistic(chunks, s, gram, mixed.at[s], side.at[s], stat.at[s])
        frob_norm = jnp.sqrt(jnp.sum(squares, axis=1, keepdims=True) + 1e-06)
        scale.append(root_gain * math.sqrt(order_n) / frob_norm)
        part = 0.25 * scale[s]
        quarter.append(part * stat[s].astype(jnp.float32))
        square.append((part * part) * product(stat[s], stat[s]))
    e2 = [jnp.where(i == j, 0.5625, 0.0) - 2.5 * quarter[s] + square[s] for s in sides]
    e4 = [2.0 * e2[s] + product(e2[s], e2[s]) for s in sides]
    rest = [square[s] - 1.25 * quarter[s] for s in sides]
    roots = []
    for s in sides:
        root = jnp.where(i == j, e2[s] + 1.0, e2[s]) + product(e4[s], rest[s])
        roots.append((jnp.sqrt(jnp.sqrt(scale[s])) * root).astype(jnp.bfloat16))
    applied = jnp.dot(gradient[...], roots[1], preferred_element_type=jnp.float32)
    update = jnp.dot(
        roots[0], applied.astype(jnp.bfloat16), preferred_element_type=jnp.float32
    )
    out[...] = (update_gain * update).astype(jnp.bfloat16)


def shape(*dims):
    return jax.ShapeDtypeStruct(dims, jnp.bfloat16)


def cost(flops, moved):
    return pl.CostEstimate(flops=flops, bytes_accessed=moved, transcendentals=0)


def exchange(array, portion, step):
    return lax.ppermute(array, ("dp", "core"), pairs(portion, step))


def first_sent(grad, tables):
    n, order_n = grad.shape[1], grad.shape[2]
    return pl.pallas_call(
        choose_kernel,
        out_shape=[shape(3, n // 2, order_n)] * 4,
        in_specs=[SMEM, VMEM],
        out_specs=[VMEM] * 4,
        compiler_params=params(most_mib),
        cost_estimate=cost(0, 12 * n * order_n),
    )(tables[0], grad)


def gradient_sum(kept, got, tables):
    half, order_n = kept[0].shape[1], kept[0].shape[2]
    n = 2 * half
    small = 1024 * 1024
    sent, kept, got = [None, None], list(kept), list(got)
    for h in range(2):
        if h == 1:
            got[1], _ = lax.optimization_barrier((got[1], sent[0]))
        sent[h], kept[h] = pl.pallas_call(
            functools.partial(first_sum_kernel, h),
            out_shape=[shape(2, half, order_n)] * 2,
            in_specs=[SMEM, VMEM, VMEM],
            out_specs=[VMEM] * 2,
            compiler_params=params(8),
            cost_estimate=cost(long_flops if h == 0 else 0, 2 * small),
        )(tables[1], kept[h], got[h])
    for h in range(2):
        sent[h], kept[h] = pl.pallas_call(
            functools.partial(second_sum_kernel, h),
            out_shape=[shape(half, order_n)] * 2,
            in_specs=[SMEM, VMEM, VMEM],
            out_specs=[VMEM] * 2,
            compiler_params=params(8),
            cost_estimate=cost(0, small),
        )(tables[2], kept[h], exchange(sent[h], h, 1))
    for h in range(2):
        sent[h] = pl.pallas_call(
            third_sum_kernel,
            out_shape=shape(half, order_n),
            in_specs=[VMEM] * 2,
            out_specs=VMEM,
            compiler_params=params(8),
            cost_estimate=cost(0, small),
        )(kept[h], exchange(sent[h], h, 2))
    got = [exchange(sent[h], h, 3) for h in range(2)]
    return pl.pallas_call(
        gram_kernel,
        out_shape=[shape(n, order_n)] * 3,
        in_specs=[VMEM] * 4,
        out_specs=[VMEM] * 3,
        compiler_params=params(16),
        cost_estimate=cost(long_flops // 2, 4 * small),
    )(*sent, *got)


def body(grad_partial, statistics, owner_table):
    n_dp = lax.axis_size("dp")
    n_owner = lax.axis_size("z") * 2
    order_b = grad_partial.shape[3]
    slab = order_b // n_dp
    slots = statistics.shape[2]
    core = lax.axis_index("core")
    col = 2 * lax.axis_index("z") + core
    lane_item = home_tables()
    tables = [jnp.asarray(t.reshape(-1)) for t in tree_tables()]

    device = owner_table.reshape(n_owner, 2 * blocks_col)
    by_column = device % n_owner
    lane_row = jnp.max(jnp.where(by_column == col, device // n_owner, -1), axis=1)
    numbers = jnp.arange(n_owner, dtype=jnp.int32)
    same = (lane_row[None, :] == lane_row[:, None]) & (numbers[None, :] < numbers[:, None])
    lane_slot = jnp.sum(same.astype(jnp.int32), axis=1)
    lane_from = jnp.where(lane_row < 0, 0, lane_row * slots + lane_slot)
    home = lax.dynamic_slice_in_dim(by_column, col, 1, axis=0)
    wanted = jnp.asarray(lane_item)[core]
    item_hot = wanted[:, None] == jnp.arange(2 * blocks_col)[None, :]
    item_from = jnp.sum(jnp.where(item_hot, home, 0), axis=1)

    packed = pl.pallas_call(
        pack_kernel,
        out_shape=shape(n_dp, slots, packed_rows, 128),
        in_specs=[HBM],
        out_specs=HBM,
        scratch_shapes=[
            pltpu.VMEM((slots, 3, order_b // 2, order_b // 2), jnp.float32),
            pltpu.VMEM((slots, n_dp, packed_rows, 128), jnp.bfloat16),
            pltpu.SemaphoreType.DMA((3 * slots,)),
            pltpu.SemaphoreType.DMA((slots,)),
        ],
        compiler_params=params(most_mib),
        cost_estimate=cost(0, 3 * 1024 * 1024),
    )(statistics[0, 0])
    spread = lax.all_to_all(packed, "dp", split_axis=0, concat_axis=0, tiled=True)
    *sent, k0, k1 = first_sent(grad_partial[0], tables)
    spread, _ = lax.optimization_barrier((spread, sent))
    got = [exchange(a, portion, 0) for portion, a in enumerate(sent)]
    lanes = pick(lane_from, spread.reshape(slots * n_dp, packed_rows, 128), long_flops // 3)
    lanes = lax.all_to_all(lanes, ("z", "core"), split_axis=0, concat_axis=0, tiled=True)
    gradient, left, right = gradient_sum((k0, k1), got, tables)
    lanes = pick(item_from, lanes).reshape(n_dp, 2, packed_rows, 128)
    chunks = lax.all_to_all(lanes, "dp", split_axis=0, concat_axis=0, tiled=True)

    full = (order_b, order_b)
    update = pl.pallas_call(
        update_kernel,
        out_shape=shape(*full),
        in_specs=[VMEM] * 4,
        out_specs=VMEM,
        scratch_shapes=[
            pltpu.VMEM((2, order_b // 2, order_b // 2), jnp.float32),
            pltpu.VMEM((2, order_b // 2, order_b // 2), jnp.float32),
            pltpu.VMEM((2,) + full, jnp.bfloat16),
        ],
        compiler_params=params(40),
        cost_estimate=cost(16 * order_b**3, 6 * 1024 * 1024),
    )(chunks, gradient, left, right)
    rows = update.reshape(n_dp, slab, order_b)
    rows = lax.all_to_all(rows, "dp", split_axis=0, concat_axis=0, tiled=True)
    return pl.pallas_call(
        output_kernel,
        out_shape=shape(blocks_col, slab, order_b),
        in_specs=[VMEM],
        out_specs=HBM,
        scratch_shapes=[pltpu.SemaphoreType.DMA((blocks_col,))],
        compiler_params=params(4),
        cost_estimate=cost(0, 512 * 1024),
    )(rows)


def solution(mesh):
    n_dp, n_owner = mesh.devices.shape
    fine = Mesh(mesh.devices.reshape(n_dp, n_owner // 2, 2), ("dp", "z", "core"))
    column = ("z", "core")
    in_specs = (P("dp", column, None, None), P("dp", column, None, None, None), P())
    out_specs = P(column, "dp", None)
    return jax.shard_map(body, mesh=fine, in_specs=in_specs, out_specs=out_specs, check_vma=False)
```

```python
import functools
import math

import jax
import jax.numpy as jnp
import numpy as np
from jax import lax
from jax.experimental import pallas as pl
from jax.experimental.pallas import tpu as pltpu
from jax.sharding import Mesh
from jax.sharding import PartitionSpec as P

decay_rate = 0.9
update_gain = 16.0
root_gain = 1.5

side_x = 4
chips = (
    ((0, 0), (0, 2), (2, 0), (1, 1), (3, 3)),
    ((1, 0), (1, 2), (3, 0), (2, 1), (0, 3)),
)
blocks_col = len(chips[0])
packed_rows = 72

long_flops = 10**11

most_mib = 60

VMEM = pl.BlockSpec(memory_space=pltpu.VMEM)
SMEM = pl.BlockSpec(memory_space=pltpu.SMEM)
HBM = pl.BlockSpec(memory_space=pltpu.HBM)


def even(v):
    return v ^ 1


def odd(v):
    return side_x - 1 - v


def order(portion, core):
    first, later = (even, odd) if core == portion else (odd, even)
    one, two = portion, 1 - portion
    return ((one, first), (one, later), (two, first), (two, later))


def pairs(portion, step):
    out = []
    for x in range(side_x):
        for y in range(side_x):
            for p in range(2):
                axis, pairing = order(portion, p)[step]
                to = (pairing(x), y) if axis == 0 else (x, pairing(y))
                out.append((2 * (side_x * x + y) + p, 2 * (side_x * to[0] + to[1]) + p))
    return out


def padded(items, count):
    assert len(items) <= count
    return (list(items) + [0] * count)[:count]


@functools.cache
def tree_tables():
    first, second, third = [], [], []
    for d in range(side_x * side_x):
        here = (d // side_x, d % side_x)
        for p in range(2):
            one, two, three = [], [], []
            for portion in range(2):
                steps = order(portion, p)
                axis, later = steps[1]
                at = [c[axis] for c in chips[p]]
                me = here[axis]
                kept = [j for j in range(blocks_col) if at[j] in (me, later(me))]
                one += padded([j for j in range(blocks_col) if j not in kept], 3)
                one += padded(kept, 3)
                go = [i for i, j in enumerate(kept) if at[j] == later(me)]
                stay = [i for i, j in enumerate(kept) if at[j] == me]
                for place in padded(go, 2) + padded(stay, 2):
                    two.append(place)
                mine = [kept[i] for i in stay]
                axis, later = steps[3]
                near = (here[axis], later(here[axis]))
                stay = [i for i, j in enumerate(mine) if chips[p][j][axis] in near]
                go = [i for i, j in enumerate(mine) if chips[p][j][axis] not in near]
                three += padded(go, 1) + padded(stay, 1)
            first.append(one)
            second.append(two)
            third.append(three)
    return [np.array(t, np.int32) for t in (first, second, third)]


@functools.cache
def home_tables():
    item = np.zeros((2, 2 * side_x * side_x), np.int32)
    for p in range(2):
        for j, (x, y) in enumerate(chips[p]):
            d = side_x * x + y
            item[p, 2 * d : 2 * d + 2] = (2 * j, 2 * j + 1)
    return item


def params(mib):
    return pltpu.CompilerParams(vmem_limit_bytes=mib * 1024 * 1024)


def add_rounded(a, b):
    return (a.astype(jnp.float32) + b.astype(jnp.float32)).astype(jnp.bfloat16)


def my_row(table):
    width = table.shape[0] // (2 * side_x * side_x)
    base = (2 * lax.axis_index("dp") + lax.axis_index("core")) * width
    return [table[base + k] for k in range(width)]


def choose_kernel(table, source, s0, s1, k0, k1):
    table = my_row(table)
    height = s0.shape[1]
    for h, (sent, kept) in enumerate(((s0, k0), (s1, k1))):
        rows = slice(h * height, (h + 1) * height)
        for u in range(3):
            sent[u] = source[table[6 * h + u], rows, :]
            kept[u] = source[table[6 * h + 3 + u], rows, :]


def first_sum_kernel(portion, table, kept, got, sent, next_kept):
    table = my_row(table)
    for u in range(4):
        place = table[4 * portion + u]
        total = add_rounded(kept[place], got[place])
        if u < 2:
            sent[u] = total
        else:
            next_kept[u - 2] = total


def second_sum_kernel(portion, table, kept, got, sent, next_kept):
    table = my_row(table)
    go, stay = table[2 * portion], table[2 * portion + 1]
    sent[...] = add_rounded(kept[go], got[go])
    next_kept[...] = add_rounded(kept[stay], got[stay])


def third_sum_kernel(kept, got, sent):
    sent[...] = add_rounded(kept[...], got[...])


def gram_kernel(a, b, r0, r1, out, left, right):
    half = a.shape[0]
    out[:half, :] = add_rounded(a[...], r0[...])
    out[half:, :] = add_rounded(b[...], r1[...])
    g = out[...]
    for gram, side in ((left, 1), (right, 0)):
        product = lax.dot_general(
            g, g, (((side,), (side,)), ((), ())), preferred_element_type=jnp.float32
        )
        gram[...] = product.astype(jnp.bfloat16)


def pick_kernel(table, source, out, staged, sems):
    group = out.shape[0] // 4
    stores = []
    for g in range(4):
        rows = pl.ds(g * group, group)
        for i in range(g * group, (g + 1) * group):
            staged[i] = source[table[i]]
        stores.append(pltpu.make_async_copy(staged.at[rows], out.at[rows], sems.at[g]))
        stores[g].start()
    for store in stores:
        store.wait()


def pick(table, source, flops=0):
    out = table.shape + source.shape[1:]
    return pl.pallas_call(
        pick_kernel,
        out_shape=jax.ShapeDtypeStruct(out, source.dtype),
        in_specs=[SMEM, VMEM],
        out_specs=HBM,
        scratch_shapes=[pltpu.VMEM(out, source.dtype), pltpu.SemaphoreType.DMA((4,))],
        compiler_params=params(4),
        cost_estimate=cost(flops, 4 * 1024 * 1024),
    )(table, source)


def output_kernel(source, out, sems):
    core = lax.axis_index("core")
    for p in range(2):

        @pl.when(core == p)
        def _():
            copies = [
                pltpu.make_async_copy(source.at[side_x * x + y], out.at[j], sems.at[j])
                for j, (x, y) in enumerate(chips[p])
            ]
            for copy in copies:
                copy.start()
            for copy in copies:
                copy.wait()


def square_iotas(n):
    return (
        lax.broadcasted_iota(jnp.int32, (n, n), 0),
        lax.broadcasted_iota(jnp.int32, (n, n), 1),
    )


def pack_kernel(stats, out, quarters, packed, in_sems, out_sems):
    half = stats.shape[1] // 2
    i, j = square_iotas(half)
    row = lax.broadcasted_iota(jnp.int32, (8, 128), 0)
    corners = ((0, 0), (0, half), (half, half))
    slots = range(stats.shape[0])
    loads = [
        [
            pltpu.make_async_copy(
                stats.at[q, pl.ds(at, half), pl.ds(left, half)],
                quarters.at[q, k],
                in_sems.at[3 * q + k],
            )
            for k, (at, left) in enumerate(corners)
        ]
        for q in slots
    ]
    stores = [
        pltpu.make_async_copy(packed.at[q], out.at[:, q], out_sems.at[q]) for q in slots
    ]
    for q in slots:
        for load in loads[q]:
            load.start()
    for q in slots:
        for load in loads[q]:
            load.wait()
        low = quarters[q, 2]
        mixed = jnp.where(i <= j, quarters[q, 0], low).astype(jnp.bfloat16)
        side = quarters[q, 1].astype(jnp.bfloat16)
        diagonal = jnp.sum(jnp.where(i == j, low, 0.0), axis=0, keepdims=True)
        tail = jnp.where(
            row == 0, diagonal[:, :128], jnp.where(row == 1, diagonal[:, 128:], 0.0)
        ).astype(jnp.bfloat16)
        strips = (mixed[:, :128], mixed[:, 128:], side[:, :128], side[:, 128:])
        for c in range(16):
            packed[q, c, :64, :] = strips[c // 4][64 * (c % 4) : 64 * (c % 4) + 64, :]
            packed[q, c, 64:, :] = tail
        stores[q].start()
    for q in slots:
        stores[q].wait()


def product(a, b):
    return jnp.dot(
        a.astype(jnp.bfloat16), b.astype(jnp.bfloat16), preferred_element_type=jnp.float32
    )


def add_statistic(chunks, s, gram, mixed, side, stat):
    half = mixed.shape[0]
    for c in range(16):
        strip = chunks[c, s, :64, :].astype(jnp.float32)
        rows = slice(64 * (c % 4), 64 * (c % 4) + 64)
        cols = slice(128 * (c // 4 % 2), 128 * (c // 4 % 2) + 128)
        if c < 8:
            mixed[rows, cols] = strip
        else:
            side[rows, cols] = strip
    tail = chunks[0, s, 64:, :].astype(jnp.float32)
    diagonal = jnp.concatenate([tail[0:1, :], tail[1:2, :]], axis=1)
    m = mixed[...]
    flipped = m.T
    i, j = square_iotas(half)
    upper, lower = slice(0, half), slice(half, 2 * half)
    low = jnp.where(i > j, m, jnp.where(i == j, diagonal, flipped))
    total = 0.0
    for old, rows, cols in (
        (jnp.where(i <= j, m, flipped), upper, upper),
        (low, lower, lower),
        (side[...], upper, lower),
    ):
        added = decay_rate * old + (1.0 - decay_rate) * gram[rows, cols].astype(jnp.float32)
        rounded = added.astype(jnp.bfloat16)
        stat[rows, cols] = rounded
        wide = rounded.astype(jnp.float32)
        squares = jnp.sum(wide * wide, axis=0, keepdims=True)
        if rows is not cols:
            stat[cols, rows] = wide.T.astype(jnp.bfloat16)
            squares = 2.0 * squares
        total = total + squares
    return total


def update_kernel(chunks, gradient, left, right, out, mixed, side, stat):
    order_n = out.shape[0]
    sides = (0, 1)
    i, j = square_iotas(order_n)
    scale, quarter, square = [], [], []
    for s, gram in zip(sides, (left, right)):
        squares = add_statistic(chunks, s, gram, mixed.at[s], side.at[s], stat.at[s])
        frob_norm = jnp.sqrt(jnp.sum(squares, axis=1, keepdims=True) + 1e-06)
        scale.append(root_gain * math.sqrt(order_n) / frob_norm)
        part = 0.25 * scale[s]
        quarter.append(part * stat[s].astype(jnp.float32))
        square.append((part * part) * product(stat[s], stat[s]))
    e2 = [jnp.where(i == j, 0.5625, 0.0) - 2.5 * quarter[s] + square[s] for s in sides]
    e4 = [2.0 * e2[s] + product(e2[s], e2[s]) for s in sides]
    rest = [square[s] - 1.25 * quarter[s] for s in sides]
    roots = []
    for s in sides:
        root = jnp.where(i == j, e2[s] + 1.0, e2[s]) + product(e4[s], rest[s])
        roots.append((jnp.sqrt(jnp.sqrt(scale[s])) * root).astype(jnp.bfloat16))
    applied = jnp.dot(gradient[...], roots[1], preferred_element_type=jnp.float32)
    update = jnp.dot(
        roots[0], applied.astype(jnp.bfloat16), preferred_element_type=jnp.float32
    )
    out[...] = (update_gain * update).astype(jnp.bfloat16)


def shape(*dims):
    return jax.ShapeDtypeStruct(dims, jnp.bfloat16)


def cost(flops, moved):
    return pl.CostEstimate(flops=flops, bytes_accessed=moved, transcendentals=0)


def exchange(array, portion, step):
    return lax.ppermute(array, ("dp", "core"), pairs(portion, step))


def first_sent(grad, tables):
    n, order_n = grad.shape[1], grad.shape[2]
    return pl.pallas_call(
        choose_kernel,
        out_shape=[shape(3, n // 2, order_n)] * 4,
        in_specs=[SMEM, VMEM],
        out_specs=[VMEM] * 4,
        compiler_params=params(most_mib),
        cost_estimate=cost(0, 12 * n * order_n),
    )(tables[0], grad)


def gradient_sum(kept, got, tables):
    half, order_n = kept[0].shape[1], kept[0].shape[2]
    n = 2 * half
    small = 1024 * 1024
    sent, kept, got = [None, None], list(kept), list(got)
    for h in range(2):
        if h == 1:
            got[1], _ = lax.optimization_barrier((got[1], sent[0]))
        sent[h], kept[h] = pl.pallas_call(
            functools.partial(first_sum_kernel, h),
            out_shape=[shape(2, half, order_n)] * 2,
            in_specs=[SMEM, VMEM, VMEM],
            out_specs=[VMEM] * 2,
            compiler_params=params(8),
            cost_estimate=cost(long_flops if h == 0 else 0, 2 * small),
        )(tables[1], kept[h], got[h])
    for h in range(2):
        sent[h], kept[h] = pl.pallas_call(
            functools.partial(second_sum_kernel, h),
            out_shape=[shape(half, order_n)] * 2,
            in_specs=[SMEM, VMEM, VMEM],
            out_specs=[VMEM] * 2,
            compiler_params=params(8),
            cost_estimate=cost(0, small),
        )(tables[2], kept[h], exchange(sent[h], h, 1))
    for h in range(2):
        sent[h] = pl.pallas_call(
            third_sum_kernel,
            out_shape=shape(half, order_n),
            in_specs=[VMEM] * 2,
            out_specs=VMEM,
            compiler_params=params(8),
            cost_estimate=cost(0, small),
        )(kept[h], exchange(sent[h], h, 2))
    got = [exchange(sent[h], h, 3) for h in range(2)]
    return pl.pallas_call(
        gram_kernel,
        out_shape=[shape(n, order_n)] * 3,
        in_specs=[VMEM] * 4,
        out_specs=[VMEM] * 3,
        compiler_params=params(16),
        cost_estimate=cost(7 * 10**9, 4 * small),
    )(*sent, *got)


def body(grad_partial, statistics, owner_table):
    n_dp = lax.axis_size("dp")
    n_owner = lax.axis_size("z") * 2
    order_b = grad_partial.shape[3]
    slab = order_b // n_dp
    slots = statistics.shape[2]
    core = lax.axis_index("core")
    col = 2 * lax.axis_index("z") + core
    lane_item = home_tables()
    tables = [jnp.asarray(t.reshape(-1)) for t in tree_tables()]

    device = owner_table.reshape(n_owner, 2 * blocks_col)
    by_column = device % n_owner
    lane_row = jnp.max(jnp.where(by_column == col, device // n_owner, -1), axis=1)
    numbers = jnp.arange(n_owner, dtype=jnp.int32)
    same = (lane_row[None, :] == lane_row[:, None]) & (numbers[None, :] < numbers[:, None])
    lane_slot = jnp.sum(same.astype(jnp.int32), axis=1)
    lane_from = jnp.where(lane_row < 0, 0, lane_row * slots + lane_slot)
    home = lax.dynamic_slice_in_dim(by_column, col, 1, axis=0)
    wanted = jnp.asarray(lane_item)[core]
    item_hot = wanted[:, None] == jnp.arange(2 * blocks_col)[None, :]
    item_from = jnp.sum(jnp.where(item_hot, home, 0), axis=1)

    packed = pl.pallas_call(
        pack_kernel,
        out_shape=shape(n_dp, slots, packed_rows, 128),
        in_specs=[HBM],
        out_specs=HBM,
        scratch_shapes=[
            pltpu.VMEM((slots, 3, order_b // 2, order_b // 2), jnp.float32),
            pltpu.VMEM((slots, n_dp, packed_rows, 128), jnp.bfloat16),
            pltpu.SemaphoreType.DMA((3 * slots,)),
            pltpu.SemaphoreType.DMA((slots,)),
        ],
        compiler_params=params(most_mib),
        cost_estimate=cost(0, 3 * 1024 * 1024),
    )(statistics[0, 0])
    spread = lax.all_to_all(packed, "dp", split_axis=0, concat_axis=0, tiled=True)
    *sent, k0, k1 = first_sent(grad_partial[0], tables)
    spread, _ = lax.optimization_barrier((spread, sent))
    got = [exchange(a, portion, 0) for portion, a in enumerate(sent)]
    lanes = pick(lane_from, spread.reshape(slots * n_dp, packed_rows, 128), long_flops // 3)
    lanes = lax.all_to_all(lanes, ("z", "core"), split_axis=0, concat_axis=0, tiled=True)
    gradient, left, right = gradient_sum((k0, k1), got, tables)
    lanes = pick(item_from, lanes).reshape(n_dp, 2, packed_rows, 128)
    chunks = lax.all_to_all(lanes, "dp", split_axis=0, concat_axis=0, tiled=True)

    full = (order_b, order_b)
    update = pl.pallas_call(
        update_kernel,
        out_shape=shape(*full),
        in_specs=[VMEM] * 4,
        out_specs=VMEM,
        scratch_shapes=[
            pltpu.VMEM((2, order_b // 2, order_b // 2), jnp.float32),
            pltpu.VMEM((2, order_b // 2, order_b // 2), jnp.float32),
            pltpu.VMEM((2,) + full, jnp.bfloat16),
        ],
        compiler_params=params(40),
        cost_estimate=cost(16 * order_b**3, 6 * 1024 * 1024),
    )(chunks, gradient, left, right)
    rows = update.reshape(n_dp, slab, order_b)
    rows = lax.all_to_all(rows, "dp", split_axis=0, concat_axis=0, tiled=True)
    return pl.pallas_call(
        output_kernel,
        out_shape=shape(blocks_col, slab, order_b),
        in_specs=[VMEM],
        out_specs=HBM,
        scratch_shapes=[pltpu.SemaphoreType.DMA((blocks_col,))],
        compiler_params=params(4),
        cost_estimate=cost(0, 512 * 1024),
    )(rows)


def solution(mesh):
    n_dp, n_owner = mesh.devices.shape
    fine = Mesh(mesh.devices.reshape(n_dp, n_owner // 2, 2), ("dp", "z", "core"))
    column = ("z", "core")
    in_specs = (P("dp", column, None, None), P("dp", column, None, None, None), P())
    out_specs = P(column, "dp", None)
    return jax.shard_map(body, mesh=fine, in_specs=in_specs, out_specs=out_specs, check_vma=False)
```

```python
import functools
import math

import jax
import jax.numpy as jnp
import numpy as np
from jax import lax
from jax.experimental import pallas as pl
from jax.experimental.pallas import tpu as pltpu
from jax.sharding import Mesh
from jax.sharding import PartitionSpec as P

decay_rate = 0.9
update_gain = 16.0
root_gain = 1.5

side_x = 4
chips = (
    ((0, 0), (0, 2), (2, 0), (1, 1), (3, 3)),
    ((1, 0), (1, 2), (3, 0), (2, 1), (0, 3)),
)
blocks_col = len(chips[0])
packed_rows = 72

long_flops = 10**11

most_mib = 60

VMEM = pl.BlockSpec(memory_space=pltpu.VMEM)
SMEM = pl.BlockSpec(memory_space=pltpu.SMEM)
HBM = pl.BlockSpec(memory_space=pltpu.HBM)


def even(v):
    return v ^ 1


def odd(v):
    return side_x - 1 - v


def order(portion, core):
    first, later = (even, odd) if core == portion else (odd, even)
    one, two = portion, 1 - portion
    return ((one, first), (one, later), (two, first), (two, later))


def pairs(portion, step):
    out = []
    for x in range(side_x):
        for y in range(side_x):
            for p in range(2):
                axis, pairing = order(portion, p)[step]
                to = (pairing(x), y) if axis == 0 else (x, pairing(y))
                out.append((2 * (side_x * x + y) + p, 2 * (side_x * to[0] + to[1]) + p))
    return out


def padded(items, count):
    assert len(items) <= count
    return (list(items) + [0] * count)[:count]


@functools.cache
def tree_tables():
    first, second, third = [], [], []
    for d in range(side_x * side_x):
        here = (d // side_x, d % side_x)
        for p in range(2):
            one, two, three = [], [], []
            for portion in range(2):
                steps = order(portion, p)
                axis, later = steps[1]
                at = [c[axis] for c in chips[p]]
                me = here[axis]
                kept = [j for j in range(blocks_col) if at[j] in (me, later(me))]
                one += padded([j for j in range(blocks_col) if j not in kept], 3)
                one += padded(kept, 3)
                go = [i for i, j in enumerate(kept) if at[j] == later(me)]
                stay = [i for i, j in enumerate(kept) if at[j] == me]
                for place in padded(go, 2) + padded(stay, 2):
                    two.append(place)
                mine = [kept[i] for i in stay]
                axis, later = steps[3]
                near = (here[axis], later(here[axis]))
                stay = [i for i, j in enumerate(mine) if chips[p][j][axis] in near]
                go = [i for i, j in enumerate(mine) if chips[p][j][axis] not in near]
                three += padded(go, 1) + padded(stay, 1)
            first.append(one)
            second.append(two)
            third.append(three)
    return [np.array(t, np.int32) for t in (first, second, third)]


@functools.cache
def home_tables():
    item = np.zeros((2, 2 * side_x * side_x), np.int32)
    for p in range(2):
        for j, (x, y) in enumerate(chips[p]):
            d = side_x * x + y
            item[p, 2 * d : 2 * d + 2] = (2 * j, 2 * j + 1)
    return item


def params(mib):
    return pltpu.CompilerParams(vmem_limit_bytes=mib * 1024 * 1024)


def add_rounded(a, b):
    return (a.astype(jnp.float32) + b.astype(jnp.float32)).astype(jnp.bfloat16)


def my_row(table):
    width = table.shape[0] // (2 * side_x * side_x)
    base = (2 * lax.axis_index("dp") + lax.axis_index("core")) * width
    return [table[base + k] for k in range(width)]


def choose_kernel(table, source, s0, s1, k0, k1):
    table = my_row(table)
    height = s0.shape[1]
    for h, (sent, kept) in enumerate(((s0, k0), (s1, k1))):
        rows = slice(h * height, (h + 1) * height)
        for u in range(3):
            sent[u] = source[table[6 * h + u], rows, :]
            kept[u] = source[table[6 * h + 3 + u], rows, :]


def first_sum_kernel(portion, table, kept, got, sent, next_kept):
    table = my_row(table)
    for u in range(4):
        place = table[4 * portion + u]
        total = add_rounded(kept[place], got[place])
        if u < 2:
            sent[u] = total
        else:
            next_kept[u - 2] = total


def second_sum_kernel(portion, table, kept, got, sent, next_kept):
    table = my_row(table)
    go, stay = table[2 * portion], table[2 * portion + 1]
    sent[...] = add_rounded(kept[go], got[go])
    next_kept[...] = add_rounded(kept[stay], got[stay])


def third_sum_kernel(kept, got, sent):
    sent[...] = add_rounded(kept[...], got[...])


def gram_kernel(a, b, r0, r1, out, left, right):
    half = a.shape[0]
    out[:half, :] = add_rounded(a[...], r0[...])
    out[half:, :] = add_rounded(b[...], r1[...])
    g = out[...]
    for gram, side in ((left, 1), (right, 0)):
        product = lax.dot_general(
            g, g, (((side,), (side,)), ((), ())), preferred_element_type=jnp.float32
        )
        gram[...] = product.astype(jnp.bfloat16)


def pick_kernel(table, source, out, staged, sems):
    group = out.shape[0] // 4
    stores = []
    for g in range(4):
        rows = pl.ds(g * group, group)
        for i in range(g * group, (g + 1) * group):
            staged[i] = source[table[i]]
        stores.append(pltpu.make_async_copy(staged.at[rows], out.at[rows], sems.at[g]))
        stores[g].start()
    for store in stores:
        store.wait()


def pick(table, source, flops=0):
    out = table.shape + source.shape[1:]
    return pl.pallas_call(
        pick_kernel,
        out_shape=jax.ShapeDtypeStruct(out, source.dtype),
        in_specs=[SMEM, VMEM],
        out_specs=HBM,
        scratch_shapes=[pltpu.VMEM(out, source.dtype), pltpu.SemaphoreType.DMA((4,))],
        compiler_params=params(4),
        cost_estimate=cost(flops, 4 * 1024 * 1024),
    )(table, source)


def output_kernel(source, out, sems):
    core = lax.axis_index("core")
    for p in range(2):

        @pl.when(core == p)
        def _():
            copies = [
                pltpu.make_async_copy(source.at[side_x * x + y], out.at[j], sems.at[j])
                for j, (x, y) in enumerate(chips[p])
            ]
            for copy in copies:
                copy.start()
            for copy in copies:
                copy.wait()


def square_iotas(n):
    return (
        lax.broadcasted_iota(jnp.int32, (n, n), 0),
        lax.broadcasted_iota(jnp.int32, (n, n), 1),
    )


def pack_kernel(stats, out, quarters, packed, in_sems, out_sems):
    half = stats.shape[1] // 2
    i, j = square_iotas(half)
    row = lax.broadcasted_iota(jnp.int32, (8, 128), 0)
    corners = ((0, 0), (0, half), (half, half))
    slots = range(stats.shape[0])
    loads = [
        [
            pltpu.make_async_copy(
                stats.at[q, pl.ds(at, half), pl.ds(left, half)],
                quarters.at[q, k],
                in_sems.at[3 * q + k],
            )
            for k, (at, left) in enumerate(corners)
        ]
        for q in slots
    ]
    stores = [
        pltpu.make_async_copy(packed.at[q], out.at[:, q], out_sems.at[q]) for q in slots
    ]
    for q in slots:
        for load in loads[q]:
            load.start()
    for q in slots:
        for load in loads[q]:
            load.wait()
        low = quarters[q, 2]
        mixed = jnp.where(i <= j, quarters[q, 0], low).astype(jnp.bfloat16)
        side = quarters[q, 1].astype(jnp.bfloat16)
        diagonal = jnp.sum(jnp.where(i == j, low, 0.0), axis=0, keepdims=True)
        tail = jnp.where(
            row == 0, diagonal[:, :128], jnp.where(row == 1, diagonal[:, 128:], 0.0)
        ).astype(jnp.bfloat16)
        strips = (mixed[:, :128], mixed[:, 128:], side[:, :128], side[:, 128:])
        for c in range(16):
            packed[q, c, :64, :] = strips[c // 4][64 * (c % 4) : 64 * (c % 4) + 64, :]
            packed[q, c, 64:, :] = tail
        stores[q].start()
    for q in slots:
        stores[q].wait()


def product(a, b):
    return jnp.dot(
        a.astype(jnp.bfloat16), b.astype(jnp.bfloat16), preferred_element_type=jnp.float32
    )


def add_statistic(chunks, s, gram, mixed, side, stat):
    half = mixed.shape[0]
    for c in range(16):
        strip = chunks[c, s, :64, :].astype(jnp.float32)
        rows = slice(64 * (c % 4), 64 * (c % 4) + 64)
        cols = slice(128 * (c // 4 % 2), 128 * (c // 4 % 2) + 128)
        if c < 8:
            mixed[rows, cols] = strip
        else:
            side[rows, cols] = strip
    tail = chunks[0, s, 64:, :].astype(jnp.float32)
    diagonal = jnp.concatenate([tail[0:1, :], tail[1:2, :]], axis=1)
    m = mixed[...]
    flipped = m.T
    i, j = square_iotas(half)
    upper, lower = slice(0, half), slice(half, 2 * half)
    low = jnp.where(i > j, m, jnp.where(i == j, diagonal, flipped))
    total = 0.0
    for old, rows, cols in (
        (jnp.where(i <= j, m, flipped), upper, upper),
        (low, lower, lower),
        (side[...], upper, lower),
    ):
        added = decay_rate * old + (1.0 - decay_rate) * gram[rows, cols].astype(jnp.float32)
        rounded = added.astype(jnp.bfloat16)
        stat[rows, cols] = rounded
        wide = rounded.astype(jnp.float32)
        squares = jnp.sum(wide * wide, axis=0, keepdims=True)
        if rows is not cols:
            stat[cols, rows] = wide.T.astype(jnp.bfloat16)
            squares = 2.0 * squares
        total = total + squares
    return total


def update_kernel(chunks, gradient, left, right, out, mixed, side, stat):
    order_n = out.shape[0]
    sides = (0, 1)
    i, j = square_iotas(order_n)
    scale, quarter, square = [], [], []
    for s, gram in zip(sides, (left, right)):
        squares = add_statistic(chunks, s, gram, mixed.at[s], side.at[s], stat.at[s])
        frob_norm = jnp.sqrt(jnp.sum(squares, axis=1, keepdims=True) + 1e-06)
        scale.append(root_gain * math.sqrt(order_n) / frob_norm)
        part = 0.25 * scale[s]
        quarter.append(part * stat[s].astype(jnp.float32))
        square.append((part * part) * product(stat[s], stat[s]))
    e2 = [jnp.where(i == j, 0.5625, 0.0) - 2.5 * quarter[s] + square[s] for s in sides]
    e4 = [2.0 * e2[s] + product(e2[s], e2[s]) for s in sides]
    rest = [square[s] - 1.25 * quarter[s] for s in sides]
    roots = []
    for s in sides:
        root = jnp.where(i == j, e2[s] + 1.0, e2[s]) + product(e4[s], rest[s])
        roots.append((jnp.sqrt(jnp.sqrt(scale[s])) * root).astype(jnp.bfloat16))
    applied = jnp.dot(gradient[...], roots[1], preferred_element_type=jnp.float32)
    update = jnp.dot(
        roots[0], applied.astype(jnp.bfloat16), preferred_element_type=jnp.float32
    )
    out[...] = (update_gain * update).astype(jnp.bfloat16)


def shape(*dims):
    return jax.ShapeDtypeStruct(dims, jnp.bfloat16)


def cost(flops, moved):
    return pl.CostEstimate(flops=flops, bytes_accessed=moved, transcendentals=0)


def exchange(array, portion, step):
    return lax.ppermute(array, ("dp", "core"), pairs(portion, step))


def first_sent(grad, tables):
    n, order_n = grad.shape[1], grad.shape[2]
    return pl.pallas_call(
        choose_kernel,
        out_shape=[shape(3, n // 2, order_n)] * 4,
        in_specs=[SMEM, VMEM],
        out_specs=[VMEM] * 4,
        compiler_params=params(most_mib),
        cost_estimate=cost(0, 12 * n * order_n),
    )(tables[0], grad)


def gradient_sum(kept, got, tables):
    half, order_n = kept[0].shape[1], kept[0].shape[2]
    n = 2 * half
    small = 1024 * 1024
    sent, kept, got = [None, None], list(kept), list(got)
    for h in range(2):
        if h == 1:
            got[1], _ = lax.optimization_barrier((got[1], sent[0]))
        sent[h], kept[h] = pl.pallas_call(
            functools.partial(first_sum_kernel, h),
            out_shape=[shape(2, half, order_n)] * 2,
            in_specs=[SMEM, VMEM, VMEM],
            out_specs=[VMEM] * 2,
            compiler_params=params(8),
            cost_estimate=cost(long_flops if h == 0 else 0, 2 * small),
        )(tables[1], kept[h], got[h])
    for h in range(2):
        sent[h], kept[h] = pl.pallas_call(
            functools.partial(second_sum_kernel, h),
            out_shape=[shape(half, order_n)] * 2,
            in_specs=[SMEM, VMEM, VMEM],
            out_specs=[VMEM] * 2,
            compiler_params=params(8),
            cost_estimate=cost(0, small),
        )(tables[2], kept[h], exchange(sent[h], h, 1))
    for h in range(2):
        sent[h] = pl.pallas_call(
            third_sum_kernel,
            out_shape=shape(half, order_n),
            in_specs=[VMEM] * 2,
            out_specs=VMEM,
            compiler_params=params(8),
            cost_estimate=cost(0, small),
        )(kept[h], exchange(sent[h], h, 2))
    got = [exchange(sent[h], h, 3) for h in range(2)]
    return pl.pallas_call(
        gram_kernel,
        out_shape=[shape(n, order_n)] * 3,
        in_specs=[VMEM] * 4,
        out_specs=[VMEM] * 3,
        compiler_params=params(16),
        cost_estimate=cost(35 * 10**8, 4 * small),
    )(*sent, *got)


def body(grad_partial, statistics, owner_table):
    n_dp = lax.axis_size("dp")
    n_owner = lax.axis_size("z") * 2
    order_b = grad_partial.shape[3]
    slab = order_b // n_dp
    slots = statistics.shape[2]
    core = lax.axis_index("core")
    col = 2 * lax.axis_index("z") + core
    lane_item = home_tables()
    tables = [jnp.asarray(t.reshape(-1)) for t in tree_tables()]

    device = owner_table.reshape(n_owner, 2 * blocks_col)
    by_column = device % n_owner
    lane_row = jnp.max(jnp.where(by_column == col, device // n_owner, -1), axis=1)
    numbers = jnp.arange(n_owner, dtype=jnp.int32)
    same = (lane_row[None, :] == lane_row[:, None]) & (numbers[None, :] < numbers[:, None])
    lane_slot = jnp.sum(same.astype(jnp.int32), axis=1)
    lane_from = jnp.where(lane_row < 0, 0, lane_row * slots + lane_slot)
    home = lax.dynamic_slice_in_dim(by_column, col, 1, axis=0)
    wanted = jnp.asarray(lane_item)[core]
    item_hot = wanted[:, None] == jnp.arange(2 * blocks_col)[None, :]
    item_from = jnp.sum(jnp.where(item_hot, home, 0), axis=1)

    packed = pl.pallas_call(
        pack_kernel,
        out_shape=shape(n_dp, slots, packed_rows, 128),
        in_specs=[HBM],
        out_specs=HBM,
        scratch_shapes=[
            pltpu.VMEM((slots, 3, order_b // 2, order_b // 2), jnp.float32),
            pltpu.VMEM((slots, n_dp, packed_rows, 128), jnp.bfloat16),
            pltpu.SemaphoreType.DMA((3 * slots,)),
            pltpu.SemaphoreType.DMA((slots,)),
        ],
        compiler_params=params(most_mib),
        cost_estimate=cost(0, 3 * 1024 * 1024),
    )(statistics[0, 0])
    spread = lax.all_to_all(packed, "dp", split_axis=0, concat_axis=0, tiled=True)
    *sent, k0, k1 = first_sent(grad_partial[0], tables)
    spread, _ = lax.optimization_barrier((spread, sent))
    got = [exchange(a, portion, 0) for portion, a in enumerate(sent)]
    lanes = pick(lane_from, spread.reshape(slots * n_dp, packed_rows, 128), long_flops // 3)
    lanes = lax.all_to_all(lanes, ("z", "core"), split_axis=0, concat_axis=0, tiled=True)
    gradient, left, right = gradient_sum((k0, k1), got, tables)
    lanes = pick(item_from, lanes).reshape(n_dp, 2, packed_rows, 128)
    chunks = lax.all_to_all(lanes, "dp", split_axis=0, concat_axis=0, tiled=True)

    full = (order_b, order_b)
    update = pl.pallas_call(
        update_kernel,
        out_shape=shape(*full),
        in_specs=[VMEM] * 4,
        out_specs=VMEM,
        scratch_shapes=[
            pltpu.VMEM((2, order_b // 2, order_b // 2), jnp.float32),
            pltpu.VMEM((2, order_b // 2, order_b // 2), jnp.float32),
            pltpu.VMEM((2,) + full, jnp.bfloat16),
        ],
        compiler_params=params(40),
        cost_estimate=cost(16 * order_b**3, 6 * 1024 * 1024),
    )(chunks, gradient, left, right)
    rows = update.reshape(n_dp, slab, order_b)
    rows = lax.all_to_all(rows, "dp", split_axis=0, concat_axis=0, tiled=True)
    return pl.pallas_call(
        output_kernel,
        out_shape=shape(blocks_col, slab, order_b),
        in_specs=[VMEM],
        out_specs=HBM,
        scratch_shapes=[pltpu.SemaphoreType.DMA((blocks_col,))],
        compiler_params=params(4),
        cost_estimate=cost(0, 512 * 1024),
    )(rows)


def solution(mesh):
    n_dp, n_owner = mesh.devices.shape
    fine = Mesh(mesh.devices.reshape(n_dp, n_owner // 2, 2), ("dp", "z", "core"))
    column = ("z", "core")
    in_specs = (P("dp", column, None, None), P("dp", column, None, None, None), P())
    out_specs = P(column, "dp", None)
    return jax.shard_map(body, mesh=fine, in_specs=in_specs, out_specs=out_specs, check_vma=False)
```

```python
import functools
import math

import jax
import jax.numpy as jnp
import numpy as np
from jax import lax
from jax.experimental import pallas as pl
from jax.experimental.pallas import tpu as pltpu
from jax.sharding import Mesh
from jax.sharding import PartitionSpec as P

decay_rate = 0.9
update_gain = 16.0
root_gain = 1.5

side_x = 4
chips = (
    ((0, 0), (0, 2), (2, 0), (1, 1), (3, 3)),
    ((1, 0), (1, 2), (3, 0), (2, 1), (0, 3)),
)
blocks_col = len(chips[0])
packed_rows = 72

long_flops = 10**11

most_mib = 60

VMEM = pl.BlockSpec(memory_space=pltpu.VMEM)
SMEM = pl.BlockSpec(memory_space=pltpu.SMEM)
HBM = pl.BlockSpec(memory_space=pltpu.HBM)


def even(v):
    return v ^ 1


def odd(v):
    return side_x - 1 - v


def order(portion, core):
    first, later = (even, odd) if core == portion else (odd, even)
    one, two = portion, 1 - portion
    return ((one, first), (one, later), (two, first), (two, later))


def pairs(portion, step):
    out = []
    for x in range(side_x):
        for y in range(side_x):
            for p in range(2):
                axis, pairing = order(portion, p)[step]
                to = (pairing(x), y) if axis == 0 else (x, pairing(y))
                out.append((2 * (side_x * x + y) + p, 2 * (side_x * to[0] + to[1]) + p))
    return out


def padded(items, count):
    assert len(items) <= count
    return (list(items) + [0] * count)[:count]


@functools.cache
def tree_tables():
    first, second, third = [], [], []
    for d in range(side_x * side_x):
        here = (d // side_x, d % side_x)
        for p in range(2):
            one, two, three = [], [], []
            for portion in range(2):
                steps = order(portion, p)
                axis, later = steps[1]
                at = [c[axis] for c in chips[p]]
                me = here[axis]
                kept = [j for j in range(blocks_col) if at[j] in (me, later(me))]
                one += padded([j for j in range(blocks_col) if j not in kept], 3)
                one += padded(kept, 3)
                go = [i for i, j in enumerate(kept) if at[j] == later(me)]
                stay = [i for i, j in enumerate(kept) if at[j] == me]
                for place in padded(go, 2) + padded(stay, 2):
                    two.append(place)
                mine = [kept[i] for i in stay]
                axis, later = steps[3]
                near = (here[axis], later(here[axis]))
                stay = [i for i, j in enumerate(mine) if chips[p][j][axis] in near]
                go = [i for i, j in enumerate(mine) if chips[p][j][axis] not in near]
                three += padded(go, 1) + padded(stay, 1)
            first.append(one)
            second.append(two)
            third.append(three)
    return [np.array(t, np.int32) for t in (first, second, third)]


@functools.cache
def home_tables():
    item = np.zeros((2, 2 * side_x * side_x), np.int32)
    for p in range(2):
        for j, (x, y) in enumerate(chips[p]):
            d = side_x * x + y
            item[p, 2 * d : 2 * d + 2] = (2 * j, 2 * j + 1)
    return item


def params(mib):
    return pltpu.CompilerParams(vmem_limit_bytes=mib * 1024 * 1024)


def add_rounded(a, b):
    return (a.astype(jnp.float32) + b.astype(jnp.float32)).astype(jnp.bfloat16)


def my_row(table):
    width = table.shape[0] // (2 * side_x * side_x)
    base = (2 * lax.axis_index("dp") + lax.axis_index("core")) * width
    return [table[base + k] for k in range(width)]


def choose_kernel(table, source, s0, s1, k0, k1, sems):
    table = my_row(table)
    height = s0.shape[1]
    copies = []
    for half_outs, first in (((s0, s1), 0), ((k0, k1), 3)):
        for h, out in enumerate(half_outs):
            for u in range(3):
                unit = source.at[table[6 * h + first + u], pl.ds(h * height, height), :]
                copies.append(pltpu.make_async_copy(unit, out.at[u], sems.at[len(copies)]))
    for copy in copies:
        copy.start()
    for copy in copies:
        copy.wait()


def first_sum_kernel(portion, table, kept, got, sent, next_kept):
    table = my_row(table)
    for u in range(4):
        place = table[4 * portion + u]
        total = add_rounded(kept[place], got[place])
        if u < 2:
            sent[u] = total
        else:
            next_kept[u - 2] = total


def second_sum_kernel(portion, table, kept, got, sent, next_kept):
    table = my_row(table)
    go, stay = table[2 * portion], table[2 * portion + 1]
    sent[...] = add_rounded(kept[go], got[go])
    next_kept[...] = add_rounded(kept[stay], got[stay])


def third_sum_kernel(kept, got, sent):
    sent[...] = add_rounded(kept[...], got[...])


def gram_kernel(a, b, r0, r1, out, left, right):
    half = a.shape[0]
    out[:half, :] = add_rounded(a[...], r0[...])
    out[half:, :] = add_rounded(b[...], r1[...])
    g = out[...]
    for gram, side in ((left, 1), (right, 0)):
        product = lax.dot_general(
            g, g, (((side,), (side,)), ((), ())), preferred_element_type=jnp.float32
        )
        gram[...] = product.astype(jnp.bfloat16)


def pick_kernel(table, source, out, staged, sems):
    group = out.shape[0] // 4
    stores = []
    for g in range(4):
        rows = pl.ds(g * group, group)
        for i in range(g * group, (g + 1) * group):
            staged[i] = source[table[i]]
        stores.append(pltpu.make_async_copy(staged.at[rows], out.at[rows], sems.at[g]))
        stores[g].start()
    for store in stores:
        store.wait()


def pick(table, source, flops=0):
    out = table.shape + source.shape[1:]
    return pl.pallas_call(
        pick_kernel,
        out_shape=jax.ShapeDtypeStruct(out, source.dtype),
        in_specs=[SMEM, VMEM],
        out_specs=HBM,
        scratch_shapes=[pltpu.VMEM(out, source.dtype), pltpu.SemaphoreType.DMA((4,))],
        compiler_params=params(4),
        cost_estimate=cost(flops, 4 * 1024 * 1024),
    )(table, source)


def output_kernel(source, out, sems):
    core = lax.axis_index("core")
    for p in range(2):

        @pl.when(core == p)
        def _():
            copies = [
                pltpu.make_async_copy(source.at[side_x * x + y], out.at[j], sems.at[j])
                for j, (x, y) in enumerate(chips[p])
            ]
            for copy in copies:
                copy.start()
            for copy in copies:
                copy.wait()


def square_iotas(n):
    return (
        lax.broadcasted_iota(jnp.int32, (n, n), 0),
        lax.broadcasted_iota(jnp.int32, (n, n), 1),
    )


def pack_kernel(stats, out, quarters, packed, in_sems, out_sems):
    half = stats.shape[1] // 2
    i, j = square_iotas(half)
    row = lax.broadcasted_iota(jnp.int32, (8, 128), 0)
    corners = ((0, 0), (0, half), (half, half))
    slots = range(stats.shape[0])
    loads = [
        [
            pltpu.make_async_copy(
                stats.at[q, pl.ds(at, half), pl.ds(left, half)],
                quarters.at[q, k],
                in_sems.at[3 * q + k],
            )
            for k, (at, left) in enumerate(corners)
        ]
        for q in slots
    ]
    stores = [
        pltpu.make_async_copy(packed.at[q], out.at[:, q], out_sems.at[q]) for q in slots
    ]
    for q in slots:
        for load in loads[q]:
            load.start()
    for q in slots:
        for load in loads[q]:
            load.wait()
        low = quarters[q, 2]
        mixed = jnp.where(i <= j, quarters[q, 0], low).astype(jnp.bfloat16)
        side = quarters[q, 1].astype(jnp.bfloat16)
        diagonal = jnp.sum(jnp.where(i == j, low, 0.0), axis=0, keepdims=True)
        tail = jnp.where(
            row == 0, diagonal[:, :128], jnp.where(row == 1, diagonal[:, 128:], 0.0)
        ).astype(jnp.bfloat16)
        strips = (mixed[:, :128], mixed[:, 128:], side[:, :128], side[:, 128:])
        for c in range(16):
            packed[q, c, :64, :] = strips[c // 4][64 * (c % 4) : 64 * (c % 4) + 64, :]
            packed[q, c, 64:, :] = tail
        stores[q].start()
    for q in slots:
        stores[q].wait()


def product(a, b):
    return jnp.dot(
        a.astype(jnp.bfloat16), b.astype(jnp.bfloat16), preferred_element_type=jnp.float32
    )


def add_statistic(chunks, s, gram, mixed, side, stat):
    half = mixed.shape[0]
    for c in range(16):
        strip = chunks[c, s, :64, :].astype(jnp.float32)
        rows = slice(64 * (c % 4), 64 * (c % 4) + 64)
        cols = slice(128 * (c // 4 % 2), 128 * (c // 4 % 2) + 128)
        if c < 8:
            mixed[rows, cols] = strip
        else:
            side[rows, cols] = strip
    tail = chunks[0, s, 64:, :].astype(jnp.float32)
    diagonal = jnp.concatenate([tail[0:1, :], tail[1:2, :]], axis=1)
    m = mixed[...]
    flipped = m.T
    i, j = square_iotas(half)
    upper, lower = slice(0, half), slice(half, 2 * half)
    low = jnp.where(i > j, m, jnp.where(i == j, diagonal, flipped))
    total = 0.0
    for old, rows, cols in (
        (jnp.where(i <= j, m, flipped), upper, upper),
        (low, lower, lower),
        (side[...], upper, lower),
    ):
        added = decay_rate * old + (1.0 - decay_rate) * gram[rows, cols].astype(jnp.float32)
        rounded = added.astype(jnp.bfloat16)
        stat[rows, cols] = rounded
        wide = rounded.astype(jnp.float32)
        squares = jnp.sum(wide * wide, axis=0, keepdims=True)
        if rows is not cols:
            stat[cols, rows] = wide.T.astype(jnp.bfloat16)
            squares = 2.0 * squares
        total = total + squares
    return total


def update_kernel(chunks, gradient, left, right, out, mixed, side, stat):
    order_n = out.shape[0]
    sides = (0, 1)
    i, j = square_iotas(order_n)
    scale, quarter, square = [], [], []
    for s, gram in zip(sides, (left, right)):
        squares = add_statistic(chunks, s, gram, mixed.at[s], side.at[s], stat.at[s])
        frob_norm = jnp.sqrt(jnp.sum(squares, axis=1, keepdims=True) + 1e-06)
        scale.append(root_gain * math.sqrt(order_n) / frob_norm)
        part = 0.25 * scale[s]
        quarter.append(part * stat[s].astype(jnp.float32))
        square.append((part * part) * product(stat[s], stat[s]))
    e2 = [jnp.where(i == j, 0.5625, 0.0) - 2.5 * quarter[s] + square[s] for s in sides]
    e4 = [2.0 * e2[s] + product(e2[s], e2[s]) for s in sides]
    rest = [square[s] - 1.25 * quarter[s] for s in sides]
    roots = []
    for s in sides:
        root = jnp.where(i == j, e2[s] + 1.0, e2[s]) + product(e4[s], rest[s])
        roots.append((jnp.sqrt(jnp.sqrt(scale[s])) * root).astype(jnp.bfloat16))
    applied = jnp.dot(gradient[...], roots[1], preferred_element_type=jnp.float32)
    update = jnp.dot(
        roots[0], applied.astype(jnp.bfloat16), preferred_element_type=jnp.float32
    )
    out[...] = (update_gain * update).astype(jnp.bfloat16)


def shape(*dims):
    return jax.ShapeDtypeStruct(dims, jnp.bfloat16)


def cost(flops, moved):
    return pl.CostEstimate(flops=flops, bytes_accessed=moved, transcendentals=0)


def exchange(array, portion, step):
    return lax.ppermute(array, ("dp", "core"), pairs(portion, step))


def first_sent(grad, tables):
    n, order_n = grad.shape[1], grad.shape[2]
    return pl.pallas_call(
        choose_kernel,
        out_shape=[shape(3, n // 2, order_n)] * 4,
        in_specs=[SMEM, VMEM],
        out_specs=[HBM] * 4,
        scratch_shapes=[pltpu.SemaphoreType.DMA((12,))],
        compiler_params=params(most_mib),
        cost_estimate=cost(0, 12 * n * order_n),
    )(tables[0], grad)


def gradient_sum(kept, got, tables):
    half, order_n = kept[0].shape[1], kept[0].shape[2]
    n = 2 * half
    small = 1024 * 1024
    sent, kept, got = [None, None], list(kept), list(got)
    for h in range(2):
        if h == 1:
            got[1], _ = lax.optimization_barrier((got[1], sent[0]))
        sent[h], kept[h] = pl.pallas_call(
            functools.partial(first_sum_kernel, h),
            out_shape=[shape(2, half, order_n)] * 2,
            in_specs=[SMEM, VMEM, VMEM],
            out_specs=[VMEM] * 2,
            compiler_params=params(8),
            cost_estimate=cost(long_flops if h == 0 else 0, 2 * small),
        )(tables[1], kept[h], got[h])
    for h in range(2):
        sent[h], kept[h] = pl.pallas_call(
            functools.partial(second_sum_kernel, h),
            out_shape=[shape(half, order_n)] * 2,
            in_specs=[SMEM, VMEM, VMEM],
            out_specs=[VMEM] * 2,
            compiler_params=params(8),
            cost_estimate=cost(0, small),
        )(tables[2], kept[h], exchange(sent[h], h, 1))
    for h in range(2):
        sent[h] = pl.pallas_call(
            third_sum_kernel,
            out_shape=shape(half, order_n),
            in_specs=[VMEM] * 2,
            out_specs=VMEM,
            compiler_params=params(8),
            cost_estimate=cost(0, small),
        )(kept[h], exchange(sent[h], h, 2))
    got = [exchange(sent[h], h, 3) for h in range(2)]
    return pl.pallas_call(
        gram_kernel,
        out_shape=[shape(n, order_n)] * 3,
        in_specs=[VMEM] * 4,
        out_specs=[VMEM] * 3,
        compiler_params=params(16),
        cost_estimate=cost(35 * 10**8, 4 * small),
    )(*sent, *got)


def body(grad_partial, statistics, owner_table):
    n_dp = lax.axis_size("dp")
    n_owner = lax.axis_size("z") * 2
    order_b = grad_partial.shape[3]
    slab = order_b // n_dp
    slots = statistics.shape[2]
    core = lax.axis_index("core")
    col = 2 * lax.axis_index("z") + core
    lane_item = home_tables()
    tables = [jnp.asarray(t.reshape(-1)) for t in tree_tables()]

    device = owner_table.reshape(n_owner, 2 * blocks_col)
    by_column = device % n_owner
    lane_row = jnp.max(jnp.where(by_column == col, device // n_owner, -1), axis=1)
    numbers = jnp.arange(n_owner, dtype=jnp.int32)
    same = (lane_row[None, :] == lane_row[:, None]) & (numbers[None, :] < numbers[:, None])
    lane_slot = jnp.sum(same.astype(jnp.int32), axis=1)
    lane_from = jnp.where(lane_row < 0, 0, lane_row * slots + lane_slot)
    home = lax.dynamic_slice_in_dim(by_column, col, 1, axis=0)
    wanted = jnp.asarray(lane_item)[core]
    item_hot = wanted[:, None] == jnp.arange(2 * blocks_col)[None, :]
    item_from = jnp.sum(jnp.where(item_hot, home, 0), axis=1)

    packed = pl.pallas_call(
        pack_kernel,
        out_shape=shape(n_dp, slots, packed_rows, 128),
        in_specs=[HBM],
        out_specs=HBM,
        scratch_shapes=[
            pltpu.VMEM((slots, 3, order_b // 2, order_b // 2), jnp.float32),
            pltpu.VMEM((slots, n_dp, packed_rows, 128), jnp.bfloat16),
            pltpu.SemaphoreType.DMA((3 * slots,)),
            pltpu.SemaphoreType.DMA((slots,)),
        ],
        compiler_params=params(most_mib),
        cost_estimate=cost(0, 3 * 1024 * 1024),
    )(statistics[0, 0])
    spread = lax.all_to_all(packed, "dp", split_axis=0, concat_axis=0, tiled=True)
    *sent, k0, k1 = first_sent(grad_partial[0], tables)
    spread, _ = lax.optimization_barrier((spread, sent))
    got = [exchange(a, portion, 0) for portion, a in enumerate(sent)]
    lanes = pick(lane_from, spread.reshape(slots * n_dp, packed_rows, 128), long_flops // 3)
    lanes = lax.all_to_all(lanes, ("z", "core"), split_axis=0, concat_axis=0, tiled=True)
    gradient, left, right = gradient_sum((k0, k1), got, tables)
    lanes = pick(item_from, lanes).reshape(n_dp, 2, packed_rows, 128)
    chunks = lax.all_to_all(lanes, "dp", split_axis=0, concat_axis=0, tiled=True)

    full = (order_b, order_b)
    update = pl.pallas_call(
        update_kernel,
        out_shape=shape(*full),
        in_specs=[VMEM] * 4,
        out_specs=VMEM,
        scratch_shapes=[
            pltpu.VMEM((2, order_b // 2, order_b // 2), jnp.float32),
            pltpu.VMEM((2, order_b // 2, order_b // 2), jnp.float32),
            pltpu.VMEM((2,) + full, jnp.bfloat16),
        ],
        compiler_params=params(40),
        cost_estimate=cost(16 * order_b**3, 6 * 1024 * 1024),
    )(chunks, gradient, left, right)
    rows = update.reshape(n_dp, slab, order_b)
    rows = lax.all_to_all(rows, "dp", split_axis=0, concat_axis=0, tiled=True)
    return pl.pallas_call(
        output_kernel,
        out_shape=shape(blocks_col, slab, order_b),
        in_specs=[VMEM],
        out_specs=HBM,
        scratch_shapes=[pltpu.SemaphoreType.DMA((blocks_col,))],
        compiler_params=params(4),
        cost_estimate=cost(0, 512 * 1024),
    )(rows)


def solution(mesh):
    n_dp, n_owner = mesh.devices.shape
    fine = Mesh(mesh.devices.reshape(n_dp, n_owner // 2, 2), ("dp", "z", "core"))
    column = ("z", "core")
    in_specs = (P("dp", column, None, None), P("dp", column, None, None, None), P())
    out_specs = P(column, "dp", None)
    return jax.shard_map(body, mesh=fine, in_specs=in_specs, out_specs=out_specs, check_vma=False)
```

```python
import functools
import math

import jax
import jax.numpy as jnp
import numpy as np
from jax import lax
from jax.experimental import pallas as pl
from jax.experimental.pallas import tpu as pltpu
from jax.sharding import Mesh
from jax.sharding import PartitionSpec as P

decay_rate = 0.9
update_gain = 16.0
root_gain = 1.5

side_x = 4
chips = (
    ((0, 0), (0, 2), (2, 0), (1, 1), (3, 3)),
    ((1, 0), (1, 2), (3, 0), (2, 1), (0, 3)),
)
blocks_col = len(chips[0])
packed_rows = 72

long_flops = 10**11

most_mib = 60

VMEM = pl.BlockSpec(memory_space=pltpu.VMEM)
SMEM = pl.BlockSpec(memory_space=pltpu.SMEM)
HBM = pl.BlockSpec(memory_space=pltpu.HBM)


def even(v):
    return v ^ 1


def odd(v):
    return side_x - 1 - v


def order(portion, core):
    first, later = (even, odd) if core == portion else (odd, even)
    one, two = portion, 1 - portion
    return ((one, first), (one, later), (two, first), (two, later))


def pairs(portion, step):
    out = []
    for x in range(side_x):
        for y in range(side_x):
            for p in range(2):
                axis, pairing = order(portion, p)[step]
                to = (pairing(x), y) if axis == 0 else (x, pairing(y))
                out.append((2 * (side_x * x + y) + p, 2 * (side_x * to[0] + to[1]) + p))
    return out


def padded(items, count):
    assert len(items) <= count
    return (list(items) + [0] * count)[:count]


@functools.cache
def tree_tables():
    first, second, third = [], [], []
    for d in range(side_x * side_x):
        here = (d // side_x, d % side_x)
        for p in range(2):
            one, two, three = [], [], []
            for portion in range(2):
                steps = order(portion, p)
                axis, later = steps[1]
                at = [c[axis] for c in chips[p]]
                me = here[axis]
                kept = [j for j in range(blocks_col) if at[j] in (me, later(me))]
                one += padded([j for j in range(blocks_col) if j not in kept], 3)
                one += padded(kept, 3)
                go = [i for i, j in enumerate(kept) if at[j] == later(me)]
                stay = [i for i, j in enumerate(kept) if at[j] == me]
                for place in padded(go, 2) + padded(stay, 2):
                    two.append(place)
                mine = [kept[i] for i in stay]
                axis, later = steps[3]
                near = (here[axis], later(here[axis]))
                stay = [i for i, j in enumerate(mine) if chips[p][j][axis] in near]
                go = [i for i, j in enumerate(mine) if chips[p][j][axis] not in near]
                three += padded(go, 1) + padded(stay, 1)
            first.append(one)
            second.append(two)
            third.append(three)
    return [np.array(t, np.int32) for t in (first, second, third)]


@functools.cache
def home_tables():
    item = np.zeros((2, 2 * side_x * side_x), np.int32)
    for p in range(2):
        for j, (x, y) in enumerate(chips[p]):
            d = side_x * x + y
            item[p, 2 * d : 2 * d + 2] = (2 * j, 2 * j + 1)
    return item


def params(mib):
    return pltpu.CompilerParams(vmem_limit_bytes=mib * 1024 * 1024)


def add_rounded(a, b):
    return (a.astype(jnp.float32) + b.astype(jnp.float32)).astype(jnp.bfloat16)


def my_row(table):
    width = table.shape[0] // (2 * side_x * side_x)
    base = (2 * lax.axis_index("dp") + lax.axis_index("core")) * width
    return [table[base + k] for k in range(width)]


def choose_kernel(table, source, s0, s1, k0, k1):
    table = my_row(table)
    height = s0.shape[1]
    for h, (sent, kept) in enumerate(((s0, k0), (s1, k1))):
        rows = slice(h * height, (h + 1) * height)
        for u in range(3):
            sent[u] = source[table[6 * h + u], rows, :]
            kept[u] = source[table[6 * h + 3 + u], rows, :]


def first_sum_kernel(portion, table, kept, got, sent, next_kept):
    table = my_row(table)
    for u in range(4):
        place = table[4 * portion + u]
        total = add_rounded(kept[place], got[place])
        if u < 2:
            sent[u] = total
        else:
            next_kept[u - 2] = total


def second_sum_kernel(portion, table, kept, got, sent, next_kept):
    table = my_row(table)
    go, stay = table[2 * portion], table[2 * portion + 1]
    sent[...] = add_rounded(kept[go], got[go])
    next_kept[...] = add_rounded(kept[stay], got[stay])


def third_sum_kernel(kept, got, sent):
    sent[...] = add_rounded(kept[...], got[...])


def gram_kernel(a, b, r0, r1, out, left, right):
    half = a.shape[0]
    out[:half, :] = add_rounded(a[...], r0[...])
    out[half:, :] = add_rounded(b[...], r1[...])
    g = out[...]
    for gram, side in ((left, 1), (right, 0)):
        product = lax.dot_general(
            g, g, (((side,), (side,)), ((), ())), preferred_element_type=jnp.float32
        )
        gram[...] = product.astype(jnp.bfloat16)


def pick_kernel(table, source, out, staged, sems):
    group = out.shape[0] // 4
    stores = []
    for g in range(4):
        rows = pl.ds(g * group, group)
        for i in range(g * group, (g + 1) * group):
            staged[i] = source[table[i]]
        stores.append(pltpu.make_async_copy(staged.at[rows], out.at[rows], sems.at[g]))
        stores[g].start()
    for store in stores:
        store.wait()


def pick(table, source, flops=0):
    out = table.shape + source.shape[1:]
    return pl.pallas_call(
        pick_kernel,
        out_shape=jax.ShapeDtypeStruct(out, source.dtype),
        in_specs=[SMEM, VMEM],
        out_specs=HBM,
        scratch_shapes=[pltpu.VMEM(out, source.dtype), pltpu.SemaphoreType.DMA((4,))],
        compiler_params=params(4),
        cost_estimate=cost(flops, 4 * 1024 * 1024),
    )(table, source)


def output_kernel(source, out, sems):
    core = lax.axis_index("core")
    for p in range(2):

        @pl.when(core == p)
        def _():
            copies = [
                pltpu.make_async_copy(source.at[side_x * x + y], out.at[j], sems.at[j])
                for j, (x, y) in enumerate(chips[p])
            ]
            for copy in copies:
                copy.start()
            for copy in copies:
                copy.wait()


def square_iotas(n):
    return (
        lax.broadcasted_iota(jnp.int32, (n, n), 0),
        lax.broadcasted_iota(jnp.int32, (n, n), 1),
    )


def pack_kernel(stats, out, quarters, packed, in_sems, out_sems):
    half = stats.shape[1] // 2
    i, j = square_iotas(half)
    row = lax.broadcasted_iota(jnp.int32, (8, 128), 0)
    corners = ((0, 0), (0, half), (half, half))
    slots = range(stats.shape[0])
    loads = [
        [
            pltpu.make_async_copy(
                stats.at[q, pl.ds(at, half), pl.ds(left, half)],
                quarters.at[q, k],
                in_sems.at[3 * q + k],
            )
            for k, (at, left) in enumerate(corners)
        ]
        for q in slots
    ]
    stores = [
        pltpu.make_async_copy(packed.at[q], out.at[:, q], out_sems.at[q]) for q in slots
    ]
    for q in slots:
        for load in loads[q]:
            load.start()
    for q in slots:
        for load in loads[q]:
            load.wait()
        low = quarters[q, 2]
        mixed = jnp.where(i <= j, quarters[q, 0], low).astype(jnp.bfloat16)
        side = quarters[q, 1].astype(jnp.bfloat16)
        diagonal = jnp.sum(jnp.where(i == j, low, 0.0), axis=0, keepdims=True)
        tail = jnp.where(
            row == 0, diagonal[:, :128], jnp.where(row == 1, diagonal[:, 128:], 0.0)
        ).astype(jnp.bfloat16)
        strips = (mixed[:, :128], mixed[:, 128:], side[:, :128], side[:, 128:])
        for c in range(16):
            packed[q, c, :64, :] = strips[c // 4][64 * (c % 4) : 64 * (c % 4) + 64, :]
            packed[q, c, 64:, :] = tail
        stores[q].start()
    for q in slots:
        stores[q].wait()


def product(a, b):
    return jnp.dot(
        a.astype(jnp.bfloat16), b.astype(jnp.bfloat16), preferred_element_type=jnp.float32
    )


def add_statistic(chunks, s, gram, mixed, side, stat):
    half = mixed.shape[0]
    for c in range(16):
        strip = chunks[c, s, :64, :].astype(jnp.float32)
        rows = slice(64 * (c % 4), 64 * (c % 4) + 64)
        cols = slice(128 * (c // 4 % 2), 128 * (c // 4 % 2) + 128)
        if c < 8:
            mixed[rows, cols] = strip
        else:
            side[rows, cols] = strip
    tail = chunks[0, s, 64:, :].astype(jnp.float32)
    diagonal = jnp.concatenate([tail[0:1, :], tail[1:2, :]], axis=1)
    m = mixed[...]
    flipped = m.T
    i, j = square_iotas(half)
    upper, lower = slice(0, half), slice(half, 2 * half)
    low = jnp.where(i > j, m, jnp.where(i == j, diagonal, flipped))
    total = 0.0
    for old, rows, cols in (
        (jnp.where(i <= j, m, flipped), upper, upper),
        (low, lower, lower),
        (side[...], upper, lower),
    ):
        added = decay_rate * old + (1.0 - decay_rate) * gram[rows, cols].astype(jnp.float32)
        rounded = added.astype(jnp.bfloat16)
        stat[rows, cols] = rounded
        wide = rounded.astype(jnp.float32)
        squares = jnp.sum(wide * wide, axis=0, keepdims=True)
        if rows is not cols:
            stat[cols, rows] = wide.T.astype(jnp.bfloat16)
            squares = 2.0 * squares
        total = total + squares
    return total


def update_kernel(chunks, gradient, left, right, out, mixed, side, stat):
    order_n = out.shape[0]
    sides = (0, 1)
    i, j = square_iotas(order_n)
    scale, quarter, square = [], [], []
    for s, gram in zip(sides, (left, right)):
        squares = add_statistic(chunks, s, gram, mixed.at[s], side.at[s], stat.at[s])
        frob_norm = jnp.sqrt(jnp.sum(squares, axis=1, keepdims=True) + 1e-06)
        scale.append(root_gain * math.sqrt(order_n) / frob_norm)
        part = 0.25 * scale[s]
        quarter.append(part * stat[s].astype(jnp.float32))
        square.append((part * part) * product(stat[s], stat[s]))
    e2 = [jnp.where(i == j, 0.5625, 0.0) - 2.5 * quarter[s] + square[s] for s in sides]
    e4 = [2.0 * e2[s] + product(e2[s], e2[s]) for s in sides]
    rest = [square[s] - 1.25 * quarter[s] for s in sides]
    roots = []
    for s in sides:
        root = jnp.where(i == j, e2[s] + 1.0, e2[s]) + product(e4[s], rest[s])
        roots.append((jnp.sqrt(jnp.sqrt(scale[s])) * root).astype(jnp.bfloat16))
    applied = jnp.dot(gradient[...], roots[1], preferred_element_type=jnp.float32)
    update = jnp.dot(
        roots[0], applied.astype(jnp.bfloat16), preferred_element_type=jnp.float32
    )
    out[...] = (update_gain * update).astype(jnp.bfloat16)


def shape(*dims):
    return jax.ShapeDtypeStruct(dims, jnp.bfloat16)


def cost(flops, moved):
    return pl.CostEstimate(flops=flops, bytes_accessed=moved, transcendentals=0)


def exchange(array, portion, step):
    return lax.ppermute(array, ("dp", "core"), pairs(portion, step))


def first_sent(grad, tables):
    n, order_n = grad.shape[1], grad.shape[2]
    return pl.pallas_call(
        choose_kernel,
        out_shape=[shape(3, n // 2, order_n)] * 4,
        in_specs=[SMEM, VMEM],
        out_specs=[VMEM] * 4,
        compiler_params=params(most_mib),
        cost_estimate=cost(0, 12 * n * order_n),
    )(tables[0], grad)


def gradient_sum(kept, got, tables):
    half, order_n = kept[0].shape[1], kept[0].shape[2]
    n = 2 * half
    small = 1024 * 1024
    sent, kept, got = [None, None], list(kept), list(got)
    for h in range(2):
        if h == 1:
            got[1], _ = lax.optimization_barrier((got[1], sent[0]))
        sent[h], kept[h] = pl.pallas_call(
            functools.partial(first_sum_kernel, h),
            out_shape=[shape(2, half, order_n)] * 2,
            in_specs=[SMEM, VMEM, VMEM],
            out_specs=[VMEM] * 2,
            compiler_params=params(8),
            cost_estimate=cost(long_flops if h == 0 else 0, 2 * small),
        )(tables[1], kept[h], got[h])
    for h in range(2):
        sent[h], kept[h] = pl.pallas_call(
            functools.partial(second_sum_kernel, h),
            out_shape=[shape(half, order_n)] * 2,
            in_specs=[SMEM, VMEM, VMEM],
            out_specs=[VMEM] * 2,
            compiler_params=params(8),
            cost_estimate=cost(0, small),
        )(tables[2], kept[h], exchange(sent[h], h, 1))
    for h in range(2):
        sent[h] = pl.pallas_call(
            third_sum_kernel,
            out_shape=shape(half, order_n),
            in_specs=[VMEM] * 2,
            out_specs=VMEM,
            compiler_params=params(8),
            cost_estimate=cost(0, small),
        )(kept[h], exchange(sent[h], h, 2))
    got = [exchange(sent[h], h, 3) for h in range(2)]
    return pl.pallas_call(
        gram_kernel,
        out_shape=[shape(n, order_n)] * 3,
        in_specs=[VMEM] * 4,
        out_specs=[VMEM] * 3,
        compiler_params=params(16),
        cost_estimate=cost(2 * 10**9, 4 * small),
    )(*sent, *got)


def body(grad_partial, statistics, owner_table):
    n_dp = lax.axis_size("dp")
    n_owner = lax.axis_size("z") * 2
    order_b = grad_partial.shape[3]
    slab = order_b // n_dp
    slots = statistics.shape[2]
    core = lax.axis_index("core")
    col = 2 * lax.axis_index("z") + core
    lane_item = home_tables()
    tables = [jnp.asarray(t.reshape(-1)) for t in tree_tables()]

    device = owner_table.reshape(n_owner, 2 * blocks_col)
    by_column = device % n_owner
    lane_row = jnp.max(jnp.where(by_column == col, device // n_owner, -1), axis=1)
    numbers = jnp.arange(n_owner, dtype=jnp.int32)
    same = (lane_row[None, :] == lane_row[:, None]) & (numbers[None, :] < numbers[:, None])
    lane_slot = jnp.sum(same.astype(jnp.int32), axis=1)
    lane_from = jnp.where(lane_row < 0, 0, lane_row * slots + lane_slot)
    home = lax.dynamic_slice_in_dim(by_column, col, 1, axis=0)
    wanted = jnp.asarray(lane_item)[core]
    item_hot = wanted[:, None] == jnp.arange(2 * blocks_col)[None, :]
    item_from = jnp.sum(jnp.where(item_hot, home, 0), axis=1)

    packed = pl.pallas_call(
        pack_kernel,
        out_shape=shape(n_dp, slots, packed_rows, 128),
        in_specs=[HBM],
        out_specs=HBM,
        scratch_shapes=[
            pltpu.VMEM((slots, 3, order_b // 2, order_b // 2), jnp.float32),
            pltpu.VMEM((slots, n_dp, packed_rows, 128), jnp.bfloat16),
            pltpu.SemaphoreType.DMA((3 * slots,)),
            pltpu.SemaphoreType.DMA((slots,)),
        ],
        compiler_params=params(most_mib),
        cost_estimate=cost(0, 3 * 1024 * 1024),
    )(statistics[0, 0])
    spread = lax.all_to_all(packed, "dp", split_axis=0, concat_axis=0, tiled=True)
    *sent, k0, k1 = first_sent(grad_partial[0], tables)
    spread, _ = lax.optimization_barrier((spread, sent))
    got = [exchange(a, portion, 0) for portion, a in enumerate(sent)]
    lanes = pick(lane_from, spread.reshape(slots * n_dp, packed_rows, 128), long_flops // 3)
    lanes = lax.all_to_all(lanes, ("z", "core"), split_axis=0, concat_axis=0, tiled=True)
    gradient, left, right = gradient_sum((k0, k1), got, tables)
    lanes = pick(item_from, lanes).reshape(n_dp, 2, packed_rows, 128)
    chunks = lax.all_to_all(lanes, "dp", split_axis=0, concat_axis=0, tiled=True)

    full = (order_b, order_b)
    update = pl.pallas_call(
        update_kernel,
        out_shape=shape(*full),
        in_specs=[VMEM] * 4,
        out_specs=VMEM,
        scratch_shapes=[
            pltpu.VMEM((2, order_b // 2, order_b // 2), jnp.float32),
            pltpu.VMEM((2, order_b // 2, order_b // 2), jnp.float32),
            pltpu.VMEM((2,) + full, jnp.bfloat16),
        ],
        compiler_params=params(40),
        cost_estimate=cost(16 * order_b**3, 6 * 1024 * 1024),
    )(chunks, gradient, left, right)
    rows = update.reshape(n_dp, slab, order_b)
    rows = lax.all_to_all(rows, "dp", split_axis=0, concat_axis=0, tiled=True)
    return pl.pallas_call(
        output_kernel,
        out_shape=shape(blocks_col, slab, order_b),
        in_specs=[VMEM],
        out_specs=HBM,
        scratch_shapes=[pltpu.SemaphoreType.DMA((blocks_col,))],
        compiler_params=params(4),
        cost_estimate=cost(0, 512 * 1024),
    )(rows)


def solution(mesh):
    n_dp, n_owner = mesh.devices.shape
    fine = Mesh(mesh.devices.reshape(n_dp, n_owner // 2, 2), ("dp", "z", "core"))
    column = ("z", "core")
    in_specs = (P("dp", column, None, None), P("dp", column, None, None, None), P())
    out_specs = P(column, "dp", None)
    return jax.shard_map(body, mesh=fine, in_specs=in_specs, out_specs=out_specs, check_vma=False)
```
